32 devices in a mesh: narrow: 4 (over y, x), wide: 8 (over z, core).
Axes of the slice: x: 2, y: 2, z: 4, core: 2. Of those that a mesh axis runs over, the one named last changes fastest.
Arguments:
- deflation: bfloat16 [8, 3, 16, 64, 256], P(None, None, 'narrow', 'wide'), may hold values from 0.25 to 1
- residual: float32 [3, 16, 64, 256], P(None, 'narrow', 'wide'), may hold values from -1 to 2
- stiffness: float32 [16, 64, 256], P('narrow', 'wide'), may hold values from 0.25 to 2.5
- mass: float32 [16, 64, 256], P('narrow', 'wide'), may hold values from 1 to 4
- stencil: float32 [27, 3, 3], replicated, may hold values from -0.625 to 0.625
- local_inverse: bfloat16 [12, 12, 12, 40, 256], P(None, None, 'narrow', 'wide'), may hold values from -1.75 to 1.75
- inverse_factor: float32 [256, 256], P(('narrow', 'wide')), as said below
- margin_range: int32 [4, 8, 2, 2], P('narrow', 'wide'), may hold values from 0 to 10, as said below
- neighbor_blocks: int32 [4, 8, 9], P('narrow', 'wide'), may hold values from -1 to 31, as said below
Outputs:
- preconditioned: float32 [3, 16, 64, 256], P(None, 'narrow', 'wide')
- coarse_blocks: float32 [4, 8, 9, 8, 8], P('narrow', 'wide')
- coarse_solution: float32 [256], replicated
The draws below stay inside these ranges and needn't reach their ends.
Inputs may be any that keep to these rules, and one draw needn't show every extreme that they name: `margin_range`: starts are 0 or 1, stops are 5 or 6 along the first dimension and 9 or 10 along the second. `neighbor_blocks`: entry (i, j, (dx + 1) * 3 + dy + 1) is the coarse block number of subdomain (i + dx, j + dy), or -1 if that lies outside the subdomain grid; the numbers of the subdomains are a permutation of 0 to 4 * 8 - 1. `inverse_factor`: zero above the diagonal.
All inputs are finite; a program needn't handle non-finite values.
Results may differ from the reference program's by a relative error of at most 0.0025.
Values may be sent and summed in bfloat16 or wider, within the bound.
A program may use at most 128 MiB of HBM per device.

```python
import math
import jax
import jax.numpy as jnp
from jax import lax

CX = 4
CY = 8
CZ = 256
VECTORS = 8
BLOCKS_X = 3
BLOCKS_Y = 5
NX = 16
NY = 64
NZ = 256
COARSE = 256
N_NARROW = 4
N_WIDE = 8


def draw_inverse_factor(key, part):
    key = jax.random.fold_in(key, 7)
    first_key, second_key = jax.random.split(key)
    scale = (3.0 * CX * CY * CZ * VECTORS * 6.0) ** (-0.5)
    diagonal = jax.random.uniform(first_key, (COARSE,), jnp.float32, 1.0, 2.0)
    lower = jax.random.normal(second_key, (COARSE, COARSE), jnp.float32) * 0.3
    lower = jnp.tril(lower * COARSE ** (-0.5), -1)
    return (scale * (jnp.diag(diagonal) + lower)).astype(jnp.float32)


def draw_margin_range(key, part):
    key = jax.random.fold_in(key, 5)
    steps = jax.random.randint(key, (N_NARROW, N_WIDE, 2, 2), 0, 2).astype(jnp.int32)
    base = jnp.array([[0, CX + 1], [0, CY + 1]], jnp.int32)
    ranges = base[None, None] + steps
    widest = jnp.array([[0, CX + 2], [0, CY + 2]], jnp.int32)
    ranges = ranges.at[0, 0].set(widest)
    return ranges.astype(jnp.int32)


def draw_neighbor_blocks(key, part):
    key = jax.random.fold_in(key, 11)
    order = jax.random.permutation(key, N_NARROW * N_WIDE).astype(jnp.int32).reshape(N_NARROW, N_WIDE)
    padded = jnp.pad(order, 1, constant_values=-1)
    pieces = [padded[1 + shift_x:1 + shift_x + N_NARROW, 1 + shift_y:1 + shift_y + N_WIDE] for shift_x in (-1, 0, 1) for shift_y in (-1, 0, 1)]
    return jnp.stack(pieces, axis=-1).astype(jnp.int32)


def levels(rng, shape, cuts, least, high):
    def one(position, shards_of):
        draws = jax.random.uniform(jax.random.fold_in(jax.random.fold_in(rng, 6), position), (shards_of,), jnp.float32, least / len(cuts), high / len(cuts))
        return jnp.repeat(jnp.exp(draws), shape[position] // shards_of).reshape((-1,) + (1,) * (len(shape) - position - 1))

    loudness = one(*cuts[0])
    for cut in cuts[1:]:
        loudness = loudness * one(*cut)
    return loudness


def bell_draw(stream_key, extent, deviation, reach, cuts=(), held_as=jnp.bfloat16):
    level = levels(stream_key, extent, cuts, -0.22, 0.18) if cuts else 1.0
    values = jax.random.normal(stream_key, extent, jnp.float32) * deviation * level
    return jnp.minimum(jnp.maximum(values, -reach), reach).astype(held_as)


def setup_inputs(seed: int = 0) -> dict:
    key_of = jax.random.split(jax.random.key(seed), 10)
    deflation = jnp.clip(0.25 + 0.75 * jax.random.uniform(key_of[0], (VECTORS, 3, NX, NY, NZ), jnp.float32) ** levels(key_of[0], (VECTORS, 3, NX, NY, NZ), ((2, 4), (3, 8)), -0.2, 0.2), 0.25, 1.0).astype(jnp.bfloat16)
    residual = jnp.clip(-1.0 + 3.0 * jax.random.uniform(key_of[1], (3, NX, NY, NZ), jnp.float32) ** levels(key_of[1], (3, NX, NY, NZ), ((1, 4), (2, 8)), -0.2, 0.2), -1.0, 2.0)
    stiffness = jnp.clip(jnp.exp(math.log(2.5) - 2.3025851 * jax.random.uniform(key_of[2], (NX, NY, NZ), jnp.float32) ** levels(key_of[2], (NX, NY, NZ), ((0, 4), (1, 8)), -0.2, 0.2)), 0.25, 2.5)
    mass = jnp.clip(jnp.exp(math.log(4.0) - 1.3862944 * jax.random.uniform(key_of[3], (NX, NY, NZ), jnp.float32) ** levels(key_of[3], (NX, NY, NZ), ((0, 4), (1, 8)), -0.2, 0.2)), 1.0, 4.0)
    stencil = bell_draw(key_of[4], (27, 3, 3), 81 ** -0.5, 0.625, (), jnp.float32)
    local_inverse = bell_draw(key_of[5], (12, 12, BLOCKS_X * N_NARROW, BLOCKS_Y * N_WIDE, NZ), 12 ** -0.5, 1.75, ((2, 4), (3, 8)))
    inverse_factor = draw_inverse_factor(jax.random.fold_in(key_of[9], 71), 0)
    margin_range = draw_margin_range(jax.random.fold_in(key_of[9], 71), 0)
    neighbor_blocks = draw_neighbor_blocks(jax.random.fold_in(key_of[9], 71), 0)
    return dict(deflation=deflation, residual=residual, stiffness=stiffness, mass=mass, stencil=stencil, local_inverse=local_inverse, inverse_factor=inverse_factor, margin_range=margin_range, neighbor_blocks=neighbor_blocks)


def side_table(shift, cells):
    where_to = jnp.arange(cells) + shift
    classes = jnp.where(where_to < 0, 0, jnp.where(where_to >= cells, 2, 1))
    return (classes[:, None] == jnp.arange(3)[None, :]).astype(jnp.float32)


def coarse_blocks_of(padded, stencil, stiffness, mass):
    vectors, components, ext_x, ext_y, depth = padded.shape
    cells_x = ext_x - 2
    cells_y = ext_y - 2
    deep = jnp.pad(padded, ((0, 0), (0, 0), (0, 0), (0, 0), (1, 1)))
    own = padded[:, :, 1:cells_x + 1, 1:cells_y + 1, :]
    blocks = jnp.zeros((3, 3, vectors, vectors), jnp.float32)
    for shift_x in (-1, 0, 1):
        for shift_y in (-1, 0, 1):
            image = jnp.zeros(own.shape, jnp.float32)
            for shift_z in (-1, 0, 1):
                piece = deep[:, :, 1 + shift_x:1 + shift_x + cells_x, 1 + shift_y:1 + shift_y + cells_y, 1 + shift_z:1 + shift_z + depth]
                offset = ((shift_x + 1) * 3 + shift_y + 1) * 3 + shift_z + 1
                image = image + jnp.einsum("ij,ajxyz->aixyz", stencil[offset], piece, precision=lax.Precision.HIGHEST)
            image = stiffness * image
            if shift_x == 0 and shift_y == 0:
                image = image + mass * own
            products = jnp.einsum("acxyz,bcxyz->abxy", own, image, precision=lax.Precision.HIGHEST)
            blocks = blocks + jnp.einsum("abxy,xs,yt->stab", products, side_table(shift_x, cells_x), side_table(shift_y, cells_y), precision=lax.Precision.HIGHEST)
    return blocks.reshape(9, vectors, vectors)


def margin_mask(extended, ranges):
    along_x = jnp.arange(extended.shape[1])
    along_y = jnp.arange(extended.shape[2])
    keep_x = (along_x >= ranges[0, 0]) & (along_x < ranges[0, 1])
    keep_y = (along_y >= ranges[1, 0]) & (along_y < ranges[1, 1])
    keep = keep_x[:, None] & keep_y[None, :]
    return jnp.where(keep[None, :, :, None], extended, jnp.zeros_like(extended))


def local_solve(inverse, extended):
    components, ext_x, ext_y, depth = extended.shape
    half_x = ext_x // 2
    half_y = ext_y // 2
    grouped = extended.reshape(components, half_x, 2, half_y, 2, depth).transpose(0, 2, 4, 1, 3, 5).reshape(components * 4, half_x, half_y, depth)
    solved = jnp.einsum("ijxyz,jxyz->ixyz", inverse.astype(jnp.float32), grouped.astype(jnp.float32), precision=lax.Precision.HIGHEST)
    solved = solved.reshape(components, 2, 2, half_x, half_y, depth).transpose(0, 3, 1, 4, 2, 5).reshape(components, ext_x, ext_y, depth)
    return solved[:, 1:ext_x - 1, 1:ext_y - 1, :]


def reference(deflation, residual, stiffness, mass, stencil, local_inverse, inverse_factor, margin_range, neighbor_blocks):
    vectors = deflation.shape[0]
    rounded = residual.astype(jnp.bfloat16)
    padded_all = jnp.pad(deflation, ((0, 0), (0, 0), (1, 1), (1, 1), (0, 0)))
    residual_all = jnp.pad(rounded, ((0, 0), (1, 1), (1, 1), (0, 0)))
    zero = jnp.int32(0)

    def per_device(index):
        row = (index // N_WIDE).astype(jnp.int32)
        column = (index % N_WIDE).astype(jnp.int32)
        start_x = (row * CX).astype(jnp.int32)
        start_y = (column * CY).astype(jnp.int32)
        padded = lax.dynamic_slice(padded_all, (zero, zero, start_x, start_y, zero), (vectors, 3, CX + 2, CY + 2, CZ)).astype(jnp.float32)
        stiff_here = lax.dynamic_slice(stiffness, (start_x, start_y, zero), (CX, CY, CZ))
        mass_here = lax.dynamic_slice(mass, (start_x, start_y, zero), (CX, CY, CZ))
        blocks = coarse_blocks_of(padded, stencil, stiff_here, mass_here)
        own = padded[:, :, 1:CX + 1, 1:CY + 1, :]
        own_residual = lax.dynamic_slice(rounded, (zero, start_x, start_y, zero), (3, CX, CY, CZ)).astype(jnp.float32)
        rhs = jnp.einsum("acxyz,cxyz->a", own, own_residual, precision=lax.Precision.HIGHEST)
        extended = lax.dynamic_slice(residual_all, (zero, start_x, start_y, zero), (3, CX + 2, CY + 2, CZ))
        extended = margin_mask(extended, margin_range[row, column])
        inverse = lax.dynamic_slice(local_inverse, (zero, zero, (row * BLOCKS_X).astype(jnp.int32), (column * BLOCKS_Y).astype(jnp.int32), zero), (12, 12, BLOCKS_X, BLOCKS_Y, CZ))
        local = local_solve(inverse, extended)
        return blocks, rhs, local

    count = N_NARROW * N_WIDE
    blocks, rhs, local = lax.map(per_device, jnp.arange(count, dtype=jnp.int32))
    listing = neighbor_blocks.reshape(count, 9)
    own_ids = listing[:, 4]
    coarse_rhs = jnp.zeros((count, vectors), jnp.float32).at[own_ids].set(rhs).reshape(-1)

    def solve(vector):
        inner = jnp.dot(inverse_factor, vector, precision=lax.Precision.HIGHEST)
        return jnp.dot(inverse_factor.T, inner, precision=lax.Precision.HIGHEST)

    first = solve(coarse_rhs)
    table = first.reshape(count, vectors)
    valid = listing >= 0
    near = jnp.where(valid[:, :, None], table[jnp.maximum(listing, 0)], jnp.zeros((count, 9, vectors), jnp.float32))
    image = jnp.einsum("dnab,dnb->da", blocks, near, precision=lax.Precision.HIGHEST)
    coarse_image = jnp.zeros((count, vectors), jnp.float32).at[own_ids].set(image).reshape(-1)
    coarse_solution = first + solve(coarse_rhs - coarse_image)
    weights = coarse_solution.reshape(count, vectors)[own_ids]

    def finish(index):
        row = (index // N_WIDE).astype(jnp.int32)
        column = (index % N_WIDE).astype(jnp.int32)
        own = lax.dynamic_slice(deflation, (zero, zero, (row * CX).astype(jnp.int32), (column * CY).astype(jnp.int32), zero), (vectors, 3, CX, CY, CZ)).astype(jnp.float32)
        return local[index] + jnp.einsum("a,acxyz->cxyz", weights[index], own, precision=lax.Precision.HIGHEST)

    result = lax.map(finish, jnp.arange(count, dtype=jnp.int32))
    preconditioned = result.reshape(N_NARROW, N_WIDE, 3, CX, CY, CZ).transpose(2, 0, 3, 1, 4, 5).reshape(3, N_NARROW * CX, N_WIDE * CY, CZ)
    coarse_blocks = blocks.reshape(N_NARROW, N_WIDE, 9, vectors, vectors)
    return preconditioned, coarse_blocks, coarse_solution
```

```python
import functools

import jax
import jax.numpy as jnp
import numpy as np
from jax import lax
from jax.experimental import pallas as pl
from jax.experimental.pallas import tpu as pltpu
from jax.sharding import PartitionSpec as P

F32 = jnp.float32
BF16 = jnp.bfloat16
HIGHEST = lax.Precision.HIGHEST
MESH = pl.DeviceIdType.MESH


def pad_to(count, unit):
    return -(-count // unit) * unit


def stencil_places(comps, nx, ny):
    rows = []
    for j in range(comps):
        rows += [(j, x, y) for x in range(nx) for y in range(ny)]
    for x in (-1, nx):
        rows += [(j, x, y) for j in range(comps) for y in range(ny)]
    for y in (-1, ny):
        face = [(j, x, y) for j in range(comps) for x in range(nx)]
        rows += face + [None] * (pad_to(len(face), 8) - len(face))
    corners = [(j, x, y) for x in (-1, nx) for y in (-1, ny) for j in range(comps)]
    rows += corners + [None] * (pad_to(len(corners), 8) - len(corners))
    cells = comps * nx * ny
    table = np.full((len(rows), 3 * cells), -1, np.int32)
    for r, row in enumerate(rows):
        if row is None:
            continue
        j, x, y = row
        for oz in range(3):
            for i in range(comps):
                for px in range(nx):
                    for py in range(ny):
                        dx, dy = x - px, y - py
                        if abs(dx) <= 1 and abs(dy) <= 1:
                            column = oz * cells + i * nx * ny + px * ny + py
                            table[r, column] = j * 9 + (dx + 1) * 3 + dy + 1
    return table


def split(values):
    high = values.astype(BF16)
    return high, (values - high.astype(F32)).astype(BF16)


def iota(shape, axis):
    return lax.broadcasted_iota(jnp.int32, shape, axis)


def load(ref, *at):
    return jnp.concatenate([ref[(h,) + at] for h in range(ref.shape[0])], axis=-1)


def store(ref, values, *at):
    for h in range(ref.shape[0]):
        ref[(h,) + at] = values[:, h * 128 : (h + 1) * 128]


def gram(left, right):
    dims = (((1,), (1,)), ((), ()))
    high, low = split(left)
    return lax.dot_general(high, right, dims, preferred_element_type=F32) + lax.dot_general(
        low, right, dims, preferred_element_type=F32
    )


def kernel(
    narrow,
    wide,
    vectors,
    comps,
    nx,
    ny,
    depth,
    deflation,
    residual,
    stiffness,
    mass,
    places,
    coupling,
    inverse_hbm,
    factor,
    margins,
    listing,
    out,
    blocks_out,
    solution_out,
    inverse,
    d32,
    r32,
    t32,
    s_parts,
    w_parts,
    stage,
    ext,
    loc,
    send_x,
    send_y,
    send_c,
    recv_x,
    recv_y,
    recv_c,
    factors,
    message,
    slots,
    inverse_sem,
    send_sems,
    recv_sems,
    wave_send,
    wave_recv,
):
    n = narrow * wide
    order = factor.shape[1]
    row = lax.axis_index("narrow")
    column = lax.axis_index("wide")
    me = row * wide + column
    cells = nx * ny
    own_rows = comps * cells

    def target_of(k):
        t = lax.rem(me + k, n)
        return (t // wide, lax.rem(t, wide))

    barrier = pltpu.get_barrier_semaphore()

    def greet(k, carry):
        pl.semaphore_signal(barrier, inc=1, device_id=target_of(k), device_id_type=MESH)
        return carry

    lax.fori_loop(1, n, greet, 0)

    inverse_copy = pltpu.make_async_copy(inverse_hbm, inverse, inverse_sem)
    inverse_copy.start()

    rounded = residual[...].astype(BF16).astype(F32).reshape(own_rows, depth)
    store(r32, rounded, pl.ds(0, own_rows))
    sums = []
    for a in range(vectors):
        d = deflation[a].astype(F32).reshape(own_rows, depth)
        store(d32, d, pl.ds(a * own_rows, own_rows))
        sums.append(jnp.sum(d * rounded, axis=0, keepdims=True))
    rhs_column = jnp.sum(jnp.concatenate(sums, axis=0), axis=1, keepdims=True)
    own_block = listing[0, 0, 4]
    own_place = iota((vectors, order), 1) == own_block * vectors + iota((vectors, order), 0)

    def placed(values):
        return jnp.sum(jnp.where(own_place, values, 0.0), axis=0, keepdims=True)

    message[0] = placed(rhs_column)

    x_rows = comps * ny
    y_rows = comps * nx
    for side, x in enumerate((0, nx - 1)):
        face = [
            load(d32, pl.ds((a * comps + j) * cells + x * ny, ny))
            for a in range(vectors)
            for j in range(comps)
        ]
        send_x[side, pl.ds(0, vectors * x_rows), :] = jnp.concatenate(face, axis=0).astype(BF16)
        stage[...] = jnp.zeros_like(stage)
        for j in range(comps):
            stage[pl.ds(j * ny, ny), :] = load(r32, pl.ds(j * cells + x * ny, ny))
        send_x[side, pl.ds(vectors * x_rows, 32), :] = stage[...].astype(BF16)
    for side, y in enumerate((0, ny - 1)):
        face = load(d32, pl.ds(y, vectors * y_rows, stride=ny))
        send_y[side, pl.ds(0, vectors * y_rows), :] = face.astype(BF16)
        stage[...] = jnp.zeros_like(stage)
        stage[pl.ds(0, y_rows), :] = load(r32, pl.ds(y, y_rows, stride=ny))
        send_y[side, pl.ds(vectors * y_rows, 16), :] = stage[pl.ds(0, 16), :].astype(BF16)
    for side_x, x in enumerate((0, nx - 1)):
        for side_y, y in enumerate((0, ny - 1)):
            stage[...] = jnp.zeros_like(stage)
            at = x * ny + y
            stage[pl.ds(0, vectors * comps), :] = load(d32, pl.ds(at, vectors * comps, stride=cells))
            stage[pl.ds(vectors * comps, comps), :] = load(r32, pl.ds(at, comps, stride=cells))
            send_c[side_x * 2 + side_y] = stage[...].astype(BF16)

    pl.semaphore_wait(barrier, n - 1)

    def wave(number):
        def one(k, carry):
            pltpu.make_async_remote_copy(
                src_ref=message.at[number],
                dst_ref=slots.at[number, k - 1],
                send_sem=wave_send.at[number],
                recv_sem=wave_recv.at[number],
                device_id=target_of(k),
                device_id_type=MESH,
            ).start()
            return carry

        lax.fori_loop(1, n, one, 0)

    def wave_sum(number):
        pltpu.make_async_copy(slots.at[number], slots.at[number], wave_recv.at[number]).wait()
        return lax.fori_loop(
            0,
            n - 1,
            lambda k, total: total + slots[number, k],
            message[number],
            unroll=n <= 32,
        )

    wave(0)

    def copies():
        found = []
        for side, shift in enumerate((-1, 1)):
            found.append((send_x.at[side], recv_x.at[1 - side], recv_x.at[side], shift, 0))
        for side, shift in enumerate((-1, 1)):
            found.append((send_y.at[side], recv_y.at[1 - side], recv_y.at[side], 0, shift))
        for side_x, shift_x in enumerate((-1, 1)):
            for side_y, shift_y in enumerate((-1, 1)):
                at = side_x * 2 + side_y
                found.append((send_c.at[at], recv_c.at[3 - at], recv_c.at[at], shift_x, shift_y))
        return found

    opposite = (1, 0, 3, 2, 7, 6, 5, 4)

    def inside(shift_x, shift_y):
        along_x = (row + shift_x >= 0) & (row + shift_x < narrow)
        along_y = (column + shift_y >= 0) & (column + shift_y < wide)
        return along_x & along_y

    def face_copy(k, source, target, shift_x, shift_y):
        return pltpu.make_async_remote_copy(
            src_ref=source,
            dst_ref=target,
            send_sem=send_sems.at[k],
            recv_sem=recv_sems.at[opposite[k]],
            device_id=(row + shift_x, column + shift_y),
            device_id_type=MESH,
        )

    for k, (source, target, _, shift_x, shift_y) in enumerate(copies()):

        @pl.when(inside(shift_x, shift_y))
        def _(k=k, source=source, target=target, shift_x=shift_x, shift_y=shift_y):
            face_copy(k, source, target, shift_x, shift_y).start()

    factors[me] = factor[...]

    def send_factor(k, carry):
        pltpu.make_async_remote_copy(
            src_ref=factor,
            dst_ref=factors.at[me],
            send_sem=wave_send.at[2],
            recv_sem=wave_recv.at[2],
            device_id=target_of(k),
            device_id_type=MESH,
        ).start()
        return carry

    lax.fori_loop(1, n, send_factor, 0)

    total_rows = places.shape[0]
    fixed = own_rows + 2 * x_rows
    chunks = [(j * cells, cells, j) for j in range(comps)]
    for side in range(2):
        chunks += [(own_rows + side * x_rows + j * ny, ny, j) for j in range(comps)]
    chunks.append((fixed, total_rows - fixed, None))
    for start, size, j in chunks:
        here = places[pl.ds(start, size), :]
        value = jnp.zeros(here.shape, F32)
        for e in range(comps * 9) if j is None else range(j * 9, j * 9 + 9):
            value = jnp.where(here == e, coupling[pl.ds(e, 1), :], value)
        s_parts[pl.ds(start, size), :] = value
    s_high, s_low = split(s_parts[...])

    lane = iota((own_rows, depth), 1)
    scale = jnp.concatenate([stiffness[...].reshape(cells, depth)] * comps, axis=0)
    weight = jnp.concatenate([mass[...].reshape(cells, depth)] * comps, axis=0)
    for a in range(vectors):
        d = load(d32, pl.ds(a * own_rows, own_rows))
        w = d * scale
        before = jnp.where(lane == depth - 1, 0.0, pltpu.roll(w, depth - 1, axis=1))
        after = jnp.where(lane == 0, 0.0, pltpu.roll(w, 1, axis=1))
        for oz, shifted in enumerate((before, w, after)):
            high, low = split(shifted)
            w_parts[a % 2, 0, pl.ds(oz * own_rows, own_rows), :] = high
            w_parts[a % 2, 1, pl.ds(oz * own_rows, own_rows), :] = low
        high = w_parts[a % 2, 0]
        low = w_parts[a % 2, 1]
        image = (
            jnp.dot(s_high, high, preferred_element_type=F32)
            + jnp.dot(s_high, low, preferred_element_type=F32)
            + jnp.dot(s_low, high, preferred_element_type=F32)
        )
        t32[a] = image
        t32[a, pl.ds(0, own_rows), :] = image[:own_rows] + weight * d

    width = 9 * vectors

    def picked(product, left_of, right_of, left_size):
        r = iota(product.shape, 0)
        c = iota(product.shape, 1)
        kept = jnp.where(left_of(r) == right_of(c), product, 0.0)
        return jnp.sum(kept.reshape(vectors, left_size, product.shape[1]), axis=1)

    def folded(values, lane_of):
        shape = (values.shape[1], width)
        chosen = (lane_of(iota(shape, 0)) == iota(shape, 1)).astype(F32)
        return jnp.dot(values, chosen, preferred_element_type=F32, precision=HIGHEST)

    total = None
    for j in range(comps):
        left = t32[:, pl.ds(j * cells, cells), :].reshape(vectors * cells, depth)
        right = jnp.concatenate(
            [load(d32, pl.ds((b * comps + j) * cells, cells)) for b in range(vectors)], axis=0
        ).astype(BF16)
        part = gram(left, right)
        total = part if total is None else total + part
    chosen = picked(total, lambda r: lax.rem(r, cells), lambda c: lax.rem(c, cells), cells)
    blocks = folded(chosen, lambda c: 4 * vectors + c // cells)

    for k, (source, target, landing, shift_x, shift_y) in enumerate(copies()):

        @pl.when(inside(shift_x, shift_y))
        def _(k=k, source=source, landing=landing, shift_x=shift_x, shift_y=shift_y):
            pltpu.make_async_remote_copy(
                src_ref=source,
                dst_ref=landing,
                send_sem=send_sems.at[k],
                recv_sem=recv_sems.at[k],
                device_id=(row + shift_x, column + shift_y),
                device_id_type=MESH,
            ).wait()

        @pl.when(jnp.logical_not(inside(shift_x, shift_y)))
        def _(landing=landing):
            landing[...] = jnp.zeros(landing.shape, BF16)

    for side in range(2):
        n_class = (1 if side == 0 else 7) * vectors
        left = t32[:, pl.ds(own_rows + side * x_rows, x_rows), :].reshape(vectors * x_rows, depth)
        part = gram(left, recv_x[side, pl.ds(0, vectors * x_rows), :])
        chosen = picked(part, lambda r: lax.rem(r, x_rows), lambda c: lax.rem(c, x_rows), x_rows)
        blocks += folded(chosen, lambda c, at=n_class: at + c // x_rows)
    y_padded = pad_to(y_rows, 8)
    for side in range(2):
        n_class = (3 if side == 0 else 5) * vectors
        left = t32[:, pl.ds(fixed + side * y_padded, y_padded), :]
        left = left.reshape(vectors * y_padded, depth)
        part = gram(left, recv_y[side, pl.ds(0, vectors * y_rows), :])
        chosen = picked(
            part, lambda r: lax.rem(r, y_padded), lambda c: lax.rem(c, y_rows), y_padded
        )
        blocks += folded(chosen, lambda c, at=n_class: at + c // y_rows)
    c_padded = pad_to(4 * comps, 8)
    left = t32[:, pl.ds(fixed + 2 * y_padded, c_padded), :].reshape(vectors * c_padded, depth)
    part = gram(left, recv_c[...].reshape(4 * 32, depth))

    def corner_row(c):
        at = lax.rem(c, 32)
        return jnp.where(at < vectors * comps, c // 32 * comps + lax.rem(at, comps), -1)

    def corner_lane(c):
        corner = c // 32
        at = lax.rem(c, 32)
        block = corner * 2 + jnp.where(corner >= 2, 2, 0)
        return jnp.where(at < vectors * comps, block * vectors + at // comps, -1)

    chosen = picked(part, lambda r: lax.rem(r, c_padded), corner_row, c_padded)
    blocks += folded(chosen, corner_lane)
    for k in range(9):
        blocks_out[0, 0, k] = blocks[:, k * vectors : (k + 1) * vectors]

    coarse_rhs = wave_sum(0)
    pltpu.make_async_copy(
        factors.at[pl.ds(0, n - 1)], factors.at[pl.ds(0, n - 1)], wave_recv.at[2]
    ).wait()

    def solve(vector):
        def one(d, total):
            f = factors[d]
            return total + f * jnp.sum(f * vector, axis=1, keepdims=True)

        zeros = jnp.zeros((factor.shape[0], order), F32)
        total = lax.fori_loop(0, n, one, zeros, unroll=n <= 32)
        return jnp.sum(total, axis=0, keepdims=True)

    first = solve(coarse_rhs)
    near = [
        iota((vectors, order), 1) == listing[0, 0, k] * vectors + iota((vectors, order), 0)
        for k in range(9)
    ]
    spread = jnp.concatenate([m.astype(F32) for m in near], axis=0)
    matrix_rows = jnp.dot(blocks, spread, preferred_element_type=F32, precision=HIGHEST)
    message[1] = placed(jnp.sum(matrix_rows * first, axis=1, keepdims=True))
    wave(1)

    for j in range(comps):
        for x in range(nx):
            store(ext, load(r32, pl.ds(j * cells + x * ny, ny)), j, 1 + x, pl.ds(1, ny))
    for side in range(2):
        at_x = side * (nx + 1)
        values = recv_x[side, pl.ds(vectors * x_rows, 32), :].astype(F32)
        for j in range(comps):
            store(ext, values[j * ny : (j + 1) * ny], j, at_x, pl.ds(1, ny))
        at_y = side * (ny + 1)
        values = recv_y[side, pl.ds(vectors * y_rows, 16), :].astype(F32)
        for j in range(comps):
            for x in range(nx):
                store(ext, values[j * nx + x : j * nx + x + 1], j, 1 + x, pl.ds(at_y, 1))
        for side_y in range(2):
            values = recv_c[side * 2 + side_y].astype(F32)
            for j in range(comps):
                at = vectors * comps + j
                store(ext, values[at : at + 1], j, at_x, pl.ds(side_y * (ny + 1), 1))

    half_x = (nx + 2) // 2
    half_y = (ny + 2) // 2
    kept_y = []
    for t in range(2):
        f = 2 * iota((half_y, depth), 0) + t
        kept_y.append((f >= margins[0, 0, 1, 0]) & (f < margins[0, 0, 1, 1]))
    inverse_copy.wait()
    for u in range(half_x):
        grouped = []
        for j in range(comps):
            for s in range(2):
                e = 2 * u + s
                kept = (e >= margins[0, 0, 0, 0]) & (e < margins[0, 0, 0, 1])
                factor_x = jnp.where(kept, 1.0, 0.0).astype(F32)
                for t in range(2):
                    values = load(ext, j, e, pl.ds(t, half_y, stride=2))
                    grouped.append(jnp.where(kept_y[t], values, 0.0) * factor_x)
        for j in range(comps):
            for s in range(2):
                x = 2 * u + s - 1
                if x < 0 or x >= nx:
                    continue
                for t in range(2):
                    i = 4 * j + 2 * s + t
                    acc = inverse[i, 0, u].astype(F32) * grouped[0]
                    for m in range(1, 4 * comps):
                        acc += inverse[i, m, u].astype(F32) * grouped[m]
                    store(loc, acc, j, x, pl.ds(t, half_y, stride=2))

    coarse_image = wave_sum(1)
    refined = first + solve(coarse_rhs - coarse_image)
    solution_out[...] = refined
    weights = jnp.sum(jnp.where(own_place, refined, 0.0), axis=1, keepdims=True)
    for j in range(comps):
        for x in range(nx):
            value = load(loc, j, x, pl.ds(1, ny))
            for a in range(vectors):
                at = (a * comps + j) * cells + x * ny
                value += weights[a : a + 1, :] * load(d32, pl.ds(at, ny))
            out[j, x] = value

    for number in range(2):
        pltpu.make_async_copy(slots.at[number], slots.at[number], wave_send.at[number]).wait()
    pltpu.make_async_copy(
        factors.at[pl.ds(0, n - 1)], factors.at[pl.ds(0, n - 1)], wave_send.at[2]
    ).wait()


def body(
    narrow,
    wide,
    deflation,
    residual,
    stiffness,
    mass,
    stencil,
    local_inverse,
    inverse_factor,
    margin_range,
    neighbor_blocks,
):
    vectors, comps, nx, ny, depth = deflation.shape
    n = narrow * wide
    order = inverse_factor.shape[1]
    cells = nx * ny
    places = stencil_places(comps, nx, ny)
    coupling = stencil.reshape(9, 3, comps, comps).transpose(3, 0, 1, 2)
    coupling = jnp.broadcast_to(
        coupling.reshape(comps * 9, 3 * comps, 1), (comps * 9, 3 * comps, cells)
    ).reshape(comps * 9, 3 * comps * cells)
    x_send = vectors * comps * ny + 32
    y_send = vectors * comps * nx + 16
    vmem = pl.BlockSpec(memory_space=pltpu.VMEM)
    smem = pl.BlockSpec(memory_space=pltpu.SMEM)
    result, blocks, refined = pl.pallas_call(
        functools.partial(kernel, narrow, wide, vectors, comps, nx, ny, depth),
        out_shape=(
            jax.ShapeDtypeStruct(residual.shape, F32),
            jax.ShapeDtypeStruct((1, 1, 9, vectors, vectors), F32),
            jax.ShapeDtypeStruct((1, order), F32),
        ),
        in_specs=[vmem] * 6 + [pl.BlockSpec(memory_space=pl.ANY), vmem, smem, smem],
        out_specs=(vmem, vmem, vmem),
        scratch_shapes=[
            pltpu.VMEM(local_inverse.shape, BF16),
            pltpu.VMEM((depth // 128, vectors * comps * cells, 128), F32),
            pltpu.VMEM((depth // 128, comps * cells, 128), F32),
            pltpu.VMEM((vectors, places.shape[0], depth), F32),
            pltpu.VMEM(places.shape, F32),
            pltpu.VMEM((2, 2, 3 * comps * cells, depth), BF16),
            pltpu.VMEM((32, depth), F32),
            pltpu.VMEM((depth // 128, comps, nx + 2, ny + 2, 128), F32),
            pltpu.VMEM((depth // 128, comps, nx, ny + 2, 128), F32),
            pltpu.VMEM((2, x_send, depth), BF16),
            pltpu.VMEM((2, y_send, depth), BF16),
            pltpu.VMEM((4, 32, depth), BF16),
            pltpu.VMEM((2, x_send, depth), BF16),
            pltpu.VMEM((2, y_send, depth), BF16),
            pltpu.VMEM((4, 32, depth), BF16),
            pltpu.VMEM((n,) + inverse_factor.shape, F32),
            pltpu.VMEM((2, 1, order), F32),
            pltpu.VMEM((2, n - 1, 1, order), F32),
            pltpu.SemaphoreType.DMA,
            pltpu.SemaphoreType.DMA((8,)),
            pltpu.SemaphoreType.DMA((8,)),
            pltpu.SemaphoreType.DMA((3,)),
            pltpu.SemaphoreType.DMA((3,)),
        ],
        compiler_params=pltpu.CompilerParams(
            collective_id=0, has_side_effects=True, vmem_limit_bytes=48 * 1024 * 1024
        ),
    )(
        deflation,
        residual,
        stiffness,
        mass,
        jnp.asarray(places),
        coupling,
        local_inverse,
        inverse_factor,
        margin_range,
        neighbor_blocks,
    )
    return result, blocks, refined.reshape(order)


def solution(mesh):
    placed = (
        P(None, None, "narrow", "wide", None),
        P(None, "narrow", "wide", None),
        P("narrow", "wide", None),
        P("narrow", "wide", None),
        P(),
        P(None, None, "narrow", "wide", None),
        P(("narrow", "wide"), None),
        P("narrow", "wide", None, None),
        P("narrow", "wide", None),
    )
    return jax.shard_map(
        functools.partial(body, mesh.shape["narrow"], mesh.shape["wide"]),
        mesh=mesh,
        in_specs=placed,
        out_specs=(P(None, "narrow", "wide", None), P("narrow", "wide", None, None, None), P()),
        check_vma=False,
    )
```

```python
import functools

import jax
import jax.numpy as jnp
import numpy as np
from jax import lax
from jax.experimental import pallas as pl
from jax.experimental.pallas import tpu as pltpu
from jax.sharding import PartitionSpec as P

F32 = jnp.float32
BF16 = jnp.bfloat16
HIGHEST = lax.Precision.HIGHEST
MESH = pl.DeviceIdType.MESH


def pad_to(count, unit):
    return -(-count // unit) * unit


def stencil_places(comps, nx, ny):
    rows = []
    for j in range(comps):
        rows += [(j, x, y) for x in range(nx) for y in range(ny)]
    for x in (-1, nx):
        rows += [(j, x, y) for j in range(comps) for y in range(ny)]
    for y in (-1, ny):
        face = [(j, x, y) for j in range(comps) for x in range(nx)]
        rows += face + [None] * (pad_to(len(face), 8) - len(face))
    corners = [(j, x, y) for x in (-1, nx) for y in (-1, ny) for j in range(comps)]
    rows += corners + [None] * (pad_to(len(corners), 8) - len(corners))
    cells = comps * nx * ny
    table = np.full((len(rows), 3 * cells), -1, np.int32)
    for r, row in enumerate(rows):
        if row is None:
            continue
        j, x, y = row
        for oz in range(3):
            for i in range(comps):
                for px in range(nx):
                    for py in range(ny):
                        dx, dy = x - px, y - py
                        if abs(dx) <= 1 and abs(dy) <= 1:
                            column = oz * cells + i * nx * ny + px * ny + py
                            table[r, column] = j * 9 + (dx + 1) * 3 + dy + 1
    return table


def split(values):
    high = values.astype(BF16)
    return high, (values - high.astype(F32)).astype(BF16)


def iota(shape, axis):
    return lax.broadcasted_iota(jnp.int32, shape, axis)


def load(ref, *at):
    return jnp.concatenate([ref[(h,) + at] for h in range(ref.shape[0])], axis=-1)


def store(ref, values, *at):
    for h in range(ref.shape[0]):
        ref[(h,) + at] = values[:, h * 128 : (h + 1) * 128]


def quotient(values, size, count):
    return sum((values >= k * size).astype(jnp.int32) for k in range(1, count))


def gram(left, right):
    dims = (((1,), (1,)), ((), ()))
    high, low = split(left)
    return lax.dot_general(high, right, dims, preferred_element_type=F32) + lax.dot_general(
        low, right, dims, preferred_element_type=F32
    )


def kernel(
    narrow,
    wide,
    vectors,
    comps,
    nx,
    ny,
    depth,
    deflation,
    residual,
    stiffness,
    mass,
    places,
    stencil,
    inverse_hbm,
    factor,
    margins,
    listing,
    out,
    blocks_out,
    solution_out,
    inverse,
    d32,
    r32,
    t32,
    s_parts,
    w_parts,
    stage,
    ext,
    loc,
    send_x,
    send_y,
    send_c,
    recv_x,
    recv_y,
    recv_c,
    factors,
    message,
    slots,
    inverse_sem,
    send_sems,
    recv_sems,
    wave_send,
    wave_recv,
):
    n = narrow * wide
    order = factor.shape[1]
    row = lax.axis_index("narrow")
    column = lax.axis_index("wide")
    me = row * wide + column
    cells = nx * ny
    own_rows = comps * cells

    def turned(here, count):
        places_of = [here + k for k in range(count)]
        return [jnp.where(at >= count, at - count, at) for at in places_of]

    target_rows = turned(row, narrow)

    def to_others(act):
        if n <= 64:
            for k in range(1, n):
                act(k - 1, (target_rows[k // wide], target_columns[k % wide]))
            return

        def one(k, carry):
            t = lax.rem(me + k, n)
            act(k - 1, (t // wide, lax.rem(t, wide)))
            return carry

        lax.fori_loop(1, n, one, 0)

    target_columns = turned(column, wide) if n <= 64 else None
    barrier = pltpu.get_barrier_semaphore()

    def greet(k, device):
        pl.semaphore_signal(barrier, inc=1, device_id=device, device_id_type=MESH)

    to_others(greet)

    inverse_copy = pltpu.make_async_copy(inverse_hbm, inverse, inverse_sem)
    inverse_copy.start()

    rounded = residual[...].astype(BF16).astype(F32).reshape(own_rows, depth)
    store(r32, rounded, pl.ds(0, own_rows))
    sums = []
    for a in range(vectors):
        d = deflation[a].astype(F32).reshape(own_rows, depth)
        store(d32, d, pl.ds(a * own_rows, own_rows))
        sums.append(jnp.sum(d * rounded, axis=0, keepdims=True))
    rhs_column = jnp.sum(jnp.concatenate(sums, axis=0), axis=1, keepdims=True)
    own_block = listing[0, 0, 4]
    own_place = iota((vectors, order), 1) == own_block * vectors + iota((vectors, order), 0)

    def placed(values):
        return jnp.sum(jnp.where(own_place, values, 0.0), axis=0, keepdims=True)

    message[0] = placed(rhs_column)

    x_rows = comps * ny
    y_rows = comps * nx
    for side, x in enumerate((0, nx - 1)):
        face = [
            load(d32, pl.ds((a * comps + j) * cells + x * ny, ny))
            for a in range(vectors)
            for j in range(comps)
        ]
        send_x[side, pl.ds(0, vectors * x_rows), :] = jnp.concatenate(face, axis=0).astype(BF16)
        stage[...] = jnp.zeros_like(stage)
        for j in range(comps):
            stage[pl.ds(j * ny, ny), :] = load(r32, pl.ds(j * cells + x * ny, ny))
        send_x[side, pl.ds(vectors * x_rows, 32), :] = stage[...].astype(BF16)
    for side, y in enumerate((0, ny - 1)):
        face = load(d32, pl.ds(y, vectors * y_rows, stride=ny))
        send_y[side, pl.ds(0, vectors * y_rows), :] = face.astype(BF16)
        stage[...] = jnp.zeros_like(stage)
        stage[pl.ds(0, y_rows), :] = load(r32, pl.ds(y, y_rows, stride=ny))
        send_y[side, pl.ds(vectors * y_rows, 16), :] = stage[pl.ds(0, 16), :].astype(BF16)
    for side_x, x in enumerate((0, nx - 1)):
        for side_y, y in enumerate((0, ny - 1)):
            stage[...] = jnp.zeros_like(stage)
            at = x * ny + y
            stage[pl.ds(0, vectors * comps), :] = load(d32, pl.ds(at, vectors * comps, stride=cells))
            stage[pl.ds(vectors * comps, comps), :] = load(r32, pl.ds(at, comps, stride=cells))
            send_c[side_x * 2 + side_y] = stage[...].astype(BF16)

    total_rows = places.shape[0]
    fixed = own_rows + 2 * x_rows
    group = quotient(iota((1, 3 * own_rows), 1), cells, 3 * comps)
    lanes_of = [group == g for g in range(3 * comps)]
    coupling = []
    for j in range(comps):
        for d in range(9):
            line = jnp.zeros((1, 3 * own_rows), F32)
            for oz in range(3):
                for i in range(comps):
                    line = jnp.where(lanes_of[oz * comps + i], stencil[i, j, d * 3 + oz], line)
            coupling.append(line)
    chunks = [(j * cells, cells, j) for j in range(comps)]
    for side in range(2):
        chunks += [(own_rows + side * x_rows + j * ny, ny, j) for j in range(comps)]
    chunks.append((fixed, total_rows - fixed, None))
    for start, size, j in chunks:
        here = places[pl.ds(start, size), :]
        value = jnp.zeros(here.shape, F32)
        for e in range(comps * 9) if j is None else range(j * 9, j * 9 + 9):
            value = jnp.where(here == e, coupling[e], value)
        s_parts[pl.ds(start, size), :] = value
    s_high, s_low = split(s_parts[...])

    pl.semaphore_wait(barrier, n - 1)

    def wave(number):
        def one(k, device):
            pltpu.make_async_remote_copy(
                src_ref=message.at[number],
                dst_ref=slots.at[number, k],
                send_sem=wave_send.at[number],
                recv_sem=wave_recv.at[number],
                device_id=device,
                device_id_type=MESH,
            ).start()

        to_others(one)

    def wave_sum(number):
        pltpu.make_async_copy(slots.at[number], slots.at[number], wave_recv.at[number]).wait()
        return lax.fori_loop(
            0,
            n - 1,
            lambda k, total: total + slots[number, k],
            message[number],
            unroll=n <= 32,
        )

    wave(0)

    def copies():
        found = []
        for side, shift in enumerate((-1, 1)):
            found.append((send_x.at[side], recv_x.at[1 - side], recv_x.at[side], shift, 0))
        for side, shift in enumerate((-1, 1)):
            found.append((send_y.at[side], recv_y.at[1 - side], recv_y.at[side], 0, shift))
        for side_x, shift_x in enumerate((-1, 1)):
            for side_y, shift_y in enumerate((-1, 1)):
                at = side_x * 2 + side_y
                found.append((send_c.at[at], recv_c.at[3 - at], recv_c.at[at], shift_x, shift_y))
        return found

    opposite = (1, 0, 3, 2, 7, 6, 5, 4)

    def inside(shift_x, shift_y):
        along_x = (row + shift_x >= 0) & (row + shift_x < narrow)
        along_y = (column + shift_y >= 0) & (column + shift_y < wide)
        return along_x & along_y

    def face_copy(k, source, target, shift_x, shift_y):
        return pltpu.make_async_remote_copy(
            src_ref=source,
            dst_ref=target,
            send_sem=send_sems.at[k],
            recv_sem=recv_sems.at[opposite[k]],
            device_id=(row + shift_x, column + shift_y),
            device_id_type=MESH,
        )

    for k, (source, target, _, shift_x, shift_y) in enumerate(copies()):

        @pl.when(inside(shift_x, shift_y))
        def _(k=k, source=source, target=target, shift_x=shift_x, shift_y=shift_y):
            face_copy(k, source, target, shift_x, shift_y).start()

    factors[me] = factor[...]

    def send_factor(k, device):
        pltpu.make_async_remote_copy(
            src_ref=factor,
            dst_ref=factors.at[me],
            send_sem=wave_send.at[2],
            recv_sem=wave_recv.at[2],
            device_id=device,
            device_id_type=MESH,
        ).start()

    to_others(send_factor)

    lane = iota((own_rows, depth), 1)
    scale = jnp.concatenate([stiffness[...].reshape(cells, depth)] * comps, axis=0)
    weight = jnp.concatenate([mass[...].reshape(cells, depth)] * comps, axis=0)
    for a in range(vectors):
        d = load(d32, pl.ds(a * own_rows, own_rows))
        w = d * scale
        before = jnp.where(lane == depth - 1, 0.0, pltpu.roll(w, depth - 1, axis=1))
        after = jnp.where(lane == 0, 0.0, pltpu.roll(w, 1, axis=1))
        for oz, shifted in enumerate((before, w, after)):
            high, low = split(shifted)
            w_parts[a % 2, 0, pl.ds(oz * own_rows, own_rows), :] = high
            w_parts[a % 2, 1, pl.ds(oz * own_rows, own_rows), :] = low
        high = w_parts[a % 2, 0]
        low = w_parts[a % 2, 1]
        image = (
            jnp.dot(s_high, high, preferred_element_type=F32)
            + jnp.dot(s_high, low, preferred_element_type=F32)
            + jnp.dot(s_low, high, preferred_element_type=F32)
        )
        t32[a] = image
        t32[a, pl.ds(0, own_rows), :] = image[:own_rows] + weight * d

    width = 9 * vectors

    def picked(product, row_of, left_size):
        columns = product.shape[1]
        kept = iota((left_size, columns), 0) == row_of(iota((1, columns), 1))
        parts = product.reshape(vectors, left_size, columns)
        return jnp.sum(jnp.where(kept[None], parts, 0.0), axis=1)

    def folded(values, lane_of):
        rows = values.shape[1]
        chosen = (lane_of(iota((rows, 1), 0)) == iota((rows, width), 1)).astype(F32)
        return jnp.dot(values, chosen, preferred_element_type=F32, precision=HIGHEST)

    def within(size):
        return lambda c: c - size * quotient(c, size, vectors)

    def lane_in(block, size):
        return lambda c: block * vectors + quotient(c, size, vectors)

    total = None
    for j in range(comps):
        left = t32[:, pl.ds(j * cells, cells), :].reshape(vectors * cells, depth)
        right = jnp.concatenate(
            [load(d32, pl.ds((b * comps + j) * cells, cells)) for b in range(vectors)], axis=0
        ).astype(BF16)
        part = gram(left, right)
        total = part if total is None else total + part
    blocks = folded(picked(total, within(cells), cells), lane_in(4, cells))

    for k, (source, target, landing, shift_x, shift_y) in enumerate(copies()):

        @pl.when(inside(shift_x, shift_y))
        def _(k=k, source=source, landing=landing, shift_x=shift_x, shift_y=shift_y):
            pltpu.make_async_remote_copy(
                src_ref=source,
                dst_ref=landing,
                send_sem=send_sems.at[k],
                recv_sem=recv_sems.at[k],
                device_id=(row + shift_x, column + shift_y),
                device_id_type=MESH,
            ).wait()

        @pl.when(jnp.logical_not(inside(shift_x, shift_y)))
        def _(landing=landing):
            landing[...] = jnp.zeros(landing.shape, BF16)

    for side in range(2):
        block = 1 if side == 0 else 7
        left = t32[:, pl.ds(own_rows + side * x_rows, x_rows), :].reshape(vectors * x_rows, depth)
        part = gram(left, recv_x[side, pl.ds(0, vectors * x_rows), :])
        blocks += folded(picked(part, within(x_rows), x_rows), lane_in(block, x_rows))
    y_padded = pad_to(y_rows, 8)
    for side in range(2):
        block = 3 if side == 0 else 5
        left = t32[:, pl.ds(fixed + side * y_padded, y_padded), :]
        left = left.reshape(vectors * y_padded, depth)
        part = gram(left, recv_y[side, pl.ds(0, vectors * y_rows), :])
        blocks += folded(picked(part, within(y_rows), y_padded), lane_in(block, y_rows))
    c_padded = pad_to(4 * comps, 8)
    left = t32[:, pl.ds(fixed + 2 * y_padded, c_padded), :].reshape(vectors * c_padded, depth)
    part = gram(left, recv_c[...].reshape(4 * 32, depth))

    def corner_parts(c):
        corner = quotient(c, 32, 4)
        at = c - 32 * corner
        vector = quotient(at, comps, vectors)
        return at < vectors * comps, corner, vector, at - comps * vector

    def corner_row(c):
        real, corner, _, j = corner_parts(c)
        return jnp.where(real, corner * comps + j, -1)

    def corner_lane(c):
        real, corner, vector, _ = corner_parts(c)
        block = corner * 2 + jnp.where(corner >= 2, 2, 0)
        return jnp.where(real, block * vectors + vector, -1)

    blocks += folded(picked(part, corner_row, c_padded), corner_lane)

    pairs = vectors * vectors
    repeated = jnp.broadcast_to(blocks[:, None, :], (vectors, vectors, width))
    right = iota((1, vectors, width), 2)
    right = right - vectors * quotient(right, vectors, 9)
    kept = jnp.where(right == iota((1, vectors, width), 1), repeated, 0.0).reshape(pairs, width)
    neighbour = quotient(iota((width, 1), 0), vectors, 9)
    to_lane = (neighbour == iota((width, 9), 1)).astype(F32)
    turned_blocks = jnp.dot(kept, to_lane, preferred_element_type=F32, precision=HIGHEST)
    blocks_out[0, 0] = turned_blocks.reshape(vectors, vectors, 9)

    coarse_rhs = wave_sum(0)
    pltpu.make_async_copy(
        factors.at[pl.ds(0, n - 1)], factors.at[pl.ds(0, n - 1)], wave_recv.at[2]
    ).wait()

    def solve(vector):
        def one(d, total):
            f = factors[d]
            return total + f * jnp.sum(f * vector, axis=1, keepdims=True)

        zeros = jnp.zeros((factor.shape[0], order), F32)
        total = lax.fori_loop(0, n, one, zeros, unroll=n <= 32)
        return jnp.sum(total, axis=0, keepdims=True)

    first = solve(coarse_rhs)
    near = [
        iota((vectors, order), 1) == listing[0, 0, k] * vectors + iota((vectors, order), 0)
        for k in range(9)
    ]
    spread = jnp.concatenate([m.astype(F32) for m in near], axis=0)
    matrix_rows = jnp.dot(blocks, spread, preferred_element_type=F32, precision=HIGHEST)
    message[1] = placed(jnp.sum(matrix_rows * first, axis=1, keepdims=True))
    wave(1)

    high_y = ny + 2

    def ext_at(j, f, e):
        return (j * high_y + f) * 8 + e

    for j in range(comps):
        for y in range(ny):
            values = load(r32, pl.ds(j * cells + y, nx, stride=ny))
            store(ext, values, pl.ds(ext_at(j, 1 + y, 1), nx))
    for side in range(2):
        at_x = side * (nx + 1)
        values = recv_x[side, pl.ds(vectors * x_rows, 32), :].astype(F32)
        for j in range(comps):
            for y in range(ny):
                line = values[j * ny + y : j * ny + y + 1]
                store(ext, line, pl.ds(ext_at(j, 1 + y, at_x), 1))
        at_y = side * (ny + 1)
        values = recv_y[side, pl.ds(vectors * y_rows, 16), :].astype(F32)
        for j in range(comps):
            store(ext, values[j * nx : (j + 1) * nx], pl.ds(ext_at(j, at_y, 1), nx))
        for side_y in range(2):
            values = recv_c[side * 2 + side_y].astype(F32)
            for j in range(comps):
                at = vectors * comps + j
                line = values[at : at + 1]
                store(ext, line, pl.ds(ext_at(j, side_y * (ny + 1), at_x), 1))

    half_x = (nx + 2) // 2
    half_y = (ny + 2) // 2
    kept_x = []
    for s in range(2):
        e = 2 * iota((half_x, depth), 0) + s
        kept_x.append((e >= margins[0, 0, 0, 0]) & (e < margins[0, 0, 0, 1]))
    inverse_copy.wait()
    for v in range(half_y):
        grouped = []
        for j in range(comps):
            for s in range(2):
                for t in range(2):
                    f = 2 * v + t
                    kept = (f >= margins[0, 0, 1, 0]) & (f < margins[0, 0, 1, 1])
                    factor_y = jnp.where(kept, 1.0, 0.0).astype(F32)
                    values = load(ext, pl.ds(ext_at(j, f, s), half_x, stride=2))
                    grouped.append(jnp.where(kept_x[s], values, 0.0) * factor_y)
        for j in range(comps):
            for s in range(2):
                for t in range(2):
                    f = 2 * v + t
                    if f == 0 or f == ny + 1:
                        continue
                    i = 4 * j + 2 * s + t
                    acc = inverse[i, 0, v].astype(F32) * grouped[0]
                    for m in range(1, 4 * comps):
                        acc += inverse[i, m, v].astype(F32) * grouped[m]
                    store(loc, acc, pl.ds(ext_at(j, f, s), half_x, stride=2))

    coarse_image = wave_sum(1)
    refined = first + solve(coarse_rhs - coarse_image)
    solution_out[...] = refined
    weights = jnp.sum(jnp.where(own_place, refined, 0.0), axis=1, keepdims=True)
    for j in range(comps):
        for x in range(nx):
            value = load(loc, pl.ds(ext_at(j, 1, 1 + x), ny, stride=8))
            for a in range(vectors):
                at = (a * comps + j) * cells + x * ny
                value += weights[a : a + 1, :] * load(d32, pl.ds(at, ny))
            out[j, x] = value

    for number in range(2):
        pltpu.make_async_copy(slots.at[number], slots.at[number], wave_send.at[number]).wait()
    pltpu.make_async_copy(
        factors.at[pl.ds(0, n - 1)], factors.at[pl.ds(0, n - 1)], wave_send.at[2]
    ).wait()


def body(
    narrow,
    wide,
    deflation,
    residual,
    stiffness,
    mass,
    stencil,
    local_inverse,
    inverse_factor,
    margin_range,
    neighbor_blocks,
):
    vectors, comps, nx, ny, depth = deflation.shape
    n = narrow * wide
    order = inverse_factor.shape[1]
    cells = nx * ny
    places = stencil_places(comps, nx, ny)
    turned_inverse = local_inverse.transpose(0, 1, 3, 2, 4)
    x_send = vectors * comps * ny + 32
    y_send = vectors * comps * nx + 16
    vmem = pl.BlockSpec(memory_space=pltpu.VMEM)
    smem = pl.BlockSpec(memory_space=pltpu.SMEM)
    result, blocks, refined = pl.pallas_call(
        functools.partial(kernel, narrow, wide, vectors, comps, nx, ny, depth),
        out_shape=(
            jax.ShapeDtypeStruct(residual.shape, F32),
            jax.ShapeDtypeStruct((1, 1, vectors, vectors, 9), F32),
            jax.ShapeDtypeStruct((1, order), F32),
        ),
        in_specs=[vmem] * 5 + [smem, pl.BlockSpec(memory_space=pl.ANY), vmem, smem, smem],
        out_specs=(vmem, vmem, vmem),
        scratch_shapes=[
            pltpu.VMEM(turned_inverse.shape, BF16),
            pltpu.VMEM((depth // 128, vectors * comps * cells, 128), F32),
            pltpu.VMEM((depth // 128, comps * cells, 128), F32),
            pltpu.VMEM((vectors, places.shape[0], depth), F32),
            pltpu.VMEM(places.shape, F32),
            pltpu.VMEM((2, 2, 3 * comps * cells, depth), BF16),
            pltpu.VMEM((32, depth), F32),
            pltpu.VMEM((depth // 128, comps * (ny + 2) * 8, 128), F32),
            pltpu.VMEM((depth // 128, comps * (ny + 2) * 8, 128), F32),
            pltpu.VMEM((2, x_send, depth), BF16),
            pltpu.VMEM((2, y_send, depth), BF16),
            pltpu.VMEM((4, 32, depth), BF16),
            pltpu.VMEM((2, x_send, depth), BF16),
            pltpu.VMEM((2, y_send, depth), BF16),
            pltpu.VMEM((4, 32, depth), BF16),
            pltpu.VMEM((n,) + inverse_factor.shape, F32),
            pltpu.VMEM((2, 1, order), F32),
            pltpu.VMEM((2, n - 1, 1, order), F32),
            pltpu.SemaphoreType.DMA,
            pltpu.SemaphoreType.DMA((8,)),
            pltpu.SemaphoreType.DMA((8,)),
            pltpu.SemaphoreType.DMA((3,)),
            pltpu.SemaphoreType.DMA((3,)),
        ],
        compiler_params=pltpu.CompilerParams(
            collective_id=0, has_side_effects=True, vmem_limit_bytes=60 * 1024 * 1024
        ),
    )(
        deflation,
        residual,
        stiffness,
        mass,
        jnp.asarray(places),
        stencil.transpose(1, 2, 0),
        turned_inverse,
        inverse_factor,
        margin_range,
        neighbor_blocks,
    )
    return result, blocks.transpose(0, 1, 4, 2, 3), refined.reshape(order)


def solution(mesh):
    placed = (
        P(None, None, "narrow", "wide", None),
        P(None, "narrow", "wide", None),
        P("narrow", "wide", None),
        P("narrow", "wide", None),
        P(),
        P(None, None, "narrow", "wide", None),
        P(("narrow", "wide"), None),
        P("narrow", "wide", None, None),
        P("narrow", "wide", None),
    )
    return jax.shard_map(
        functools.partial(body, mesh.shape["narrow"], mesh.shape["wide"]),
        mesh=mesh,
        in_specs=placed,
        out_specs=(P(None, "narrow", "wide", None), P("narrow", "wide", None, None, None), P()),
        check_vma=False,
    )
```

```python
import functools

import jax
import jax.numpy as jnp
import numpy as np
from jax import lax
from jax.experimental import pallas as pl
from jax.experimental.pallas import tpu as pltpu
from jax.sharding import PartitionSpec as P

F32 = jnp.float32
BF16 = jnp.bfloat16
HIGHEST = lax.Precision.HIGHEST
MESH = pl.DeviceIdType.MESH


def pad_to(count, unit):
    return -(-count // unit) * unit


def stencil_places(comps, nx, ny):
    rows = []
    for j in range(comps):
        rows += [(j, x, y) for x in range(nx) for y in range(ny)]
    for x in (-1, nx):
        rows += [(j, x, y) for j in range(comps) for y in range(ny)]
    for y in (-1, ny):
        face = [(j, x, y) for j in range(comps) for x in range(nx)]
        rows += face + [None] * (pad_to(len(face), 8) - len(face))
    corners = [(j, x, y) for x in (-1, nx) for y in (-1, ny) for j in range(comps)]
    rows += corners + [None] * (pad_to(len(corners), 8) - len(corners))
    cells = comps * nx * ny
    table = np.full((len(rows), 3 * cells), -1, np.int32)
    for r, row in enumerate(rows):
        if row is None:
            continue
        j, x, y = row
        for oz in range(3):
            for i in range(comps):
                for px in range(nx):
                    for py in range(ny):
                        dx, dy = x - px, y - py
                        if abs(dx) <= 1 and abs(dy) <= 1:
                            column = oz * cells + i * nx * ny + px * ny + py
                            table[r, column] = j * 9 + (dx + 1) * 3 + dy + 1
    return table


def split(values):
    high = values.astype(BF16)
    return high, (values - high.astype(F32)).astype(BF16)


def iota(shape, axis):
    return lax.broadcasted_iota(jnp.int32, shape, axis)


def load(ref, *at):
    return jnp.concatenate([ref[(h,) + at] for h in range(ref.shape[0])], axis=-1)


def store(ref, values, *at):
    for h in range(ref.shape[0]):
        ref[(h,) + at] = values[:, h * 128 : (h + 1) * 128]


def quotient(values, size, count):
    return sum((values >= k * size).astype(jnp.int32) for k in range(1, count))


def gram(left, right):
    dims = (((1,), (1,)), ((), ()))
    high, low = split(left)
    return lax.dot_general(high, right, dims, preferred_element_type=F32) + lax.dot_general(
        low, right, dims, preferred_element_type=F32
    )


def kernel(
    narrow,
    wide,
    vectors,
    comps,
    nx,
    ny,
    depth,
    deflation,
    residual,
    stiffness,
    mass,
    places,
    stencil,
    inverse_hbm,
    factor,
    margins,
    listing,
    out,
    blocks_out,
    solution_out,
    inverse,
    d32,
    r32,
    t32,
    s_parts,
    stage,
    ext,
    loc,
    send_x,
    send_y,
    send_c,
    recv_x,
    recv_y,
    recv_c,
    factors,
    message,
    slots,
    inverse_sem,
    send_sems,
    recv_sems,
    wave_send,
    wave_recv,
):
    n = narrow * wide
    order = factor.shape[1]
    row = lax.axis_index("narrow")
    column = lax.axis_index("wide")
    me = row * wide + column
    cells = nx * ny
    own_rows = comps * cells

    def turned(here, count):
        places_of = [here + k for k in range(count)]
        return [jnp.where(at >= count, at - count, at) for at in places_of]

    target_rows = turned(row, narrow)

    target_columns = turned(column, wide)

    def to_others(act, step=1):
        for k in range(step, n, step):
            act(k // step - 1, (target_rows[k // wide], target_columns[k % wide]))
    barrier = pltpu.get_barrier_semaphore()

    def greet(k, device):
        pl.semaphore_signal(barrier, inc=1, device_id=device, device_id_type=MESH)

    to_others(greet)

    inverse_copy = pltpu.make_async_copy(inverse_hbm, inverse, inverse_sem)
    inverse_copy.start()

    rounded = residual[...].astype(BF16).astype(F32).reshape(own_rows, depth)
    store(r32, rounded, pl.ds(0, own_rows))

    def rows_of(a):
        return pl.ds(pl.multiple_of(a * own_rows, own_rows), own_rows)

    def widen(a, carry):
        d = deflation[a].astype(F32).reshape(own_rows, depth)
        store(d32, d, rows_of(a))
        stage[pl.ds(a, 1), :] = jnp.sum(d * rounded, axis=0, keepdims=True)
        return carry

    lax.fori_loop(0, vectors, widen, 0, unroll=2)
    rhs_column = jnp.sum(stage[pl.ds(0, vectors), :], axis=1, keepdims=True)
    own_block = listing[0, 0, 4]
    own_place = iota((vectors, order), 1) == own_block * vectors + iota((vectors, order), 0)

    def placed(values):
        return jnp.sum(jnp.where(own_place, values, 0.0), axis=0, keepdims=True)

    message[0] = placed(rhs_column)

    x_rows = comps * ny
    y_rows = comps * nx
    for side, x in enumerate((0, nx - 1)):
        face = [
            load(d32, pl.ds((a * comps + j) * cells + x * ny, ny))
            for a in range(vectors)
            for j in range(comps)
        ]
        send_x[side, pl.ds(0, vectors * x_rows), :] = jnp.concatenate(face, axis=0).astype(BF16)
        stage[...] = jnp.zeros_like(stage)
        for j in range(comps):
            stage[pl.ds(j * ny, ny), :] = load(r32, pl.ds(j * cells + x * ny, ny))
        send_x[side, pl.ds(vectors * x_rows, 32), :] = stage[...].astype(BF16)
    for side, y in enumerate((0, ny - 1)):
        face = load(d32, pl.ds(y, vectors * y_rows, stride=ny))
        send_y[side, pl.ds(0, vectors * y_rows), :] = face.astype(BF16)
        stage[...] = jnp.zeros_like(stage)
        stage[pl.ds(0, y_rows), :] = load(r32, pl.ds(y, y_rows, stride=ny))
        send_y[side, pl.ds(vectors * y_rows, 16), :] = stage[pl.ds(0, 16), :].astype(BF16)
    for side_x, x in enumerate((0, nx - 1)):
        for side_y, y in enumerate((0, ny - 1)):
            stage[...] = jnp.zeros_like(stage)
            at = x * ny + y
            stage[pl.ds(0, vectors * comps), :] = load(d32, pl.ds(at, vectors * comps, stride=cells))
            stage[pl.ds(vectors * comps, comps), :] = load(r32, pl.ds(at, comps, stride=cells))
            send_c[side_x * 2 + side_y] = stage[...].astype(BF16)

    total_rows = places.shape[0]
    fixed = own_rows + 2 * x_rows
    group = quotient(iota((1, 3 * own_rows), 1), cells, 3 * comps)
    lanes_of = [group == g for g in range(3 * comps)]
    coupling = []
    for j in range(comps):
        for d in range(9):
            line = jnp.zeros((1, 3 * own_rows), F32)
            for oz in range(3):
                for i in range(comps):
                    line = jnp.where(lanes_of[oz * comps + i], stencil[i, j, d * 3 + oz], line)
            coupling.append(line)
    chunks = [(j * cells, cells, j) for j in range(comps)]
    for side in range(2):
        chunks += [(own_rows + side * x_rows + j * ny, ny, j) for j in range(comps)]
    chunks.append((fixed, total_rows - fixed, None))
    for start, size, j in chunks:
        here = places[pl.ds(start, size), :]
        value = jnp.zeros(here.shape, F32)
        for e in range(comps * 9) if j is None else range(j * 9, j * 9 + 9):
            value = jnp.where(here == e, coupling[e], value)
        s_parts[pl.ds(start, size), :] = value
    s_high, s_low = split(s_parts[...])

    pl.semaphore_wait(barrier, n - 1)

    def wave(number):
        def one(k, device):
            pltpu.make_async_remote_copy(
                src_ref=message.at[number],
                dst_ref=slots.at[number, k],
                send_sem=wave_send.at[number],
                recv_sem=wave_recv.at[number],
                device_id=device,
                device_id_type=MESH,
            ).start()

        to_others(one)

    def wave_sum(number):
        pltpu.make_async_copy(slots.at[number], slots.at[number], wave_recv.at[number]).wait()
        return lax.fori_loop(
            0,
            n - 1,
            lambda k, total: total + slots[number, k],
            message[number],
            unroll=n <= 32,
        )

    wave(0)

    def copies():
        found = []
        for side, shift in enumerate((-1, 1)):
            found.append((send_x.at[side], recv_x.at[1 - side], recv_x.at[side], shift, 0))
        for side, shift in enumerate((-1, 1)):
            found.append((send_y.at[side], recv_y.at[1 - side], recv_y.at[side], 0, shift))
        for side_x, shift_x in enumerate((-1, 1)):
            for side_y, shift_y in enumerate((-1, 1)):
                at = side_x * 2 + side_y
                found.append((send_c.at[at], recv_c.at[3 - at], recv_c.at[at], shift_x, shift_y))
        return found

    opposite = (1, 0, 3, 2, 7, 6, 5, 4)

    def inside(shift_x, shift_y):
        along_x = (row + shift_x >= 0) & (row + shift_x < narrow)
        along_y = (column + shift_y >= 0) & (column + shift_y < wide)
        return along_x & along_y

    def face_copy(k, source, target, shift_x, shift_y):
        return pltpu.make_async_remote_copy(
            src_ref=source,
            dst_ref=target,
            send_sem=send_sems.at[k],
            recv_sem=recv_sems.at[opposite[k]],
            device_id=(row + shift_x, column + shift_y),
            device_id_type=MESH,
        )

    for k, (source, target, _, shift_x, shift_y) in enumerate(copies()):

        @pl.when(inside(shift_x, shift_y))
        def _(k=k, source=source, target=target, shift_x=shift_x, shift_y=shift_y):
            face_copy(k, source, target, shift_x, shift_y).start()

    parity = lax.rem(column, 2)
    half_index = row * (wide // 2) + column // 2
    partner = (row, column + 1 - 2 * parity)
    factors[parity, half_index] = factor[...]

    def send_factor(k, device):
        pltpu.make_async_remote_copy(
            src_ref=factor,
            dst_ref=factors.at[parity, half_index],
            send_sem=wave_send.at[2],
            recv_sem=wave_recv.at[2],
            device_id=device,
            device_id_type=MESH,
        ).start()

    to_others(send_factor, 2)

    def others_rows():
        some = factors.at[0, pl.ds(0, n // 2 - 1)]
        return some, some

    lane = iota((own_rows, depth), 1)
    scale = jnp.concatenate([stiffness[...].reshape(cells, depth)] * comps, axis=0)
    weight = jnp.concatenate([mass[...].reshape(cells, depth)] * comps, axis=0)

    def adjoint(a, carry):
        d = load(d32, rows_of(a))
        w = d * scale
        before = jnp.where(lane == depth - 1, 0.0, pltpu.roll(w, depth - 1, axis=1))
        after = jnp.where(lane == 0, 0.0, pltpu.roll(w, 1, axis=1))
        parts = [split(shifted) for shifted in (before, w, after)]
        high = jnp.concatenate([part[0] for part in parts], axis=0)
        low = jnp.concatenate([part[1] for part in parts], axis=0)
        image = (
            jnp.dot(s_high, high, preferred_element_type=F32)
            + jnp.dot(s_high, low, preferred_element_type=F32)
            + jnp.dot(s_low, high, preferred_element_type=F32)
        )
        t32[a, pl.ds(own_rows, total_rows - own_rows), :] = image[own_rows:]
        t32[a, pl.ds(0, own_rows), :] = image[:own_rows] + weight * d
        return carry

    lax.fori_loop(0, vectors, adjoint, 0, unroll=2)

    some, same = others_rows()
    pltpu.make_async_copy(some, same, wave_recv.at[2]).wait()
    hand_on = pltpu.make_async_remote_copy(
        src_ref=factors.at[parity],
        dst_ref=factors.at[parity],
        send_sem=wave_send.at[3],
        recv_sem=wave_recv.at[3],
        device_id=partner,
        device_id_type=MESH,
    )
    hand_on.start()

    width = 9 * vectors

    def picked(product, row_of, left_size):
        columns = product.shape[1]
        kept = iota((left_size, columns), 0) == row_of(iota((1, columns), 1))
        parts = product.reshape(vectors, left_size, columns)
        return jnp.sum(jnp.where(kept[None], parts, 0.0), axis=1)

    def folded(values, lane_of):
        rows = values.shape[1]
        chosen = (lane_of(iota((rows, 1), 0)) == iota((rows, width), 1)).astype(F32)
        return jnp.dot(values, chosen, preferred_element_type=F32, precision=HIGHEST)

    def within(size):
        return lambda c: c - size * quotient(c, size, vectors)

    def lane_in(block, size):
        return lambda c: block * vectors + quotient(c, size, vectors)

    total = None
    for j in range(comps):
        left = t32[:, pl.ds(j * cells, cells), :].reshape(vectors * cells, depth)
        right = jnp.concatenate(
            [load(d32, pl.ds((b * comps + j) * cells, cells)) for b in range(vectors)], axis=0
        ).astype(BF16)
        part = gram(left, right)
        total = part if total is None else total + part
    blocks = folded(picked(total, within(cells), cells), lane_in(4, cells))

    for k, (source, target, landing, shift_x, shift_y) in enumerate(copies()):

        @pl.when(inside(shift_x, shift_y))
        def _(k=k, source=source, landing=landing, shift_x=shift_x, shift_y=shift_y):
            pltpu.make_async_remote_copy(
                src_ref=source,
                dst_ref=landing,
                send_sem=send_sems.at[k],
                recv_sem=recv_sems.at[k],
                device_id=(row + shift_x, column + shift_y),
                device_id_type=MESH,
            ).wait()

        @pl.when(jnp.logical_not(inside(shift_x, shift_y)))
        def _(landing=landing):
            landing[...] = jnp.zeros(landing.shape, BF16)

    for side in range(2):
        block = 1 if side == 0 else 7
        left = t32[:, pl.ds(own_rows + side * x_rows, x_rows), :].reshape(vectors * x_rows, depth)
        part = gram(left, recv_x[side, pl.ds(0, vectors * x_rows), :])
        blocks += folded(picked(part, within(x_rows), x_rows), lane_in(block, x_rows))
    y_padded = pad_to(y_rows, 8)
    for side in range(2):
        block = 3 if side == 0 else 5
        left = t32[:, pl.ds(fixed + side * y_padded, y_padded), :]
        left = left.reshape(vectors * y_padded, depth)
        part = gram(left, recv_y[side, pl.ds(0, vectors * y_rows), :])
        blocks += folded(picked(part, within(y_rows), y_padded), lane_in(block, y_rows))
    c_padded = pad_to(4 * comps, 8)
    left = t32[:, pl.ds(fixed + 2 * y_padded, c_padded), :].reshape(vectors * c_padded, depth)
    part = gram(left, recv_c[...].reshape(4 * 32, depth))

    def corner_parts(c):
        corner = quotient(c, 32, 4)
        at = c - 32 * corner
        vector = quotient(at, comps, vectors)
        return at < vectors * comps, corner, vector, at - comps * vector

    def corner_row(c):
        real, corner, _, j = corner_parts(c)
        return jnp.where(real, corner * comps + j, -1)

    def corner_lane(c):
        real, corner, vector, _ = corner_parts(c)
        block = corner * 2 + jnp.where(corner >= 2, 2, 0)
        return jnp.where(real, block * vectors + vector, -1)

    blocks += folded(picked(part, corner_row, c_padded), corner_lane)

    pairs = vectors * vectors
    repeated = jnp.broadcast_to(blocks[:, None, :], (vectors, vectors, width))
    right = iota((1, vectors, width), 2)
    right = right - vectors * quotient(right, vectors, 9)
    kept = jnp.where(right == iota((1, vectors, width), 1), repeated, 0.0).reshape(pairs, width)
    neighbour = quotient(iota((width, 1), 0), vectors, 9)
    to_lane = (neighbour == iota((width, 9), 1)).astype(F32)
    turned_blocks = jnp.dot(kept, to_lane, preferred_element_type=F32, precision=HIGHEST)
    blocks_out[0, 0] = turned_blocks.reshape(vectors, vectors, 9)

    coarse_rhs = wave_sum(0)
    hand_on.wait()

    def solve(vector):
        def one(d, total):
            for half in range(2):
                f = factors[half, d]
                total = total + f * jnp.sum(f * vector, axis=1, keepdims=True)
            return total

        zeros = jnp.zeros((factor.shape[0], order), F32)
        total = lax.fori_loop(0, n // 2, one, zeros, unroll=8)
        return jnp.sum(total, axis=0, keepdims=True)

    first = solve(coarse_rhs)
    near = [
        iota((vectors, order), 1) == listing[0, 0, k] * vectors + iota((vectors, order), 0)
        for k in range(9)
    ]
    spread = jnp.concatenate([m.astype(F32) for m in near], axis=0)
    matrix_rows = jnp.dot(blocks, spread, preferred_element_type=F32, precision=HIGHEST)
    message[1] = placed(jnp.sum(matrix_rows * first, axis=1, keepdims=True))
    wave(1)

    high_y = ny + 2

    def ext_at(j, f, e):
        return (j * high_y + f) * 8 + e

    for j in range(comps):
        for y in range(ny):
            values = load(r32, pl.ds(j * cells + y, nx, stride=ny))
            store(ext, values, pl.ds(ext_at(j, 1 + y, 1), nx))
    for side in range(2):
        at_x = side * (nx + 1)
        values = recv_x[side, pl.ds(vectors * x_rows, 32), :].astype(F32)
        for j in range(comps):
            for y in range(ny):
                line = values[j * ny + y : j * ny + y + 1]
                store(ext, line, pl.ds(ext_at(j, 1 + y, at_x), 1))
        at_y = side * (ny + 1)
        values = recv_y[side, pl.ds(vectors * y_rows, 16), :].astype(F32)
        for j in range(comps):
            store(ext, values[j * nx : (j + 1) * nx], pl.ds(ext_at(j, at_y, 1), nx))
        for side_y in range(2):
            values = recv_c[side * 2 + side_y].astype(F32)
            for j in range(comps):
                at = vectors * comps + j
                line = values[at : at + 1]
                store(ext, line, pl.ds(ext_at(j, side_y * (ny + 1), at_x), 1))

    half_x = (nx + 2) // 2
    half_y = (ny + 2) // 2
    kept_x = []
    for s in range(2):
        e = 2 * iota((half_x, depth), 0) + s
        kept_x.append((e >= margins[0, 0, 0, 0]) & (e < margins[0, 0, 0, 1]))
    inverse_copy.wait()

    def local_row(v, carry):
        grouped = []
        for j in range(comps):
            for s in range(2):
                for t in range(2):
                    f = 2 * v + t
                    kept = (f >= margins[0, 0, 1, 0]) & (f < margins[0, 0, 1, 1])
                    factor_y = jnp.where(kept, 1.0, 0.0).astype(F32)
                    values = load(ext, pl.ds(ext_at(j, f, s), half_x, stride=2))
                    grouped.append(jnp.where(kept_x[s], values, 0.0) * factor_y)
        for j in range(comps):
            for s in range(2):
                for t in range(2):
                    i = 4 * j + 2 * s + t
                    acc = inverse[i, 0, v].astype(F32) * grouped[0]
                    for m in range(1, 4 * comps):
                        acc += inverse[i, m, v].astype(F32) * grouped[m]
                    store(loc, acc, pl.ds(ext_at(j, 2 * v + t, s), half_x, stride=2))
        return carry

    lax.fori_loop(0, half_y, local_row, 0)

    coarse_image = wave_sum(1)
    refined = first + solve(coarse_rhs - coarse_image)
    solution_out[...] = refined
    weights = jnp.sum(jnp.where(own_place, refined, 0.0), axis=1, keepdims=True)
    for j in range(comps):
        for x in range(nx):
            value = load(loc, pl.ds(ext_at(j, 1, 1 + x), ny, stride=8))
            for a in range(vectors):
                at = (a * comps + j) * cells + x * ny
                value += weights[a : a + 1, :] * load(d32, pl.ds(at, ny))
            out[j, x] = value

    for number in range(2):
        pltpu.make_async_copy(slots.at[number], slots.at[number], wave_send.at[number]).wait()
    pltpu.make_async_copy(some, same, wave_send.at[2]).wait()


def write_out(*refs):
    sources, targets, sems = refs[:3], refs[3:6], refs[6]
    copies = [
        pltpu.make_async_copy(source, target, sems.at[k])
        for k, (source, target) in enumerate(zip(sources, targets))
    ]
    for copy in copies:
        copy.start()
    for copy in copies:
        copy.wait()


def body(
    narrow,
    wide,
    deflation,
    residual,
    stiffness,
    mass,
    stencil,
    local_inverse,
    inverse_factor,
    margin_range,
    neighbor_blocks,
):
    vectors, comps, nx, ny, depth = deflation.shape
    n = narrow * wide
    order = inverse_factor.shape[1]
    cells = nx * ny
    places = stencil_places(comps, nx, ny)
    turned_inverse = local_inverse.transpose(0, 1, 3, 2, 4)
    x_send = vectors * comps * ny + 32
    y_send = vectors * comps * nx + 16
    vmem = pl.BlockSpec(memory_space=pltpu.VMEM)
    smem = pl.BlockSpec(memory_space=pltpu.SMEM)
    results = pl.pallas_call(
        functools.partial(kernel, narrow, wide, vectors, comps, nx, ny, depth),
        out_shape=(
            jax.ShapeDtypeStruct(residual.shape, F32),
            jax.ShapeDtypeStruct((1, 1, vectors, vectors, 9), F32),
            jax.ShapeDtypeStruct((1, order), F32),
        ),
        in_specs=[vmem] * 5 + [smem, pl.BlockSpec(memory_space=pltpu.HBM), vmem, smem, smem],
        out_specs=(vmem, vmem, vmem),
        scratch_shapes=[
            pltpu.VMEM(turned_inverse.shape, BF16),
            pltpu.VMEM((depth // 128, vectors * comps * cells, 128), F32),
            pltpu.VMEM((depth // 128, comps * cells, 128), F32),
            pltpu.VMEM((vectors, places.shape[0], depth), F32),
            pltpu.VMEM(places.shape, F32),
            pltpu.VMEM((32, depth), F32),
            pltpu.VMEM((depth // 128, comps * (ny + 2) * 8, 128), F32),
            pltpu.VMEM((depth // 128, comps * (ny + 2) * 8, 128), F32),
            pltpu.VMEM((2, x_send, depth), BF16),
            pltpu.VMEM((2, y_send, depth), BF16),
            pltpu.VMEM((4, 32, depth), BF16),
            pltpu.VMEM((2, x_send, depth), BF16),
            pltpu.VMEM((2, y_send, depth), BF16),
            pltpu.VMEM((4, 32, depth), BF16),
            pltpu.VMEM((2, n // 2) + inverse_factor.shape, F32),
            pltpu.VMEM((2, 1, order), F32),
            pltpu.VMEM((2, n - 1, 1, order), F32),
            pltpu.SemaphoreType.DMA,
            pltpu.SemaphoreType.DMA((8,)),
            pltpu.SemaphoreType.DMA((8,)),
            pltpu.SemaphoreType.DMA((4,)),
            pltpu.SemaphoreType.DMA((4,)),
        ],
        compiler_params=pltpu.CompilerParams(
            collective_id=0, has_side_effects=True, vmem_limit_bytes=40 * 1024 * 1024
        ),
    )(
        deflation,
        residual,
        stiffness,
        mass,
        jnp.asarray(places),
        stencil.transpose(1, 2, 0),
        turned_inverse,
        inverse_factor,
        margin_range,
        neighbor_blocks,
    )
    result, blocks, refined = pl.pallas_call(
        write_out,
        out_shape=tuple(jax.ShapeDtypeStruct(r.shape, r.dtype) for r in results),
        in_specs=[vmem] * 3,
        out_specs=tuple(pl.BlockSpec(memory_space=pltpu.HBM) for _ in results),
        scratch_shapes=[pltpu.SemaphoreType.DMA((3,))],
    )(*results)
    return result, blocks.transpose(0, 1, 4, 2, 3), refined.reshape(order)


def solution(mesh):
    placed = (
        P(None, None, "narrow", "wide", None),
        P(None, "narrow", "wide", None),
        P("narrow", "wide", None),
        P("narrow", "wide", None),
        P(),
        P(None, None, "narrow", "wide", None),
        P(("narrow", "wide"), None),
        P("narrow", "wide", None, None),
        P("narrow", "wide", None),
    )
    return jax.shard_map(
        functools.partial(body, mesh.shape["narrow"], mesh.shape["wide"]),
        mesh=mesh,
        in_specs=placed,
        out_specs=(P(None, "narrow", "wide", None), P("narrow", "wide", None, None, None), P()),
        check_vma=False,
    )
```

```python
import functools

import jax
import jax.numpy as jnp
import numpy as np
from jax import lax
from jax.experimental import pallas as pl
from jax.experimental.pallas import tpu as pltpu
from jax.sharding import PartitionSpec as P

F32 = jnp.float32
BF16 = jnp.bfloat16
MESH = pl.DeviceIdType.MESH


def pad_to(count, unit):
    return -(-count // unit) * unit


def stencil_places(comps, nx, ny):
    rows = []
    for j in range(comps):
        rows += [(j, x, y) for x in range(nx) for y in range(ny)]
    for x in (-1, nx):
        rows += [(j, x, y) for j in range(comps) for y in range(ny)]
    for y in (-1, ny):
        face = [(j, x, y) for j in range(comps) for x in range(nx)]
        rows += face + [None] * (pad_to(len(face), 8) - len(face))
    corners = [(j, x, y) for x in (-1, nx) for y in (-1, ny) for j in range(comps)]
    rows += corners + [None] * (pad_to(len(corners), 8) - len(corners))
    cells = comps * nx * ny
    table = np.full((len(rows), 3 * cells), -1, np.int32)
    for r, row in enumerate(rows):
        if row is None:
            continue
        j, x, y = row
        for oz in range(3):
            for i in range(comps):
                for px in range(nx):
                    for py in range(ny):
                        dx, dy = x - px, y - py
                        if abs(dx) <= 1 and abs(dy) <= 1:
                            column = oz * cells + i * nx * ny + px * ny + py
                            table[r, column] = j * 9 + (dx + 1) * 3 + dy + 1
    return table


def split(values):
    high = values.astype(BF16)
    return high, (values - high.astype(F32)).astype(BF16)


def iota(shape, axis):
    return lax.broadcasted_iota(jnp.int32, shape, axis)


def load(ref, *at):
    return jnp.concatenate([ref[(h,) + at] for h in range(ref.shape[0])], axis=-1)


def store(ref, values, *at):
    for h in range(ref.shape[0]):
        ref[(h,) + at] = values[:, h * 128 : (h + 1) * 128]


def quotient(values, size, count):
    return sum((values >= k * size).astype(jnp.int32) for k in range(1, count))


def exact_dot(values, chosen):
    rows = values.shape[0]
    high = values.astype(BF16).astype(F32)
    middle = (values - high).astype(BF16).astype(F32)
    low = values - high - middle
    parts = jnp.concatenate([high, middle, low], axis=0).astype(BF16)
    product = jnp.dot(parts, chosen.astype(BF16), preferred_element_type=F32)
    return product[:rows] + product[rows : 2 * rows] + product[2 * rows :]


def gram(left, right):
    dims = (((1,), (1,)), ((), ()))
    high, low = split(left)
    return lax.dot_general(high, right, dims, preferred_element_type=F32) + lax.dot_general(
        low, right, dims, preferred_element_type=F32
    )


def kernel(
    narrow,
    wide,
    vectors,
    comps,
    nx,
    ny,
    depth,
    *refs,
):
    operands, results = refs[:10], refs[10:13]
    held, staged = refs[13:23], refs[23:26]
    deflation, residual, stiffness, mass, places, stencil = held[:6]
    inverse, factor, margins, listing = held[6:]
    out, blocks_out, solution_out = staged
    (
        d32,
        r32,
        t32,
        s_parts,
        stage,
        ext,
        loc,
        send_x,
        send_y,
        send_c,
        recv_x,
        recv_y,
        recv_c,
        factors,
        message,
        partial,
        slots_narrow,
        slots_wide,
        in_sems,
        out_sems,
        send_sems,
        recv_sems,
        wave_send,
        wave_recv,
    ) = refs[26:]
    order = factor.shape[1]
    row = lax.axis_index("narrow")
    column = lax.axis_index("wide")
    cells = nx * ny
    own_rows = comps * cells

    fetches = [
        pltpu.make_async_copy(source, target, in_sems.at[k])
        for k, (source, target) in enumerate(zip(operands, held))
    ]
    for fetch in fetches:
        fetch.start()

    def turned(here, count):
        places_of = [here + k for k in range(1, count)]
        return [jnp.where(at >= count, at - count, at) for at in places_of]

    along_narrow = [(at, column) for at in turned(row, narrow)]
    along_wide = [(row, at) for at in turned(column, wide)]
    diagonals = [(x, y) for x in (-1, 1) for y in (-1, 1)]

    def inside(shift_x, shift_y):
        along_x = (row + shift_x >= 0) & (row + shift_x < narrow)
        along_y = (column + shift_y >= 0) & (column + shift_y < wide)
        return along_x & along_y

    barrier = pltpu.get_barrier_semaphore()

    def greet(device):
        pl.semaphore_signal(barrier, inc=1, device_id=device, device_id_type=MESH)

    greetings = narrow - 1 + wide - 1
    for device in along_narrow + along_wide:
        greet(device)
    for shift_x, shift_y in diagonals:
        greetings += jnp.where(inside(shift_x, shift_y), 1, 0)

        @pl.when(inside(shift_x, shift_y))
        def _(shift_x=shift_x, shift_y=shift_y):
            greet((row + shift_x, column + shift_y))

    for k, fetch in enumerate(fetches):
        if k != 6:
            fetch.wait()

    rounded = residual[...].astype(BF16).astype(F32).reshape(own_rows, depth)
    store(r32, rounded, pl.ds(0, own_rows))

    def rows_of(a):
        return pl.ds(pl.multiple_of(a * own_rows, own_rows), own_rows)

    def widen(a, carry):
        d = deflation[a].astype(F32).reshape(own_rows, depth)
        store(d32, d, rows_of(a))
        stage[pl.ds(a, 1), :] = jnp.sum(d * rounded, axis=0, keepdims=True)
        return carry

    lax.fori_loop(0, vectors, widen, 0, unroll=2)
    rhs_column = jnp.sum(stage[pl.ds(0, vectors), :], axis=1, keepdims=True)
    own_block = listing[0, 0, 4]
    own_place = iota((vectors, order), 1) == own_block * vectors + iota((vectors, order), 0)

    def placed(values):
        return jnp.sum(jnp.where(own_place, values, 0.0), axis=0, keepdims=True)

    message[0] = placed(rhs_column)

    x_rows = comps * ny
    y_rows = comps * nx
    for side, x in enumerate((0, nx - 1)):
        face = [
            load(d32, pl.ds((a * comps + j) * cells + x * ny, ny))
            for a in range(vectors)
            for j in range(comps)
        ]
        send_x[side, pl.ds(0, vectors * x_rows), :] = jnp.concatenate(face, axis=0).astype(BF16)
        stage[...] = jnp.zeros_like(stage)
        for j in range(comps):
            stage[pl.ds(j * ny, ny), :] = load(r32, pl.ds(j * cells + x * ny, ny))
        send_x[side, pl.ds(vectors * x_rows, 32), :] = stage[...].astype(BF16)
    for side, y in enumerate((0, ny - 1)):
        face = load(d32, pl.ds(y, vectors * y_rows, stride=ny))
        send_y[side, pl.ds(0, vectors * y_rows), :] = face.astype(BF16)
        stage[...] = jnp.zeros_like(stage)
        stage[pl.ds(0, y_rows), :] = load(r32, pl.ds(y, y_rows, stride=ny))
        send_y[side, pl.ds(vectors * y_rows, 16), :] = stage[pl.ds(0, 16), :].astype(BF16)
    for side_x, x in enumerate((0, nx - 1)):
        for side_y, y in enumerate((0, ny - 1)):
            stage[...] = jnp.zeros_like(stage)
            at = x * ny + y
            stage[pl.ds(0, vectors * comps), :] = load(d32, pl.ds(at, vectors * comps, stride=cells))
            stage[pl.ds(vectors * comps, comps), :] = load(r32, pl.ds(at, comps, stride=cells))
            send_c[side_x * 2 + side_y] = stage[...].astype(BF16)

    total_rows = places.shape[0]
    fixed = own_rows + 2 * x_rows
    group = quotient(iota((1, 3 * own_rows), 1), cells, 3 * comps)
    lanes_of = [group == g for g in range(3 * comps)]
    coupling = []
    for j in range(comps):
        for d in range(9):
            line = jnp.zeros((1, 3 * own_rows), F32)
            for oz in range(3):
                for i in range(comps):
                    line = jnp.where(lanes_of[oz * comps + i], stencil[i, j, d * 3 + oz], line)
            coupling.append(line)
    chunks = [(j * cells, cells, j) for j in range(comps)]
    for side in range(2):
        chunks += [(own_rows + side * x_rows + j * ny, ny, j) for j in range(comps)]
    chunks.append((fixed, total_rows - fixed, None))
    for start, size, j in chunks:
        here = places[pl.ds(start, size), :]
        value = jnp.zeros(here.shape, F32)
        for e in range(comps * 9) if j is None else range(j * 9, j * 9 + 9):
            value = jnp.where(here == e, coupling[e], value)
        s_parts[pl.ds(start, size), pl.ds(0, 3 * own_rows)] = value
    high, low = split(s_parts[:, pl.ds(0, 3 * own_rows)])
    s_parts[:, pl.ds(3 * own_rows, 3 * own_rows)] = high.astype(F32)
    s_parts[:, pl.ds(6 * own_rows, 3 * own_rows)] = low.astype(F32)
    s_all = s_parts[...].astype(BF16)

    pl.semaphore_wait(barrier, greetings)

    def spread_out(source, landing, sem, devices):
        for k, device in enumerate(devices):
            pltpu.make_async_remote_copy(
                src_ref=source,
                dst_ref=landing(k),
                send_sem=wave_send.at[sem],
                recv_sem=wave_recv.at[sem],
                device_id=device,
                device_id_type=MESH,
            ).start()

    def await_all(ref, sems, sem):
        pltpu.make_async_copy(ref, ref, sems.at[sem]).wait()

    def summed(ref, number, start):
        for k in range(ref.shape[1]):
            start = start + ref[number, k]
        return start

    def wave_start(number):
        landing = lambda k: slots_narrow.at[number, k]
        spread_out(message.at[number], landing, 2 * number, along_narrow)

    def wave_middle(number):
        await_all(slots_narrow.at[number], wave_recv, 2 * number)
        partial[number] = summed(slots_narrow, number, message[number])
        landing = lambda k: slots_wide.at[number, k]
        spread_out(partial.at[number], landing, 2 * number + 1, along_wide)

    def wave_end(number):
        await_all(slots_wide.at[number], wave_recv, 2 * number + 1)
        return summed(slots_wide, number, partial[number])

    wave_start(0)

    parity = lax.rem(column, 2)
    half_column = column // 2
    factors[parity, half_column, row] = factor[...]
    spread_out(factor, lambda k: factors.at[parity, half_column, row], 4, along_narrow)
    narrow_rows = factors.at[0, 0, pl.ds(0, narrow - 1)]
    wide_rows = factors.at[0, pl.ds(0, wide // 2 - 1)]

    def copies():
        found = []
        for side, shift in enumerate((-1, 1)):
            found.append((send_x.at[side], recv_x.at[1 - side], recv_x.at[side], shift, 0))
        for side, shift in enumerate((-1, 1)):
            found.append((send_y.at[side], recv_y.at[1 - side], recv_y.at[side], 0, shift))
        for side_x, shift_x in enumerate((-1, 1)):
            for side_y, shift_y in enumerate((-1, 1)):
                at = side_x * 2 + side_y
                found.append((send_c.at[at], recv_c.at[3 - at], recv_c.at[at], shift_x, shift_y))
        return found

    opposite = (1, 0, 3, 2, 7, 6, 5, 4)

    def face_copy(k, source, target, shift_x, shift_y):
        return pltpu.make_async_remote_copy(
            src_ref=source,
            dst_ref=target,
            send_sem=send_sems.at[k],
            recv_sem=recv_sems.at[opposite[k]],
            device_id=(row + shift_x, column + shift_y),
            device_id_type=MESH,
        )

    for k, (source, target, _, shift_x, shift_y) in enumerate(copies()):

        @pl.when(inside(shift_x, shift_y))
        def _(k=k, source=source, target=target, shift_x=shift_x, shift_y=shift_y):
            face_copy(k, source, target, shift_x, shift_y).start()

    lane = iota((own_rows, depth), 1)
    scale = jnp.concatenate([stiffness[...].reshape(cells, depth)] * comps, axis=0)
    weight = jnp.concatenate([mass[...].reshape(cells, depth)] * comps, axis=0)

    def adjoint(a, carry):
        d = load(d32, rows_of(a))
        w = d * scale
        before = jnp.where(lane == depth - 1, 0.0, pltpu.roll(w, depth - 1, axis=1))
        after = jnp.where(lane == 0, 0.0, pltpu.roll(w, 1, axis=1))
        parts = [split(shifted) for shifted in (before, w, after)]
        highs, lows = [part[0] for part in parts], [part[1] for part in parts]
        w_all = jnp.concatenate(highs + lows + highs, axis=0)
        image = jnp.dot(s_all, w_all, preferred_element_type=F32)
        t32[a, pl.ds(own_rows, total_rows - own_rows), :] = image[own_rows:]
        t32[a, pl.ds(0, own_rows), :] = image[:own_rows] + weight * d
        return carry

    lax.fori_loop(0, vectors // 2, adjoint, 0, unroll=2)
    wave_middle(0)
    await_all(narrow_rows, wave_recv, 4)
    mine = factors.at[parity, half_column]
    spread_out(mine, lambda k: mine, 5, along_wide[1::2])
    lax.fori_loop(vectors // 2, vectors, adjoint, 0, unroll=2)
    await_all(wide_rows, wave_recv, 5)
    hand_on = pltpu.make_async_remote_copy(
        src_ref=factors.at[parity],
        dst_ref=factors.at[parity],
        send_sem=wave_send.at[6],
        recv_sem=wave_recv.at[6],
        device_id=(row, column + 1 - 2 * parity),
        device_id_type=MESH,
    )
    hand_on.start()

    width = 9 * vectors

    def picked(product, row_of, left_size):
        columns = product.shape[1]
        kept = iota((left_size, columns), 0) == row_of(iota((1, columns), 1))
        parts = product.reshape(vectors, left_size, columns)
        return jnp.sum(jnp.where(kept[None], parts, 0.0), axis=1)

    def folded(values, lane_of):
        rows = values.shape[1]
        chosen = (lane_of(iota((rows, 1), 0)) == iota((rows, width), 1)).astype(F32)
        return exact_dot(values, chosen)

    def within(size):
        return lambda c: c - size * quotient(c, size, vectors)

    def lane_in(block, size):
        return lambda c: block * vectors + quotient(c, size, vectors)

    total = None
    for j in range(comps):
        left = t32[:, pl.ds(j * cells, cells), :].reshape(vectors * cells, depth)
        right = jnp.concatenate(
            [load(d32, pl.ds((b * comps + j) * cells, cells)) for b in range(vectors)], axis=0
        ).astype(BF16)
        part = gram(left, right)
        total = part if total is None else total + part
    blocks = folded(picked(total, within(cells), cells), lane_in(4, cells))

    for k, (source, target, landing, shift_x, shift_y) in enumerate(copies()):

        @pl.when(inside(shift_x, shift_y))
        def _(k=k, source=source, landing=landing, shift_x=shift_x, shift_y=shift_y):
            pltpu.make_async_remote_copy(
                src_ref=source,
                dst_ref=landing,
                send_sem=send_sems.at[k],
                recv_sem=recv_sems.at[k],
                device_id=(row + shift_x, column + shift_y),
                device_id_type=MESH,
            ).wait()

        @pl.when(jnp.logical_not(inside(shift_x, shift_y)))
        def _(landing=landing):
            landing[...] = jnp.zeros(landing.shape, BF16)

    for side in range(2):
        block = 1 if side == 0 else 7
        left = t32[:, pl.ds(own_rows + side * x_rows, x_rows), :].reshape(vectors * x_rows, depth)
        part = gram(left, recv_x[side, pl.ds(0, vectors * x_rows), :])
        blocks += folded(picked(part, within(x_rows), x_rows), lane_in(block, x_rows))
    y_padded = pad_to(y_rows, 8)
    for side in range(2):
        block = 3 if side == 0 else 5
        left = t32[:, pl.ds(fixed + side * y_padded, y_padded), :]
        left = left.reshape(vectors * y_padded, depth)
        part = gram(left, recv_y[side, pl.ds(0, vectors * y_rows), :])
        blocks += folded(picked(part, within(y_rows), y_padded), lane_in(block, y_rows))
    c_padded = pad_to(4 * comps, 8)
    left = t32[:, pl.ds(fixed + 2 * y_padded, c_padded), :].reshape(vectors * c_padded, depth)
    part = gram(left, recv_c[...].reshape(4 * 32, depth))

    def corner_parts(c):
        corner = quotient(c, 32, 4)
        at = c - 32 * corner
        vector = quotient(at, comps, vectors)
        return at < vectors * comps, corner, vector, at - comps * vector

    def corner_row(c):
        real, corner, _, j = corner_parts(c)
        return jnp.where(real, corner * comps + j, -1)

    def corner_lane(c):
        real, corner, vector, _ = corner_parts(c)
        block = corner * 2 + jnp.where(corner >= 2, 2, 0)
        return jnp.where(real, block * vectors + vector, -1)

    blocks += folded(picked(part, corner_row, c_padded), corner_lane)

    out_copies = [
        pltpu.make_async_copy(source, target, out_sems.at[k])
        for k, (source, target) in enumerate(zip(staged, results))
    ]

    pairs = vectors * vectors
    repeated = jnp.broadcast_to(blocks[:, None, :], (vectors, vectors, width))
    right = iota((1, vectors, width), 2)
    right = right - vectors * quotient(right, vectors, 9)
    kept = jnp.where(right == iota((1, vectors, width), 1), repeated, 0.0).reshape(pairs, width)
    neighbour = quotient(iota((width, 1), 0), vectors, 9)
    to_lane = (neighbour == iota((width, 9), 1)).astype(F32)
    turned_blocks = exact_dot(kept, to_lane)
    blocks_out[0, 0] = turned_blocks.reshape(vectors, vectors, 9)
    out_copies[1].start()

    coarse_rhs = wave_end(0)
    hand_on.wait()

    def solve(vector):
        def one(d, total):
            for k in range(2 * narrow):
                f = factors[k // narrow, d, k % narrow]
                total = total + f * jnp.sum(f * vector, axis=1, keepdims=True)
            return total

        zeros = jnp.zeros((factor.shape[0], order), F32)
        total = lax.fori_loop(0, wide // 2, one, zeros, unroll=4)
        return jnp.sum(total, axis=0, keepdims=True)

    first = solve(coarse_rhs)
    near = [
        iota((vectors, order), 1) == listing[0, 0, k] * vectors + iota((vectors, order), 0)
        for k in range(9)
    ]
    spread = jnp.concatenate([m.astype(F32) for m in near], axis=0)
    matrix_rows = exact_dot(blocks, spread)
    message[1] = placed(jnp.sum(matrix_rows * first, axis=1, keepdims=True))
    wave_start(1)

    high_y = ny + 2

    def ext_at(j, f, e):
        return (j * high_y + f) * 8 + e

    for j in range(comps):
        for y in range(ny):
            values = load(r32, pl.ds(j * cells + y, nx, stride=ny))
            store(ext, values, pl.ds(ext_at(j, 1 + y, 1), nx))
    for side in range(2):
        at_x = side * (nx + 1)
        values = recv_x[side, pl.ds(vectors * x_rows, 32), :].astype(F32)
        for j in range(comps):
            for y in range(ny):
                line = values[j * ny + y : j * ny + y + 1]
                store(ext, line, pl.ds(ext_at(j, 1 + y, at_x), 1))
        at_y = side * (ny + 1)
        values = recv_y[side, pl.ds(vectors * y_rows, 16), :].astype(F32)
        for j in range(comps):
            store(ext, values[j * nx : (j + 1) * nx], pl.ds(ext_at(j, at_y, 1), nx))
        for side_y in range(2):
            values = recv_c[side * 2 + side_y].astype(F32)
            for j in range(comps):
                at = vectors * comps + j
                line = values[at : at + 1]
                store(ext, line, pl.ds(ext_at(j, side_y * (ny + 1), at_x), 1))

    half_x = (nx + 2) // 2
    half_y = (ny + 2) // 2
    kept_x = []
    for s in range(2):
        e = 2 * iota((half_x, depth), 0) + s
        kept_x.append((e >= margins[0, 0, 0, 0]) & (e < margins[0, 0, 0, 1]))
    fetches[6].wait()
    wave_middle(1)

    def local_row(v, carry):
        grouped = []
        for j in range(comps):
            for s in range(2):
                for t in range(2):
                    f = 2 * v + t
                    kept = (f >= margins[0, 0, 1, 0]) & (f < margins[0, 0, 1, 1])
                    factor_y = jnp.where(kept, 1.0, 0.0).astype(F32)
                    values = load(ext, pl.ds(ext_at(j, f, s), half_x, stride=2))
                    grouped.append(jnp.where(kept_x[s], values, 0.0) * factor_y)
        for j in range(comps):
            for s in range(2):
                for t in range(2):
                    i = 4 * j + 2 * s + t
                    acc = inverse[i, 0, v].astype(F32) * grouped[0]
                    for m in range(1, 4 * comps):
                        acc += inverse[i, m, v].astype(F32) * grouped[m]
                    store(loc, acc, pl.ds(ext_at(j, 2 * v + t, s), half_x, stride=2))
        return carry

    lax.fori_loop(0, half_y, local_row, 0)

    coarse_image = wave_end(1)
    refined = first + solve(coarse_rhs - coarse_image)
    solution_out[...] = refined
    out_copies[2].start()
    weights = jnp.sum(jnp.where(own_place, refined, 0.0), axis=1, keepdims=True)
    for j in range(comps):
        for x in range(nx):
            value = load(loc, pl.ds(ext_at(j, 1, 1 + x), ny, stride=8))
            for a in range(vectors):
                at = (a * comps + j) * cells + x * ny
                value += weights[a : a + 1, :] * load(d32, pl.ds(at, ny))
            out[j, x] = value

    out_copies[0].start()
    for number in range(2):
        await_all(slots_narrow.at[number], wave_send, 2 * number)
        await_all(slots_wide.at[number], wave_send, 2 * number + 1)
    await_all(narrow_rows, wave_send, 4)
    await_all(wide_rows, wave_send, 5)
    for copy in out_copies:
        copy.wait()


def write_out(*refs):
    sources, targets, sems = refs[:3], refs[3:6], refs[6]
    copies = [
        pltpu.make_async_copy(source, target, sems.at[k])
        for k, (source, target) in enumerate(zip(sources, targets))
    ]
    for copy in copies:
        copy.start()
    for copy in copies:
        copy.wait()


def body(
    narrow,
    wide,
    deflation,
    residual,
    stiffness,
    mass,
    stencil,
    local_inverse,
    inverse_factor,
    margin_range,
    neighbor_blocks,
):
    vectors, comps, nx, ny, depth = deflation.shape
    order = inverse_factor.shape[1]
    cells = nx * ny
    places = stencil_places(comps, nx, ny)
    turned_inverse = local_inverse.transpose(0, 1, 3, 2, 4)
    x_send = vectors * comps * ny + 32
    y_send = vectors * comps * nx + 16
    anywhere = pl.BlockSpec(memory_space=pl.ANY)
    operands = (
        deflation,
        residual,
        stiffness,
        mass,
        jnp.asarray(places),
        stencil.transpose(1, 2, 0),
        turned_inverse,
        inverse_factor,
        margin_range,
        neighbor_blocks,
    )
    spaces = [pltpu.VMEM] * 5 + [pltpu.SMEM] + [pltpu.VMEM] * 2 + [pltpu.SMEM] * 2
    shapes = (
        jax.ShapeDtypeStruct(residual.shape, F32),
        jax.ShapeDtypeStruct((1, 1, vectors, vectors, 9), F32),
        jax.ShapeDtypeStruct((1, order), F32),
    )
    results = pl.pallas_call(
        functools.partial(kernel, narrow, wide, vectors, comps, nx, ny, depth),
        out_shape=shapes,
        in_specs=[anywhere] * len(operands),
        out_specs=(anywhere,) * len(shapes),
        scratch_shapes=[space(o.shape, o.dtype) for space, o in zip(spaces, operands)]
        + [pltpu.VMEM(shape.shape, shape.dtype) for shape in shapes]
        + [
            pltpu.VMEM((depth // 128, vectors * comps * cells, 128), F32),
            pltpu.VMEM((depth // 128, comps * cells, 128), F32),
            pltpu.VMEM((vectors, places.shape[0], depth), F32),
            pltpu.VMEM((places.shape[0], 9 * comps * cells), F32),
            pltpu.VMEM((32, depth), F32),
            pltpu.VMEM((depth // 128, comps * (ny + 2) * 8, 128), F32),
            pltpu.VMEM((depth // 128, comps * (ny + 2) * 8, 128), F32),
            pltpu.VMEM((2, x_send, depth), BF16),
            pltpu.VMEM((2, y_send, depth), BF16),
            pltpu.VMEM((4, 32, depth), BF16),
            pltpu.VMEM((2, x_send, depth), BF16),
            pltpu.VMEM((2, y_send, depth), BF16),
            pltpu.VMEM((4, 32, depth), BF16),
            pltpu.VMEM((2, wide // 2, narrow) + inverse_factor.shape, F32),
            pltpu.VMEM((2, 1, order), F32),
            pltpu.VMEM((2, 1, order), F32),
            pltpu.VMEM((2, narrow - 1, 1, order), F32),
            pltpu.VMEM((2, wide - 1, 1, order), F32),
            pltpu.SemaphoreType.DMA((len(operands),)),
            pltpu.SemaphoreType.DMA((len(shapes),)),
            pltpu.SemaphoreType.DMA((8,)),
            pltpu.SemaphoreType.DMA((8,)),
            pltpu.SemaphoreType.DMA((7,)),
            pltpu.SemaphoreType.DMA((7,)),
        ],
        compiler_params=pltpu.CompilerParams(
            collective_id=0, has_side_effects=True, vmem_limit_bytes=60 * 1024 * 1024
        ),
    )(*operands)
    result, blocks, refined = pl.pallas_call(
        write_out,
        out_shape=tuple(jax.ShapeDtypeStruct(r.shape, r.dtype) for r in results),
        in_specs=[anywhere] * 3,
        out_specs=(anywhere,) * 3,
        scratch_shapes=[pltpu.SemaphoreType.DMA((3,))],
        compiler_params=pltpu.CompilerParams(vmem_limit_bytes=60 * 1024 * 1024),
    )(*results)
    return result, blocks.transpose(0, 1, 4, 2, 3), refined.reshape(order)


def solution(mesh):
    placed = (
        P(None, None, "narrow", "wide", None),
        P(None, "narrow", "wide", None),
        P("narrow", "wide", None),
        P("narrow", "wide", None),
        P(),
        P(None, None, "narrow", "wide", None),
        P(("narrow", "wide"), None),
        P("narrow", "wide", None, None),
        P("narrow", "wide", None),
    )
    return jax.shard_map(
        functools.partial(body, mesh.shape["narrow"], mesh.shape["wide"]),
        mesh=mesh,
        in_specs=placed,
        out_specs=(P(None, "narrow", "wide", None), P("narrow", "wide", None, None, None), P()),
        check_vma=False,
    )
```

```python
import functools

import jax
import jax.numpy as jnp
import numpy as np
from jax import lax
from jax.experimental import pallas as pl
from jax.experimental.pallas import tpu as pltpu
from jax.sharding import PartitionSpec as P

F32 = jnp.float32
BF16 = jnp.bfloat16
MESH = pl.DeviceIdType.MESH


def pad_to(count, unit):
    return -(-count // unit) * unit


def stencil_places(comps, nx, ny):
    rows = []
    for j in range(comps):
        rows += [(j, x, y) for x in range(nx) for y in range(ny)]
    for x in (-1, nx):
        rows += [(j, x, y) for j in range(comps) for y in range(ny)]
    for y in (-1, ny):
        face = [(j, x, y) for j in range(comps) for x in range(nx)]
        rows += face + [None] * (pad_to(len(face), 8) - len(face))
    corners = [(j, x, y) for x in (-1, nx) for y in (-1, ny) for j in range(comps)]
    rows += corners + [None] * (pad_to(len(corners), 8) - len(corners))
    cells = comps * nx * ny
    table = np.full((len(rows), 3 * cells), -1, np.int32)
    for r, row in enumerate(rows):
        if row is None:
            continue
        j, x, y = row
        for oz in range(3):
            for i in range(comps):
                for px in range(nx):
                    for py in range(ny):
                        dx, dy = x - px, y - py
                        if abs(dx) <= 1 and abs(dy) <= 1:
                            column = oz * cells + i * nx * ny + px * ny + py
                            table[r, column] = j * 9 + (dx + 1) * 3 + dy + 1
    return table


def split(values):
    high = values.astype(BF16)
    return high, (values - high.astype(F32)).astype(BF16)


def iota(shape, axis):
    return lax.broadcasted_iota(jnp.int32, shape, axis)


def load(ref, *at):
    return jnp.concatenate([ref[(h,) + at] for h in range(ref.shape[0])], axis=-1)


def store(ref, values, *at):
    for h in range(ref.shape[0]):
        ref[(h,) + at] = values[:, h * 128 : (h + 1) * 128]


def quotient(values, size, count):
    return sum((values >= k * size).astype(jnp.int32) for k in range(1, count))


def exact_dot(values, chosen):
    rows = values.shape[0]
    high = values.astype(BF16).astype(F32)
    middle = (values - high).astype(BF16).astype(F32)
    low = values - high - middle
    parts = jnp.concatenate([high, middle, low], axis=0).astype(BF16)
    product = jnp.dot(parts, chosen.astype(BF16), preferred_element_type=F32)
    return product[:rows] + product[rows : 2 * rows] + product[2 * rows :]


def gram(left, right):
    dims = (((1,), (1,)), ((), ()))
    high, low = split(left)
    return lax.dot_general(high, right, dims, preferred_element_type=F32) + lax.dot_general(
        low, right, dims, preferred_element_type=F32
    )


def kernel(
    narrow,
    wide,
    vectors,
    comps,
    nx,
    ny,
    depth,
    *refs,
):
    operands, results = refs[:10], refs[10:13]
    held, staged = refs[13:23], refs[23:26]
    deflation, residual, stiffness, mass, places, stencil = held[:6]
    inverse, factor, margins, listing = held[6:]
    out, blocks_out, solution_out = staged
    (
        d32,
        r32,
        t32,
        s_parts,
        stage,
        ext,
        loc,
        send_x,
        send_y,
        send_c,
        recv_x,
        recv_y,
        recv_c,
        factors,
        message,
        partial,
        slots_narrow,
        slots_wide,
        in_sems,
        out_sems,
        send_sems,
        recv_sems,
        wave_send,
        wave_recv,
    ) = refs[26:]
    order = factor.shape[1]
    row = lax.axis_index("narrow")
    column = lax.axis_index("wide")
    cells = nx * ny
    own_rows = comps * cells

    fetches = [
        pltpu.make_async_copy(source, target, in_sems.at[k])
        for k, (source, target) in enumerate(zip(operands, held))
    ]
    for fetch in fetches:
        fetch.start()

    def turned(here, count):
        places_of = [here + k for k in range(1, count)]
        return [jnp.where(at >= count, at - count, at) for at in places_of]

    along_narrow = [(at, column) for at in turned(row, narrow)]
    along_wide = [(row, at) for at in turned(column, wide)]
    diagonals = [(x, y) for x in (-1, 1) for y in (-1, 1)]

    def inside(shift_x, shift_y):
        along_x = (row + shift_x >= 0) & (row + shift_x < narrow)
        along_y = (column + shift_y >= 0) & (column + shift_y < wide)
        return along_x & along_y

    barrier = pltpu.get_barrier_semaphore()

    def greet(device):
        pl.semaphore_signal(barrier, inc=1, device_id=device, device_id_type=MESH)

    greetings = narrow - 1 + wide - 1
    for device in along_narrow + along_wide:
        greet(device)
    for shift_x, shift_y in diagonals:
        greetings += jnp.where(inside(shift_x, shift_y), 1, 0)

        @pl.when(inside(shift_x, shift_y))
        def _(shift_x=shift_x, shift_y=shift_y):
            greet((row + shift_x, column + shift_y))

    for k, fetch in enumerate(fetches):
        if k != 6:
            fetch.wait()

    rounded = residual[...].astype(BF16).astype(F32).reshape(own_rows, depth)
    store(r32, rounded, pl.ds(0, own_rows))

    def rows_of(a):
        return pl.ds(pl.multiple_of(a * own_rows, own_rows), own_rows)

    def widen(a, carry):
        d = deflation[a].astype(F32).reshape(own_rows, depth)
        store(d32, d, rows_of(a))
        stage[pl.ds(a, 1), :] = jnp.sum(d * rounded, axis=0, keepdims=True)
        return carry

    lax.fori_loop(0, vectors, widen, 0, unroll=2)
    rhs_column = jnp.sum(stage[pl.ds(0, vectors), :], axis=1, keepdims=True)
    own_block = listing[0, 0, 4]
    own_place = iota((vectors, order), 1) == own_block * vectors + iota((vectors, order), 0)

    def placed(values):
        return jnp.sum(jnp.where(own_place, values, 0.0), axis=0, keepdims=True)

    message[0] = placed(rhs_column)

    x_rows = comps * ny
    y_rows = comps * nx
    for side, x in enumerate((0, nx - 1)):
        face = [
            load(d32, pl.ds((a * comps + j) * cells + x * ny, ny))
            for a in range(vectors)
            for j in range(comps)
        ]
        send_x[side, pl.ds(0, vectors * x_rows), :] = jnp.concatenate(face, axis=0).astype(BF16)
        stage[...] = jnp.zeros_like(stage)
        for j in range(comps):
            stage[pl.ds(j * ny, ny), :] = load(r32, pl.ds(j * cells + x * ny, ny))
        send_x[side, pl.ds(vectors * x_rows, 32), :] = stage[...].astype(BF16)
    for side, y in enumerate((0, ny - 1)):
        face = load(d32, pl.ds(y, vectors * y_rows, stride=ny))
        send_y[side, pl.ds(0, vectors * y_rows), :] = face.astype(BF16)
        stage[...] = jnp.zeros_like(stage)
        stage[pl.ds(0, y_rows), :] = load(r32, pl.ds(y, y_rows, stride=ny))
        send_y[side, pl.ds(vectors * y_rows, 16), :] = stage[pl.ds(0, 16), :].astype(BF16)
    for side_x, x in enumerate((0, nx - 1)):
        for side_y, y in enumerate((0, ny - 1)):
            stage[...] = jnp.zeros_like(stage)
            at = x * ny + y
            stage[pl.ds(0, vectors * comps), :] = load(d32, pl.ds(at, vectors * comps, stride=cells))
            stage[pl.ds(vectors * comps, comps), :] = load(r32, pl.ds(at, comps, stride=cells))
            send_c[side_x * 2 + side_y] = stage[...].astype(BF16)

    pl.semaphore_wait(barrier, greetings)

    def spread_out(source, landing, sem, devices):
        for k, device in enumerate(devices):
            pltpu.make_async_remote_copy(
                src_ref=source,
                dst_ref=landing(k),
                send_sem=wave_send.at[sem],
                recv_sem=wave_recv.at[sem],
                device_id=device,
                device_id_type=MESH,
            ).start()

    def await_all(ref, sems, sem):
        pltpu.make_async_copy(ref, ref, sems.at[sem]).wait()

    def summed(ref, number, start):
        for k in range(ref.shape[1]):
            start = start + ref[number, k]
        return start

    def wave_start(number):
        landing = lambda k: slots_narrow.at[number, k]
        spread_out(message.at[number], landing, 2 * number, along_narrow)

    def wave_middle(number):
        await_all(slots_narrow.at[number], wave_recv, 2 * number)
        partial[number] = summed(slots_narrow, number, message[number])
        landing = lambda k: slots_wide.at[number, k]
        spread_out(partial.at[number], landing, 2 * number + 1, along_wide)

    def wave_end(number):
        await_all(slots_wide.at[number], wave_recv, 2 * number + 1)
        return summed(slots_wide, number, partial[number])

    wave_start(0)

    parity = lax.rem(column, 2)
    half_column = column // 2
    factors[parity, half_column, row] = factor[...]
    spread_out(factor, lambda k: factors.at[parity, half_column, row], 4, along_narrow)
    narrow_rows = factors.at[0, 0, pl.ds(0, narrow - 1)]
    wide_rows = factors.at[0, pl.ds(0, wide // 2 - 1)]

    def copies():
        found = []
        for side, shift in enumerate((-1, 1)):
            found.append((send_x.at[side], recv_x.at[1 - side], recv_x.at[side], shift, 0))
        for side, shift in enumerate((-1, 1)):
            found.append((send_y.at[side], recv_y.at[1 - side], recv_y.at[side], 0, shift))
        for side_x, shift_x in enumerate((-1, 1)):
            for side_y, shift_y in enumerate((-1, 1)):
                at = side_x * 2 + side_y
                found.append((send_c.at[at], recv_c.at[3 - at], recv_c.at[at], shift_x, shift_y))
        return found

    opposite = (1, 0, 3, 2, 7, 6, 5, 4)

    def face_copy(k, source, target, shift_x, shift_y):
        return pltpu.make_async_remote_copy(
            src_ref=source,
            dst_ref=target,
            send_sem=send_sems.at[k],
            recv_sem=recv_sems.at[opposite[k]],
            device_id=(row + shift_x, column + shift_y),
            device_id_type=MESH,
        )

    for k, (source, target, _, shift_x, shift_y) in enumerate(copies()):

        @pl.when(inside(shift_x, shift_y))
        def _(k=k, source=source, target=target, shift_x=shift_x, shift_y=shift_y):
            face_copy(k, source, target, shift_x, shift_y).start()

    total_rows = places.shape[0]
    fixed = own_rows + 2 * x_rows
    group = quotient(iota((1, 3 * own_rows), 1), cells, 3 * comps)
    lanes_of = [group == g for g in range(3 * comps)]
    coupling = []
    for j in range(comps):
        for d in range(9):
            line = jnp.zeros((1, 3 * own_rows), F32)
            for oz in range(3):
                for i in range(comps):
                    line = jnp.where(lanes_of[oz * comps + i], stencil[i, j, d * 3 + oz], line)
            coupling.append(line)
    chunks = [(j * cells, cells, j) for j in range(comps)]
    for side in range(2):
        chunks += [(own_rows + side * x_rows + j * ny, ny, j) for j in range(comps)]
    chunks.append((fixed, total_rows - fixed, None))
    for start, size, j in chunks:
        here = places[pl.ds(start, size), :]
        value = jnp.zeros(here.shape, F32)
        for e in range(comps * 9) if j is None else range(j * 9, j * 9 + 9):
            value = jnp.where(here == e, coupling[e], value)
        s_parts[pl.ds(start, size), pl.ds(0, 3 * own_rows)] = value
    high, low = split(s_parts[:, pl.ds(0, 3 * own_rows)])
    s_parts[:, pl.ds(3 * own_rows, 3 * own_rows)] = high.astype(F32)
    s_parts[:, pl.ds(6 * own_rows, 3 * own_rows)] = low.astype(F32)
    s_all = s_parts[...].astype(BF16)

    lane = iota((own_rows, depth), 1)
    scale = jnp.concatenate([stiffness[...].reshape(cells, depth)] * comps, axis=0)
    weight = jnp.concatenate([mass[...].reshape(cells, depth)] * comps, axis=0)

    def adjoint(a, carry):
        d = load(d32, rows_of(a))
        w = d * scale
        before = jnp.where(lane == depth - 1, 0.0, pltpu.roll(w, depth - 1, axis=1))
        after = jnp.where(lane == 0, 0.0, pltpu.roll(w, 1, axis=1))
        parts = [split(shifted) for shifted in (before, w, after)]
        highs, lows = [part[0] for part in parts], [part[1] for part in parts]
        w_all = jnp.concatenate(highs + lows + highs, axis=0)
        image = jnp.dot(s_all, w_all, preferred_element_type=F32)
        t32[a, pl.ds(own_rows, total_rows - own_rows), :] = image[own_rows:]
        t32[a, pl.ds(0, own_rows), :] = image[:own_rows] + weight * d
        return carry

    lax.fori_loop(0, vectors // 2, adjoint, 0, unroll=2)
    wave_middle(0)
    await_all(narrow_rows, wave_recv, 4)
    mine = factors.at[parity, half_column]
    spread_out(mine, lambda k: mine, 5, along_wide[1::2])
    lax.fori_loop(vectors // 2, vectors, adjoint, 0, unroll=2)
    await_all(wide_rows, wave_recv, 5)
    hand_on = pltpu.make_async_remote_copy(
        src_ref=factors.at[parity],
        dst_ref=factors.at[parity],
        send_sem=wave_send.at[6],
        recv_sem=wave_recv.at[6],
        device_id=(row, column + 1 - 2 * parity),
        device_id_type=MESH,
    )
    hand_on.start()

    width = 9 * vectors

    def picked(product, row_of, left_size):
        columns = product.shape[1]
        kept = iota((left_size, columns), 0) == row_of(iota((1, columns), 1))
        parts = product.reshape(vectors, left_size, columns)
        return jnp.sum(jnp.where(kept[None], parts, 0.0), axis=1)

    def folded(values, lane_of):
        rows = values.shape[1]
        chosen = (lane_of(iota((rows, 1), 0)) == iota((rows, width), 1)).astype(F32)
        return exact_dot(values, chosen)

    def within(size):
        return lambda c: c - size * quotient(c, size, vectors)

    def lane_in(block, size):
        return lambda c: block * vectors + quotient(c, size, vectors)

    total = None
    for j in range(comps):
        left = t32[:, pl.ds(j * cells, cells), :].reshape(vectors * cells, depth)
        right = jnp.concatenate(
            [load(d32, pl.ds((b * comps + j) * cells, cells)) for b in range(vectors)], axis=0
        ).astype(BF16)
        part = gram(left, right)
        total = part if total is None else total + part

    for k, (source, target, landing, shift_x, shift_y) in enumerate(copies()):

        @pl.when(inside(shift_x, shift_y))
        def _(k=k, source=source, landing=landing, shift_x=shift_x, shift_y=shift_y):
            pltpu.make_async_remote_copy(
                src_ref=source,
                dst_ref=landing,
                send_sem=send_sems.at[k],
                recv_sem=recv_sems.at[k],
                device_id=(row + shift_x, column + shift_y),
                device_id_type=MESH,
            ).wait()

        @pl.when(jnp.logical_not(inside(shift_x, shift_y)))
        def _(landing=landing):
            landing[...] = jnp.zeros(landing.shape, BF16)

    y_padded = pad_to(y_rows, 8)
    c_padded = pad_to(4 * comps, 8)

    def corner_parts(c):
        corner = quotient(c, 32, 4)
        at = c - 32 * corner
        vector = quotient(at, comps, vectors)
        return at < vectors * comps, corner, vector, at - comps * vector

    def corner_row(c):
        real, corner, _, j = corner_parts(c)
        return jnp.where(real, corner * comps + j, -1)

    def corner_lane(c):
        real, corner, vector, _ = corner_parts(c)
        block = corner * 2 + jnp.where(corner >= 2, 2, 0)
        return jnp.where(real, block * vectors + vector, -1)

    coarse_rhs = wave_end(0)
    hand_on.wait()

    def solve(vector):
        def one(d, total):
            for k in range(2 * narrow):
                f = factors[k // narrow, d, k % narrow]
                total = total + f * jnp.sum(f * vector, axis=1, keepdims=True)
            return total

        zeros = jnp.zeros((factor.shape[0], order), F32)
        total = lax.fori_loop(0, wide // 2, one, zeros, unroll=4)
        return jnp.sum(total, axis=0, keepdims=True)

    first = solve(coarse_rhs)
    near = [
        iota((vectors, order), 1) == listing[0, 0, k] * vectors + iota((vectors, order), 0)
        for k in range(9)
    ]
    parts_of = [jnp.sum(jnp.where(m, first, 0.0), axis=1, keepdims=True) for m in near]

    def weights_on(lanes, block):
        chosen = iota((vectors, lanes.shape[1]), 0) == lanes
        return jnp.sum(jnp.where(chosen, parts_of[block], 0.0), axis=0, keepdims=True)

    def mixed(values, weights, row_of, count):
        lanes = iota((1, values.shape[0]), 1)
        matrix = jnp.where(iota((count, values.shape[0]), 0) == row_of(lanes), weights, 0.0)
        high = matrix.astype(BF16).astype(F32)
        both = jnp.concatenate([high, matrix - high], axis=0).astype(BF16)
        product = jnp.dot(both, values, preferred_element_type=F32)
        return product[:count] + product[count:]

    field = parts_of[4][0:1, :] * load(d32, rows_of(0))
    for b in range(1, vectors):
        field += parts_of[4][b : b + 1, :] * load(d32, rows_of(b))
    fields = [field]
    for side, block in enumerate((1, 7)):
        lanes = quotient(iota((1, vectors * x_rows), 1), x_rows, vectors)
        values = recv_x[side, pl.ds(0, vectors * x_rows), :]
        fields.append(mixed(values, weights_on(lanes, block), within(x_rows), x_rows))
    for side, block in enumerate((3, 5)):
        lanes = quotient(iota((1, vectors * y_rows), 1), y_rows, vectors)
        values = recv_y[side, pl.ds(0, vectors * y_rows), :]
        fields.append(mixed(values, weights_on(lanes, block), within(y_rows), y_padded))
    real, corner, vector, _ = corner_parts(iota((1, 4 * 32), 1))
    weights = jnp.zeros((1, 4 * 32), F32)
    for k, block in enumerate((0, 2, 6, 8)):
        weights += weights_on(jnp.where(real & (corner == k), vector, -1), block)
    fields.append(mixed(recv_c[...].reshape(4 * 32, depth), weights, corner_row, c_padded))
    field = jnp.concatenate(fields, axis=0)

    def imaged(a, carry):
        stage[pl.ds(a, 1), :] = jnp.sum(t32[a] * field, axis=0, keepdims=True)
        return carry

    lax.fori_loop(0, vectors, imaged, 0, unroll=2)
    message[1] = placed(jnp.sum(stage[pl.ds(0, vectors), :], axis=1, keepdims=True))
    wave_start(1)

    blocks = folded(picked(total, within(cells), cells), lane_in(4, cells))
    for side in range(2):
        block = 1 if side == 0 else 7
        left = t32[:, pl.ds(own_rows + side * x_rows, x_rows), :].reshape(vectors * x_rows, depth)
        part = gram(left, recv_x[side, pl.ds(0, vectors * x_rows), :])
        blocks += folded(picked(part, within(x_rows), x_rows), lane_in(block, x_rows))
    wave_middle(1)
    for side in range(2):
        block = 3 if side == 0 else 5
        left = t32[:, pl.ds(fixed + side * y_padded, y_padded), :]
        left = left.reshape(vectors * y_padded, depth)
        part = gram(left, recv_y[side, pl.ds(0, vectors * y_rows), :])
        blocks += folded(picked(part, within(y_rows), y_padded), lane_in(block, y_rows))
    left = t32[:, pl.ds(fixed + 2 * y_padded, c_padded), :].reshape(vectors * c_padded, depth)
    part = gram(left, recv_c[...].reshape(4 * 32, depth))

    blocks += folded(picked(part, corner_row, c_padded), corner_lane)

    out_copies = [
        pltpu.make_async_copy(source, target, out_sems.at[k])
        for k, (source, target) in enumerate(zip(staged, results))
    ]

    pairs = vectors * vectors
    repeated = jnp.broadcast_to(blocks[:, None, :], (vectors, vectors, width))
    right = iota((1, vectors, width), 2)
    right = right - vectors * quotient(right, vectors, 9)
    kept = jnp.where(right == iota((1, vectors, width), 1), repeated, 0.0).reshape(pairs, width)
    neighbour = quotient(iota((width, 1), 0), vectors, 9)
    to_lane = (neighbour == iota((width, 9), 1)).astype(F32)
    turned_blocks = exact_dot(kept, to_lane)
    blocks_out[0, 0] = turned_blocks.reshape(vectors, vectors, 9)
    out_copies[1].start()

    high_y = ny + 2

    def ext_at(j, f, e):
        return (j * high_y + f) * 8 + e

    for j in range(comps):
        for y in range(ny):
            values = load(r32, pl.ds(j * cells + y, nx, stride=ny))
            store(ext, values, pl.ds(ext_at(j, 1 + y, 1), nx))
    for side in range(2):
        at_x = side * (nx + 1)
        values = recv_x[side, pl.ds(vectors * x_rows, 32), :].astype(F32)
        for j in range(comps):
            for y in range(ny):
                line = values[j * ny + y : j * ny + y + 1]
                store(ext, line, pl.ds(ext_at(j, 1 + y, at_x), 1))
        at_y = side * (ny + 1)
        values = recv_y[side, pl.ds(vectors * y_rows, 16), :].astype(F32)
        for j in range(comps):
            store(ext, values[j * nx : (j + 1) * nx], pl.ds(ext_at(j, at_y, 1), nx))
        for side_y in range(2):
            values = recv_c[side * 2 + side_y].astype(F32)
            for j in range(comps):
                at = vectors * comps + j
                line = values[at : at + 1]
                store(ext, line, pl.ds(ext_at(j, side_y * (ny + 1), at_x), 1))

    half_x = (nx + 2) // 2
    half_y = (ny + 2) // 2
    kept_x = []
    for s in range(2):
        e = 2 * iota((half_x, depth), 0) + s
        kept_x.append((e >= margins[0, 0, 0, 0]) & (e < margins[0, 0, 0, 1]))
    fetches[6].wait()

    def local_row(v, carry):
        grouped = []
        for j in range(comps):
            for s in range(2):
                for t in range(2):
                    f = 2 * v + t
                    kept = (f >= margins[0, 0, 1, 0]) & (f < margins[0, 0, 1, 1])
                    factor_y = jnp.where(kept, 1.0, 0.0).astype(F32)
                    values = load(ext, pl.ds(ext_at(j, f, s), half_x, stride=2))
                    grouped.append(jnp.where(kept_x[s], values, 0.0) * factor_y)
        for j in range(comps):
            for s in range(2):
                for t in range(2):
                    i = 4 * j + 2 * s + t
                    acc = inverse[i, 0, v].astype(F32) * grouped[0]
                    for m in range(1, 4 * comps):
                        acc += inverse[i, m, v].astype(F32) * grouped[m]
                    store(loc, acc, pl.ds(ext_at(j, 2 * v + t, s), half_x, stride=2))
        return carry

    lax.fori_loop(0, half_y, local_row, 0)

    coarse_image = wave_end(1)
    refined = first + solve(coarse_rhs - coarse_image)
    solution_out[...] = refined
    out_copies[2].start()
    weights = jnp.sum(jnp.where(own_place, refined, 0.0), axis=1, keepdims=True)
    for j in range(comps):
        for x in range(nx):
            value = load(loc, pl.ds(ext_at(j, 1, 1 + x), ny, stride=8))
            for a in range(vectors):
                at = (a * comps + j) * cells + x * ny
                value += weights[a : a + 1, :] * load(d32, pl.ds(at, ny))
            out[j, x] = value

    out_copies[0].start()
    for number in range(2):
        await_all(slots_narrow.at[number], wave_send, 2 * number)
        await_all(slots_wide.at[number], wave_send, 2 * number + 1)
    await_all(narrow_rows, wave_send, 4)
    await_all(wide_rows, wave_send, 5)
    for copy in out_copies:
        copy.wait()


def write_out(*refs):
    sources, targets, sems = refs[:3], refs[3:6], refs[6]
    copies = [
        pltpu.make_async_copy(source, target, sems.at[k])
        for k, (source, target) in enumerate(zip(sources, targets))
    ]
    for copy in copies:
        copy.start()
    for copy in copies:
        copy.wait()


def body(
    narrow,
    wide,
    deflation,
    residual,
    stiffness,
    mass,
    stencil,
    local_inverse,
    inverse_factor,
    margin_range,
    neighbor_blocks,
):
    vectors, comps, nx, ny, depth = deflation.shape
    order = inverse_factor.shape[1]
    cells = nx * ny
    places = stencil_places(comps, nx, ny)
    turned_inverse = local_inverse.transpose(0, 1, 3, 2, 4)
    x_send = vectors * comps * ny + 32
    y_send = vectors * comps * nx + 16
    anywhere = pl.BlockSpec(memory_space=pl.ANY)
    operands = (
        deflation,
        residual,
        stiffness,
        mass,
        jnp.asarray(places),
        stencil.transpose(1, 2, 0),
        turned_inverse,
        inverse_factor,
        margin_range,
        neighbor_blocks,
    )
    spaces = [pltpu.VMEM] * 5 + [pltpu.SMEM] + [pltpu.VMEM] * 2 + [pltpu.SMEM] * 2
    shapes = (
        jax.ShapeDtypeStruct(residual.shape, F32),
        jax.ShapeDtypeStruct((1, 1, vectors, vectors, 9), F32),
        jax.ShapeDtypeStruct((1, order), F32),
    )
    results = pl.pallas_call(
        functools.partial(kernel, narrow, wide, vectors, comps, nx, ny, depth),
        out_shape=shapes,
        in_specs=[anywhere] * len(operands),
        out_specs=(anywhere,) * len(shapes),
        scratch_shapes=[space(o.shape, o.dtype) for space, o in zip(spaces, operands)]
        + [pltpu.VMEM(shape.shape, shape.dtype) for shape in shapes]
        + [
            pltpu.VMEM((depth // 128, vectors * comps * cells, 128), F32),
            pltpu.VMEM((depth // 128, comps * cells, 128), F32),
            pltpu.VMEM((vectors, places.shape[0], depth), F32),
            pltpu.VMEM((places.shape[0], 9 * comps * cells), F32),
            pltpu.VMEM((32, depth), F32),
            pltpu.VMEM((depth // 128, comps * (ny + 2) * 8, 128), F32),
            pltpu.VMEM((depth // 128, comps * (ny + 2) * 8, 128), F32),
            pltpu.VMEM((2, x_send, depth), BF16),
            pltpu.VMEM((2, y_send, depth), BF16),
            pltpu.VMEM((4, 32, depth), BF16),
            pltpu.VMEM((2, x_send, depth), BF16),
            pltpu.VMEM((2, y_send, depth), BF16),
            pltpu.VMEM((4, 32, depth), BF16),
            pltpu.VMEM((2, wide // 2, narrow) + inverse_factor.shape, F32),
            pltpu.VMEM((2, 1, order), F32),
            pltpu.VMEM((2, 1, order), F32),
            pltpu.VMEM((2, narrow - 1, 1, order), F32),
            pltpu.VMEM((2, wide - 1, 1, order), F32),
            pltpu.SemaphoreType.DMA((len(operands),)),
            pltpu.SemaphoreType.DMA((len(shapes),)),
            pltpu.SemaphoreType.DMA((8,)),
            pltpu.SemaphoreType.DMA((8,)),
            pltpu.SemaphoreType.DMA((7,)),
            pltpu.SemaphoreType.DMA((7,)),
        ],
        compiler_params=pltpu.CompilerParams(
            collective_id=0, has_side_effects=True, vmem_limit_bytes=60 * 1024 * 1024
        ),
    )(*operands)
    result, blocks, refined = pl.pallas_call(
        write_out,
        out_shape=tuple(jax.ShapeDtypeStruct(r.shape, r.dtype) for r in results),
        in_specs=[pl.BlockSpec(memory_space=pltpu.VMEM)] * 3,
        out_specs=(anywhere,) * 3,
        scratch_shapes=[pltpu.SemaphoreType.DMA((3,))],
        compiler_params=pltpu.CompilerParams(vmem_limit_bytes=60 * 1024 * 1024),
    )(*results)
    return result, blocks.transpose(0, 1, 4, 2, 3), refined.reshape(order)


def solution(mesh):
    placed = (
        P(None, None, "narrow", "wide", None),
        P(None, "narrow", "wide", None),
        P("narrow", "wide", None),
        P("narrow", "wide", None),
        P(),
        P(None, None, "narrow", "wide", None),
        P(("narrow", "wide"), None),
        P("narrow", "wide", None, None),
        P("narrow", "wide", None),
    )
    return jax.shard_map(
        functools.partial(body, mesh.shape["narrow"], mesh.shape["wide"]),
        mesh=mesh,
        in_specs=placed,
        out_specs=(P(None, "narrow", "wide", None), P("narrow", "wide", None, None, None), P()),
        check_vma=False,
    )
```

```python
import functools

import jax
import jax.numpy as jnp
import numpy as np
from jax import lax
from jax.experimental import pallas as pl
from jax.experimental.pallas import tpu as pltpu
from jax.sharding import PartitionSpec as P

F32 = jnp.float32
BF16 = jnp.bfloat16
MESH = pl.DeviceIdType.MESH


def pad_to(count, unit):
    return -(-count // unit) * unit


def stencil_places(comps, nx, ny):
    rows = []
    for j in range(comps):
        rows += [(j, x, y) for x in range(nx) for y in range(ny)]
    for x in (-1, nx):
        rows += [(j, x, y) for j in range(comps) for y in range(ny)]
    for y in (-1, ny):
        face = [(j, x, y) for j in range(comps) for x in range(nx)]
        rows += face + [None] * (pad_to(len(face), 8) - len(face))
    corners = [(j, x, y) for x in (-1, nx) for y in (-1, ny) for j in range(comps)]
    rows += corners + [None] * (pad_to(len(corners), 8) - len(corners))
    cells = comps * nx * ny
    table = np.full((len(rows), 3 * cells), -1, np.int32)
    for r, row in enumerate(rows):
        if row is None:
            continue
        j, x, y = row
        for oz in range(3):
            for i in range(comps):
                for px in range(nx):
                    for py in range(ny):
                        dx, dy = x - px, y - py
                        if abs(dx) <= 1 and abs(dy) <= 1:
                            column = oz * cells + i * nx * ny + px * ny + py
                            table[r, column] = j * 9 + (dx + 1) * 3 + dy + 1
    return table


def split(values):
    high = values.astype(BF16)
    return high, (values - high.astype(F32)).astype(BF16)


def iota(shape, axis):
    return lax.broadcasted_iota(jnp.int32, shape, axis)


def load(ref, *at):
    return jnp.concatenate([ref[(h,) + at] for h in range(ref.shape[0])], axis=-1)


def store(ref, values, *at):
    for h in range(ref.shape[0]):
        ref[(h,) + at] = values[:, h * 128 : (h + 1) * 128]


def quotient(values, size, count):
    return sum((values >= k * size).astype(jnp.int32) for k in range(1, count))


def exact_dot(values, chosen):
    rows = values.shape[0]
    high = values.astype(BF16).astype(F32)
    middle = (values - high).astype(BF16).astype(F32)
    low = values - high - middle
    parts = jnp.concatenate([high, middle, low], axis=0).astype(BF16)
    product = jnp.dot(parts, chosen.astype(BF16), preferred_element_type=F32)
    return product[:rows] + product[rows : 2 * rows] + product[2 * rows :]


def gram(left, right):
    dims = (((1,), (1,)), ((), ()))
    high, low = split(left)
    return lax.dot_general(high, right, dims, preferred_element_type=F32) + lax.dot_general(
        low, right, dims, preferred_element_type=F32
    )


def kernel(
    narrow,
    wide,
    vectors,
    comps,
    nx,
    ny,
    depth,
    *refs,
):
    operands, held = refs[:10], refs[13:23]
    deflation, residual, stiffness, mass, places, stencil = held[:6]
    inverse, factor, margins, listing = held[6:]
    out, blocks_out, solution_out = refs[10:13]
    (
        d32,
        r32,
        t32,
        s_parts,
        stage,
        ext,
        loc,
        send_x,
        send_y,
        send_c,
        recv_x,
        recv_y,
        recv_c,
        factors,
        message,
        partial,
        slots_narrow,
        slots_wide,
        in_sems,
        send_sems,
        recv_sems,
        wave_send,
        wave_recv,
    ) = refs[23:]
    order = factor.shape[1]
    row = lax.axis_index("narrow")
    column = lax.axis_index("wide")
    cells = nx * ny
    own_rows = comps * cells

    fetches = [
        pltpu.make_async_copy(source, target, in_sems.at[k])
        for k, (source, target) in enumerate(zip(operands, held))
    ]
    for fetch in fetches:
        fetch.start()

    def turned(here, count):
        places_of = [here + k for k in range(1, count)]
        return [jnp.where(at >= count, at - count, at) for at in places_of]

    along_narrow = [(at, column) for at in turned(row, narrow)]
    along_wide = [(row, at) for at in turned(column, wide)]
    diagonals = [(x, y) for x in (-1, 1) for y in (-1, 1)]

    def inside(shift_x, shift_y):
        along_x = (row + shift_x >= 0) & (row + shift_x < narrow)
        along_y = (column + shift_y >= 0) & (column + shift_y < wide)
        return along_x & along_y

    barrier = pltpu.get_barrier_semaphore()

    def greet(device):
        pl.semaphore_signal(barrier, inc=1, device_id=device, device_id_type=MESH)

    greetings = narrow - 1 + wide - 1
    for device in along_narrow + along_wide:
        greet(device)
    for shift_x, shift_y in diagonals:
        greetings += jnp.where(inside(shift_x, shift_y), 1, 0)

        @pl.when(inside(shift_x, shift_y))
        def _(shift_x=shift_x, shift_y=shift_y):
            greet((row + shift_x, column + shift_y))

    for k, fetch in enumerate(fetches):
        if k != 6:
            fetch.wait()

    rounded = residual[...].astype(BF16).astype(F32).reshape(own_rows, depth)
    store(r32, rounded, pl.ds(0, own_rows))

    def rows_of(a):
        return pl.ds(pl.multiple_of(a * own_rows, own_rows), own_rows)

    def widen(a, carry):
        d = deflation[a].astype(F32).reshape(own_rows, depth)
        store(d32, d, rows_of(a))
        stage[pl.ds(a, 1), :] = jnp.sum(d * rounded, axis=0, keepdims=True)
        return carry

    lax.fori_loop(0, vectors, widen, 0, unroll=2)
    rhs_column = jnp.sum(stage[pl.ds(0, vectors), :], axis=1, keepdims=True)
    own_block = listing[0, 0, 4]
    own_place = iota((vectors, order), 1) == own_block * vectors + iota((vectors, order), 0)

    def placed(values):
        return jnp.sum(jnp.where(own_place, values, 0.0), axis=0, keepdims=True)

    message[0] = placed(rhs_column)

    x_rows = comps * ny
    y_rows = comps * nx
    for side, x in enumerate((0, nx - 1)):
        face = [
            load(d32, pl.ds((a * comps + j) * cells + x * ny, ny))
            for a in range(vectors)
            for j in range(comps)
        ]
        send_x[side, pl.ds(0, vectors * x_rows), :] = jnp.concatenate(face, axis=0).astype(BF16)
        stage[...] = jnp.zeros_like(stage)
        for j in range(comps):
            stage[pl.ds(j * ny, ny), :] = load(r32, pl.ds(j * cells + x * ny, ny))
        send_x[side, pl.ds(vectors * x_rows, 32), :] = stage[...].astype(BF16)
    for side, y in enumerate((0, ny - 1)):
        face = load(d32, pl.ds(y, vectors * y_rows, stride=ny))
        send_y[side, pl.ds(0, vectors * y_rows), :] = face.astype(BF16)
        stage[...] = jnp.zeros_like(stage)
        stage[pl.ds(0, y_rows), :] = load(r32, pl.ds(y, y_rows, stride=ny))
        send_y[side, pl.ds(vectors * y_rows, 16), :] = stage[pl.ds(0, 16), :].astype(BF16)
    for side_x, x in enumerate((0, nx - 1)):
        for side_y, y in enumerate((0, ny - 1)):
            stage[...] = jnp.zeros_like(stage)
            at = x * ny + y
            stage[pl.ds(0, vectors * comps), :] = load(d32, pl.ds(at, vectors * comps, stride=cells))
            stage[pl.ds(vectors * comps, comps), :] = load(r32, pl.ds(at, comps, stride=cells))
            send_c[side_x * 2 + side_y] = stage[...].astype(BF16)

    pl.semaphore_wait(barrier, greetings)

    def spread_out(source, landing, sem, devices):
        for k, device in enumerate(devices):
            pltpu.make_async_remote_copy(
                src_ref=source,
                dst_ref=landing(k),
                send_sem=wave_send.at[sem],
                recv_sem=wave_recv.at[sem],
                device_id=device,
                device_id_type=MESH,
            ).start()

    def await_all(ref, sems, sem):
        pltpu.make_async_copy(ref, ref, sems.at[sem]).wait()

    def summed(ref, number, start):
        for k in range(ref.shape[1]):
            start = start + ref[number, k]
        return start

    def wave_start(number):
        landing = lambda k: slots_narrow.at[number, k]
        spread_out(message.at[number], landing, 2 * number, along_narrow)

    def wave_middle(number):
        await_all(slots_narrow.at[number], wave_recv, 2 * number)
        partial[number] = summed(slots_narrow, number, message[number])
        landing = lambda k: slots_wide.at[number, k]
        spread_out(partial.at[number], landing, 2 * number + 1, along_wide)

    def wave_end(number):
        await_all(slots_wide.at[number], wave_recv, 2 * number + 1)
        return summed(slots_wide, number, partial[number])

    wave_start(0)

    parity = lax.rem(column, 2)
    half_column = column // 2
    factors[parity, half_column, row] = factor[...]
    spread_out(factor, lambda k: factors.at[parity, half_column, row], 4, along_narrow)
    narrow_rows = factors.at[0, 0, pl.ds(0, narrow - 1)]
    wide_rows = factors.at[0, pl.ds(0, wide // 2 - 1)]

    def copies():
        found = []
        for side, shift in enumerate((-1, 1)):
            found.append((send_x.at[side], recv_x.at[1 - side], recv_x.at[side], shift, 0))
        for side, shift in enumerate((-1, 1)):
            found.append((send_y.at[side], recv_y.at[1 - side], recv_y.at[side], 0, shift))
        for side_x, shift_x in enumerate((-1, 1)):
            for side_y, shift_y in enumerate((-1, 1)):
                at = side_x * 2 + side_y
                found.append((send_c.at[at], recv_c.at[3 - at], recv_c.at[at], shift_x, shift_y))
        return found

    opposite = (1, 0, 3, 2, 7, 6, 5, 4)

    def face_copy(k, source, target, shift_x, shift_y):
        return pltpu.make_async_remote_copy(
            src_ref=source,
            dst_ref=target,
            send_sem=send_sems.at[k],
            recv_sem=recv_sems.at[opposite[k]],
            device_id=(row + shift_x, column + shift_y),
            device_id_type=MESH,
        )

    for k, (source, target, _, shift_x, shift_y) in enumerate(copies()):

        @pl.when(inside(shift_x, shift_y))
        def _(k=k, source=source, target=target, shift_x=shift_x, shift_y=shift_y):
            face_copy(k, source, target, shift_x, shift_y).start()

    total_rows = places.shape[0]
    fixed = own_rows + 2 * x_rows
    group = quotient(iota((1, 3 * own_rows), 1), cells, 3 * comps)
    lanes_of = [group == g for g in range(3 * comps)]
    coupling = []
    for j in range(comps):
        for d in range(9):
            line = jnp.zeros((1, 3 * own_rows), F32)
            for oz in range(3):
                for i in range(comps):
                    line = jnp.where(lanes_of[oz * comps + i], stencil[i, j, d * 3 + oz], line)
            coupling.append(line)
    all_j = range(comps)
    chunks = [(j * cells, cells, range(j * 9, j * 9 + 9)) for j in all_j]
    for side in range(2):
        at = own_rows + side * x_rows
        for j in all_j:
            dx = j * 9 + 6 * side
            chunks.append((at + j * ny, ny, range(dx, dx + 3)))
    y_size = pad_to(y_rows, 8)
    for side in range(2):
        entries = [j * 9 + 3 * dx + 2 * side for j in all_j for dx in range(3)]
        chunks.append((fixed + side * y_size, y_size, entries))
    corner_entries = [j * 9 + d for j in all_j for d in (0, 2, 6, 8)]
    chunks.append((fixed + 2 * y_size, total_rows - fixed - 2 * y_size, corner_entries))
    for start, size, entries in chunks:
        here = places[pl.ds(start, size), :]
        value = jnp.zeros(here.shape, F32)
        for e in entries:
            value = jnp.where(here == e, coupling[e], value)
        s_parts[pl.ds(start, size), pl.ds(0, 3 * own_rows)] = value
    high, low = split(s_parts[:, pl.ds(0, 3 * own_rows)])
    s_parts[:, pl.ds(3 * own_rows, 3 * own_rows)] = high.astype(F32)
    s_parts[:, pl.ds(6 * own_rows, 3 * own_rows)] = low.astype(F32)
    s_all = s_parts[...].astype(BF16)

    lane = iota((own_rows, depth), 1)
    scale = jnp.concatenate([stiffness[...].reshape(cells, depth)] * comps, axis=0)
    weight = jnp.concatenate([mass[...].reshape(cells, depth)] * comps, axis=0)

    def adjoint(a, carry):
        d = load(d32, rows_of(a))
        w = d * scale
        before = jnp.where(lane == depth - 1, 0.0, pltpu.roll(w, depth - 1, axis=1))
        after = jnp.where(lane == 0, 0.0, pltpu.roll(w, 1, axis=1))
        parts = [split(shifted) for shifted in (before, w, after)]
        highs, lows = [part[0] for part in parts], [part[1] for part in parts]
        w_all = jnp.concatenate(highs + lows + highs, axis=0)
        image = jnp.dot(s_all, w_all, preferred_element_type=F32)
        t32[a, pl.ds(own_rows, total_rows - own_rows), :] = image[own_rows:]
        t32[a, pl.ds(0, own_rows), :] = image[:own_rows] + weight * d
        return carry

    lax.fori_loop(0, vectors // 2, adjoint, 0, unroll=4)
    wave_middle(0)
    await_all(narrow_rows, wave_recv, 4)
    mine = factors.at[parity, half_column]
    spread_out(mine, lambda k: mine, 5, along_wide[1::2])
    lax.fori_loop(vectors // 2, vectors, adjoint, 0, unroll=4)
    await_all(wide_rows, wave_recv, 5)
    hand_on = pltpu.make_async_remote_copy(
        src_ref=factors.at[parity],
        dst_ref=factors.at[parity],
        send_sem=wave_send.at[6],
        recv_sem=wave_recv.at[6],
        device_id=(row, column + 1 - 2 * parity),
        device_id_type=MESH,
    )
    hand_on.start()

    width = 9 * vectors

    def picked(product, row_of, left_size):
        columns = product.shape[1]
        kept = iota((left_size, columns), 0) == row_of(iota((1, columns), 1))
        parts = product.reshape(vectors, left_size, columns)
        return jnp.sum(jnp.where(kept[None], parts, 0.0), axis=1)

    def folded(values, lane_of):
        rows = values.shape[1]
        chosen = (lane_of(iota((rows, 1), 0)) == iota((rows, width), 1)).astype(F32)
        return exact_dot(values, chosen)

    def within(size):
        return lambda c: c - size * quotient(c, size, vectors)

    def lane_in(block, size):
        return lambda c: block * vectors + quotient(c, size, vectors)

    total = None
    for j in range(comps):
        left = t32[:, pl.ds(j * cells, cells), :].reshape(vectors * cells, depth)
        right = jnp.concatenate(
            [load(d32, pl.ds((b * comps + j) * cells, cells)) for b in range(vectors)], axis=0
        ).astype(BF16)
        part = gram(left, right)
        total = part if total is None else total + part

    for k, (source, target, landing, shift_x, shift_y) in enumerate(copies()):

        @pl.when(inside(shift_x, shift_y))
        def _(k=k, source=source, landing=landing, shift_x=shift_x, shift_y=shift_y):
            pltpu.make_async_remote_copy(
                src_ref=source,
                dst_ref=landing,
                send_sem=send_sems.at[k],
                recv_sem=recv_sems.at[k],
                device_id=(row + shift_x, column + shift_y),
                device_id_type=MESH,
            ).wait()

        @pl.when(jnp.logical_not(inside(shift_x, shift_y)))
        def _(landing=landing):
            landing[...] = jnp.zeros(landing.shape, BF16)

    y_padded = pad_to(y_rows, 8)
    c_padded = pad_to(4 * comps, 8)

    def corner_parts(c):
        corner = quotient(c, 32, 4)
        at = c - 32 * corner
        vector = quotient(at, comps, vectors)
        return at < vectors * comps, corner, vector, at - comps * vector

    def corner_row(c):
        real, corner, _, j = corner_parts(c)
        return jnp.where(real, corner * comps + j, -1)

    def corner_lane(c):
        real, corner, vector, _ = corner_parts(c)
        block = corner * 2 + jnp.where(corner >= 2, 2, 0)
        return jnp.where(real, block * vectors + vector, -1)

    coarse_rhs = wave_end(0)
    hand_on.wait()

    def solve(vector):
        def one(d, total):
            for k in range(2 * narrow):
                f = factors[k // narrow, d, k % narrow]
                total = total + f * jnp.sum(f * vector, axis=1, keepdims=True)
            return total

        zeros = jnp.zeros((factor.shape[0], order), F32)
        total = lax.fori_loop(0, wide // 2, one, zeros, unroll=4)
        return jnp.sum(total, axis=0, keepdims=True)

    first = solve(coarse_rhs)
    near = [
        iota((vectors, order), 1) == listing[0, 0, k] * vectors + iota((vectors, order), 0)
        for k in range(9)
    ]
    parts_of = [jnp.sum(jnp.where(m, first, 0.0), axis=1, keepdims=True) for m in near]

    def weights_on(lanes, block):
        chosen = iota((vectors, lanes.shape[1]), 0) == lanes
        return jnp.sum(jnp.where(chosen, parts_of[block], 0.0), axis=0, keepdims=True)

    def mixed(values, weights, row_of, count):
        lanes = iota((1, values.shape[0]), 1)
        matrix = jnp.where(iota((count, values.shape[0]), 0) == row_of(lanes), weights, 0.0)
        high = matrix.astype(BF16).astype(F32)
        both = jnp.concatenate([high, matrix - high], axis=0).astype(BF16)
        product = jnp.dot(both, values, preferred_element_type=F32)
        return product[:count] + product[count:]

    field = parts_of[4][0:1, :] * load(d32, rows_of(0))
    for b in range(1, vectors):
        field += parts_of[4][b : b + 1, :] * load(d32, rows_of(b))
    fields = [field]
    for side, block in enumerate((1, 7)):
        lanes = quotient(iota((1, vectors * x_rows), 1), x_rows, vectors)
        values = recv_x[side, pl.ds(0, vectors * x_rows), :]
        fields.append(mixed(values, weights_on(lanes, block), within(x_rows), x_rows))
    for side, block in enumerate((3, 5)):
        lanes = quotient(iota((1, vectors * y_rows), 1), y_rows, vectors)
        values = recv_y[side, pl.ds(0, vectors * y_rows), :]
        fields.append(mixed(values, weights_on(lanes, block), within(y_rows), y_padded))
    real, corner, vector, _ = corner_parts(iota((1, 4 * 32), 1))
    weights = jnp.zeros((1, 4 * 32), F32)
    for k, block in enumerate((0, 2, 6, 8)):
        weights += weights_on(jnp.where(real & (corner == k), vector, -1), block)
    fields.append(mixed(recv_c[...].reshape(4 * 32, depth), weights, corner_row, c_padded))
    field = jnp.concatenate(fields, axis=0)

    def imaged(a, carry):
        stage[pl.ds(a, 1), :] = jnp.sum(t32[a] * field, axis=0, keepdims=True)
        return carry

    lax.fori_loop(0, vectors, imaged, 0, unroll=2)
    message[1] = placed(jnp.sum(stage[pl.ds(0, vectors), :], axis=1, keepdims=True))
    wave_start(1)

    blocks = folded(picked(total, within(cells), cells), lane_in(4, cells))
    for side in range(2):
        block = 1 if side == 0 else 7
        left = t32[:, pl.ds(own_rows + side * x_rows, x_rows), :].reshape(vectors * x_rows, depth)
        part = gram(left, recv_x[side, pl.ds(0, vectors * x_rows), :])
        blocks += folded(picked(part, within(x_rows), x_rows), lane_in(block, x_rows))
    wave_middle(1)
    for side in range(2):
        block = 3 if side == 0 else 5
        left = t32[:, pl.ds(fixed + side * y_padded, y_padded), :]
        left = left.reshape(vectors * y_padded, depth)
        part = gram(left, recv_y[side, pl.ds(0, vectors * y_rows), :])
        blocks += folded(picked(part, within(y_rows), y_padded), lane_in(block, y_rows))
    left = t32[:, pl.ds(fixed + 2 * y_padded, c_padded), :].reshape(vectors * c_padded, depth)
    part = gram(left, recv_c[...].reshape(4 * 32, depth))

    blocks += folded(picked(part, corner_row, c_padded), corner_lane)

    pairs = vectors * vectors
    repeated = jnp.broadcast_to(blocks[:, None, :], (vectors, vectors, width))
    right = iota((1, vectors, width), 2)
    right = right - vectors * quotient(right, vectors, 9)
    kept = jnp.where(right == iota((1, vectors, width), 1), repeated, 0.0).reshape(pairs, width)
    neighbour = quotient(iota((width, 1), 0), vectors, 9)
    to_lane = (neighbour == iota((width, 9), 1)).astype(F32)
    turned_blocks = exact_dot(kept, to_lane)
    blocks_out[0, 0] = turned_blocks.reshape(vectors, vectors, 9)

    high_y = ny + 2

    def ext_at(j, f, e):
        return (j * high_y + f) * 8 + e

    for j in range(comps):
        for y in range(ny):
            values = load(r32, pl.ds(j * cells + y, nx, stride=ny))
            store(ext, values, pl.ds(ext_at(j, 1 + y, 1), nx))
    for side in range(2):
        at_x = side * (nx + 1)
        values = recv_x[side, pl.ds(vectors * x_rows, 32), :].astype(F32)
        for j in range(comps):
            for y in range(ny):
                line = values[j * ny + y : j * ny + y + 1]
                store(ext, line, pl.ds(ext_at(j, 1 + y, at_x), 1))
        at_y = side * (ny + 1)
        values = recv_y[side, pl.ds(vectors * y_rows, 16), :].astype(F32)
        for j in range(comps):
            store(ext, values[j * nx : (j + 1) * nx], pl.ds(ext_at(j, at_y, 1), nx))
        for side_y in range(2):
            values = recv_c[side * 2 + side_y].astype(F32)
            for j in range(comps):
                at = vectors * comps + j
                line = values[at : at + 1]
                store(ext, line, pl.ds(ext_at(j, side_y * (ny + 1), at_x), 1))

    half_x = (nx + 2) // 2
    half_y = (ny + 2) // 2
    kept_x = []
    for s in range(2):
        e = 2 * iota((half_x, depth), 0) + s
        kept_x.append((e >= margins[0, 0, 0, 0]) & (e < margins[0, 0, 0, 1]))
    fetches[6].wait()

    def local_row(v, carry):
        grouped = []
        for j in range(comps):
            for s in range(2):
                for t in range(2):
                    f = 2 * v + t
                    kept = (f >= margins[0, 0, 1, 0]) & (f < margins[0, 0, 1, 1])
                    factor_y = jnp.where(kept, 1.0, 0.0).astype(F32)
                    values = load(ext, pl.ds(ext_at(j, f, s), half_x, stride=2))
                    grouped.append(jnp.where(kept_x[s], values, 0.0) * factor_y)
        for j in range(comps):
            for s in range(2):
                for t in range(2):
                    i = 4 * j + 2 * s + t
                    acc = inverse[i, 0, v].astype(F32) * grouped[0]
                    for m in range(1, 4 * comps):
                        acc += inverse[i, m, v].astype(F32) * grouped[m]
                    store(loc, acc, pl.ds(ext_at(j, 2 * v + t, s), half_x, stride=2))
        return carry

    lax.fori_loop(0, half_y, local_row, 0)

    coarse_image = wave_end(1)
    refined = first + solve(coarse_rhs - coarse_image)
    solution_out[...] = refined
    weights = jnp.sum(jnp.where(own_place, refined, 0.0), axis=1, keepdims=True)
    for j in range(comps):
        for x in range(nx):
            value = load(loc, pl.ds(ext_at(j, 1, 1 + x), ny, stride=8))
            for a in range(vectors):
                at = (a * comps + j) * cells + x * ny
                value += weights[a : a + 1, :] * load(d32, pl.ds(at, ny))
            out[j, x] = value

    for number in range(2):
        await_all(slots_narrow.at[number], wave_send, 2 * number)
        await_all(slots_wide.at[number], wave_send, 2 * number + 1)
    await_all(narrow_rows, wave_send, 4)
    await_all(wide_rows, wave_send, 5)


def write_out(*refs):
    sources, targets, sems = refs[:3], refs[3:6], refs[6]
    copies = [
        pltpu.make_async_copy(source, target, sems.at[k])
        for k, (source, target) in enumerate(zip(sources, targets))
    ]
    for copy in copies:
        copy.start()
    for copy in copies:
        copy.wait()


def body(
    narrow,
    wide,
    deflation,
    residual,
    stiffness,
    mass,
    stencil,
    local_inverse,
    inverse_factor,
    margin_range,
    neighbor_blocks,
):
    vectors, comps, nx, ny, depth = deflation.shape
    order = inverse_factor.shape[1]
    cells = nx * ny
    places = stencil_places(comps, nx, ny)
    turned_inverse = local_inverse.transpose(0, 1, 3, 2, 4)
    x_send = vectors * comps * ny + 32
    y_send = vectors * comps * nx + 16
    anywhere = pl.BlockSpec(memory_space=pl.ANY)
    operands = (
        deflation,
        residual,
        stiffness,
        mass,
        jnp.asarray(places),
        stencil.transpose(1, 2, 0),
        turned_inverse,
        inverse_factor,
        margin_range,
        neighbor_blocks,
    )
    spaces = [pltpu.VMEM] * 5 + [pltpu.SMEM] + [pltpu.VMEM] * 2 + [pltpu.SMEM] * 2
    shapes = (
        jax.ShapeDtypeStruct(residual.shape, F32),
        jax.ShapeDtypeStruct((1, 1, vectors, vectors, 9), F32),
        jax.ShapeDtypeStruct((1, order), F32),
    )
    results = pl.pallas_call(
        functools.partial(kernel, narrow, wide, vectors, comps, nx, ny, depth),
        out_shape=tuple(pltpu.VMEM(shape.shape, shape.dtype) for shape in shapes),
        in_specs=[anywhere] * len(operands),
        out_specs=(pl.BlockSpec(memory_space=pltpu.VMEM),) * len(shapes),
        scratch_shapes=[space(o.shape, o.dtype) for space, o in zip(spaces, operands)]
        + [
            pltpu.VMEM((depth // 128, vectors * comps * cells, 128), F32),
            pltpu.VMEM((depth // 128, comps * cells, 128), F32),
            pltpu.VMEM((vectors, places.shape[0], depth), F32),
            pltpu.VMEM((places.shape[0], 9 * comps * cells), F32),
            pltpu.VMEM((32, depth), F32),
            pltpu.VMEM((depth // 128, comps * (ny + 2) * 8, 128), F32),
            pltpu.VMEM((depth // 128, comps * (ny + 2) * 8, 128), F32),
            pltpu.VMEM((2, x_send, depth), BF16),
            pltpu.VMEM((2, y_send, depth), BF16),
            pltpu.VMEM((4, 32, depth), BF16),
            pltpu.VMEM((2, x_send, depth), BF16),
            pltpu.VMEM((2, y_send, depth), BF16),
            pltpu.VMEM((4, 32, depth), BF16),
            pltpu.VMEM((2, wide // 2, narrow) + inverse_factor.shape, F32),
            pltpu.VMEM((2, 1, order), F32),
            pltpu.VMEM((2, 1, order), F32),
            pltpu.VMEM((2, narrow - 1, 1, order), F32),
            pltpu.VMEM((2, wide - 1, 1, order), F32),
            pltpu.SemaphoreType.DMA((len(operands),)),
            pltpu.SemaphoreType.DMA((8,)),
            pltpu.SemaphoreType.DMA((8,)),
            pltpu.SemaphoreType.DMA((7,)),
            pltpu.SemaphoreType.DMA((7,)),
        ],
        compiler_params=pltpu.CompilerParams(
            collective_id=0, has_side_effects=True, vmem_limit_bytes=60 * 1024 * 1024
        ),
    )(*operands)
    result, blocks, refined = pl.pallas_call(
        write_out,
        out_shape=tuple(jax.ShapeDtypeStruct(r.shape, r.dtype) for r in results),
        in_specs=[pl.BlockSpec(memory_space=pltpu.VMEM)] * 3,
        out_specs=(anywhere,) * 3,
        scratch_shapes=[pltpu.SemaphoreType.DMA((3,))],
        compiler_params=pltpu.CompilerParams(vmem_limit_bytes=2 * 1024 * 1024),
    )(*results)
    return result, blocks.transpose(0, 1, 4, 2, 3), refined.reshape(order)


def solution(mesh):
    placed = (
        P(None, None, "narrow", "wide", None),
        P(None, "narrow", "wide", None),
        P("narrow", "wide", None),
        P("narrow", "wide", None),
        P(),
        P(None, None, "narrow", "wide", None),
        P(("narrow", "wide"), None),
        P("narrow", "wide", None, None),
        P("narrow", "wide", None),
    )
    return jax.shard_map(
        functools.partial(body, mesh.shape["narrow"], mesh.shape["wide"]),
        mesh=mesh,
        in_specs=placed,
        out_specs=(P(None, "narrow", "wide", None), P("narrow", "wide", None, None, None), P()),
        check_vma=False,
    )
```

```python
import functools

import jax
import jax.numpy as jnp
import numpy as np
from jax import lax
from jax.experimental import pallas as pl
from jax.experimental.pallas import tpu as pltpu
from jax.sharding import PartitionSpec as P

F32 = jnp.float32
BF16 = jnp.bfloat16
MESH = pl.DeviceIdType.MESH


def pad_to(count, unit):
    return -(-count // unit) * unit


def stencil_places(comps, nx, ny):
    rows = []
    for j in range(comps):
        rows += [(j, x, y) for x in range(nx) for y in range(ny)]
    for x in (-1, nx):
        rows += [(j, x, y) for j in range(comps) for y in range(ny)]
    for y in (-1, ny):
        face = [(j, x, y) for j in range(comps) for x in range(nx)]
        rows += face + [None] * (pad_to(len(face), 8) - len(face))
    corners = [(j, x, y) for x in (-1, nx) for y in (-1, ny) for j in range(comps)]
    rows += corners + [None] * (pad_to(len(corners), 8) - len(corners))
    cells = comps * nx * ny
    table = np.full((len(rows), 3 * cells), -1, np.int32)
    for r, row in enumerate(rows):
        if row is None:
            continue
        j, x, y = row
        for oz in range(3):
            for i in range(comps):
                for px in range(nx):
                    for py in range(ny):
                        dx, dy = x - px, y - py
                        if abs(dx) <= 1 and abs(dy) <= 1:
                            column = oz * cells + i * nx * ny + px * ny + py
                            table[r, column] = j * 9 + (dx + 1) * 3 + dy + 1
    return table


def split(values):
    high = values.astype(BF16)
    return high, (values - high.astype(F32)).astype(BF16)


def iota(shape, axis):
    return lax.broadcasted_iota(jnp.int32, shape, axis)


def load(ref, *at):
    return jnp.concatenate([ref[(h,) + at] for h in range(ref.shape[0])], axis=-1)


def store(ref, values, *at):
    for h in range(ref.shape[0]):
        ref[(h,) + at] = values[:, h * 128 : (h + 1) * 128]


def quotient(values, size, count):
    return sum((values >= k * size).astype(jnp.int32) for k in range(1, count))


def exact_dot(values, chosen):
    rows = values.shape[0]
    high = values.astype(BF16).astype(F32)
    middle = (values - high).astype(BF16).astype(F32)
    low = values - high - middle
    parts = jnp.concatenate([high, middle, low], axis=0).astype(BF16)
    product = jnp.dot(parts, chosen.astype(BF16), preferred_element_type=F32)
    return product[:rows] + product[rows : 2 * rows] + product[2 * rows :]


def gram(left, right):
    dims = (((1,), (1,)), ((), ()))
    rows = left.shape[0]
    both = jnp.concatenate(split(left), axis=0)
    product = lax.dot_general(both, right, dims, preferred_element_type=F32)
    return product[:rows] + product[rows:]


def kernel(
    narrow,
    wide,
    vectors,
    comps,
    nx,
    ny,
    depth,
    *refs,
):
    operands, held = refs[:10], refs[13:23]
    deflation, residual, stiffness, mass, places, stencil = held[:6]
    inverse, factor, margins, listing = held[6:]
    out, blocks_out, solution_out = refs[10:13]
    (
        d32,
        r32,
        t32,
        s_parts,
        stage,
        ext,
        loc,
        send_x,
        send_y,
        send_c,
        recv_x,
        recv_y,
        recv_c,
        factors,
        message,
        partial,
        slots_narrow,
        slots_wide,
        in_sems,
        send_sems,
        recv_sems,
        wave_send,
        wave_recv,
    ) = refs[23:]
    order = factor.shape[1]
    row = lax.axis_index("narrow")
    column = lax.axis_index("wide")
    cells = nx * ny
    own_rows = comps * cells

    fetches = [
        pltpu.make_async_copy(source, target, in_sems.at[k])
        for k, (source, target) in enumerate(zip(operands, held))
    ]
    for fetch in fetches:
        fetch.start()

    def turned(here, count):
        places_of = [here + k for k in range(1, count)]
        return [jnp.where(at >= count, at - count, at) for at in places_of]

    along_narrow = [(at, column) for at in turned(row, narrow)]
    along_wide = [(row, at) for at in turned(column, wide)]
    diagonals = [(x, y) for x in (-1, 1) for y in (-1, 1)]

    def inside(shift_x, shift_y):
        along_x = (row + shift_x >= 0) & (row + shift_x < narrow)
        along_y = (column + shift_y >= 0) & (column + shift_y < wide)
        return along_x & along_y

    barrier = pltpu.get_barrier_semaphore()

    def greet(device):
        pl.semaphore_signal(barrier, inc=1, device_id=device, device_id_type=MESH)

    greetings = narrow - 1 + wide - 1
    for device in along_narrow + along_wide:
        greet(device)
    for shift_x, shift_y in diagonals:
        greetings += jnp.where(inside(shift_x, shift_y), 1, 0)

        @pl.when(inside(shift_x, shift_y))
        def _(shift_x=shift_x, shift_y=shift_y):
            greet((row + shift_x, column + shift_y))

    for k, fetch in enumerate(fetches):
        if k != 6:
            fetch.wait()

    rounded = residual[...].astype(BF16).astype(F32).reshape(own_rows, depth)
    store(r32, rounded, pl.ds(0, own_rows))

    def rows_of(a):
        return pl.ds(pl.multiple_of(a * own_rows, own_rows), own_rows)

    def widen(a, carry):
        d = deflation[a].astype(F32).reshape(own_rows, depth)
        store(d32, d, rows_of(a))
        stage[pl.ds(a, 1), :] = jnp.sum(d * rounded, axis=0, keepdims=True)
        return carry

    lax.fori_loop(0, vectors, widen, 0, unroll=2)
    rhs_column = jnp.sum(stage[pl.ds(0, vectors), :], axis=1, keepdims=True)
    own_block = listing[0, 0, 4]
    own_place = iota((vectors, order), 1) == own_block * vectors + iota((vectors, order), 0)

    def placed(values):
        return jnp.sum(jnp.where(own_place, values, 0.0), axis=0, keepdims=True)

    message[0] = placed(rhs_column)

    x_rows = comps * ny
    y_rows = comps * nx
    for side, x in enumerate((0, nx - 1)):
        face = [
            load(d32, pl.ds((a * comps + j) * cells + x * ny, ny))
            for a in range(vectors)
            for j in range(comps)
        ]
        send_x[side, pl.ds(0, vectors * x_rows), :] = jnp.concatenate(face, axis=0).astype(BF16)
        stage[...] = jnp.zeros_like(stage)
        for j in range(comps):
            stage[pl.ds(j * ny, ny), :] = load(r32, pl.ds(j * cells + x * ny, ny))
        send_x[side, pl.ds(vectors * x_rows, 32), :] = stage[...].astype(BF16)
    for side, y in enumerate((0, ny - 1)):
        face = load(d32, pl.ds(y, vectors * y_rows, stride=ny))
        send_y[side, pl.ds(0, vectors * y_rows), :] = face.astype(BF16)
        stage[...] = jnp.zeros_like(stage)
        stage[pl.ds(0, y_rows), :] = load(r32, pl.ds(y, y_rows, stride=ny))
        send_y[side, pl.ds(vectors * y_rows, 16), :] = stage[pl.ds(0, 16), :].astype(BF16)
    for side_x, x in enumerate((0, nx - 1)):
        for side_y, y in enumerate((0, ny - 1)):
            stage[...] = jnp.zeros_like(stage)
            at = x * ny + y
            stage[pl.ds(0, vectors * comps), :] = load(d32, pl.ds(at, vectors * comps, stride=cells))
            stage[pl.ds(vectors * comps, comps), :] = load(r32, pl.ds(at, comps, stride=cells))
            send_c[side_x * 2 + side_y] = stage[...].astype(BF16)

    pl.semaphore_wait(barrier, greetings)

    def spread_out(source, landing, sem, devices):
        for k, device in enumerate(devices):
            pltpu.make_async_remote_copy(
                src_ref=source,
                dst_ref=landing(k),
                send_sem=wave_send.at[sem],
                recv_sem=wave_recv.at[sem],
                device_id=device,
                device_id_type=MESH,
            ).start()

    def await_all(ref, sems, sem):
        pltpu.make_async_copy(ref, ref, sems.at[sem]).wait()

    def summed(ref, number, start):
        for k in range(ref.shape[1]):
            start = start + ref[number, k]
        return start

    def wave_start(number):
        landing = lambda k: slots_narrow.at[number, k]
        spread_out(message.at[number], landing, 2 * number, along_narrow)

    def wave_middle(number):
        await_all(slots_narrow.at[number], wave_recv, 2 * number)
        partial[number] = summed(slots_narrow, number, message[number])
        landing = lambda k: slots_wide.at[number, k]
        spread_out(partial.at[number], landing, 2 * number + 1, along_wide)

    def wave_end(number):
        await_all(slots_wide.at[number], wave_recv, 2 * number + 1)
        return summed(slots_wide, number, partial[number])

    wave_start(0)

    parity = lax.rem(column, 2)
    half_column = column // 2
    factors[parity, half_column, row] = factor[...]
    spread_out(factor, lambda k: factors.at[parity, half_column, row], 4, along_narrow)
    narrow_rows = factors.at[0, 0, pl.ds(0, narrow - 1)]
    wide_rows = factors.at[0, pl.ds(0, wide // 2 - 1)]

    def copies():
        found = []
        for side, shift in enumerate((-1, 1)):
            found.append((send_x.at[side], recv_x.at[1 - side], recv_x.at[side], shift, 0))
        for side, shift in enumerate((-1, 1)):
            found.append((send_y.at[side], recv_y.at[1 - side], recv_y.at[side], 0, shift))
        for side_x, shift_x in enumerate((-1, 1)):
            for side_y, shift_y in enumerate((-1, 1)):
                at = side_x * 2 + side_y
                found.append((send_c.at[at], recv_c.at[3 - at], recv_c.at[at], shift_x, shift_y))
        return found

    opposite = (1, 0, 3, 2, 7, 6, 5, 4)

    def face_copy(k, source, target, shift_x, shift_y):
        return pltpu.make_async_remote_copy(
            src_ref=source,
            dst_ref=target,
            send_sem=send_sems.at[k],
            recv_sem=recv_sems.at[opposite[k]],
            device_id=(row + shift_x, column + shift_y),
            device_id_type=MESH,
        )

    for k, (source, target, _, shift_x, shift_y) in enumerate(copies()):

        @pl.when(inside(shift_x, shift_y))
        def _(k=k, source=source, target=target, shift_x=shift_x, shift_y=shift_y):
            face_copy(k, source, target, shift_x, shift_y).start()

    total_rows = places.shape[0]
    fixed = own_rows + 2 * x_rows
    group = quotient(iota((1, 3 * own_rows), 1), cells, 3 * comps)
    lanes_of = [group == g for g in range(3 * comps)]
    coupling = []
    for j in range(comps):
        for d in range(9):
            line = jnp.zeros((1, 3 * own_rows), F32)
            for oz in range(3):
                for i in range(comps):
                    line = jnp.where(lanes_of[oz * comps + i], stencil[i, j, d * 3 + oz], line)
            coupling.append(line)
    all_j = range(comps)
    chunks = [(j * cells, cells, range(j * 9, j * 9 + 9)) for j in all_j]
    for side in range(2):
        at = own_rows + side * x_rows
        for j in all_j:
            dx = j * 9 + 6 * side
            chunks.append((at + j * ny, ny, range(dx, dx + 3)))
    y_size = pad_to(y_rows, 8)
    for side in range(2):
        entries = [j * 9 + 3 * dx + 2 * side for j in all_j for dx in range(3)]
        chunks.append((fixed + side * y_size, y_size, entries))
    corner_entries = [j * 9 + d for j in all_j for d in (0, 2, 6, 8)]
    chunks.append((fixed + 2 * y_size, total_rows - fixed - 2 * y_size, corner_entries))
    for start, size, entries in chunks:
        here = places[pl.ds(start, size), :]
        value = jnp.zeros(here.shape, F32)
        for e in entries:
            value = jnp.where(here == e, coupling[e], value)
        s_parts[pl.ds(start, size), pl.ds(0, 3 * own_rows)] = value
    high, low = split(s_parts[:, pl.ds(0, 3 * own_rows)])
    s_parts[:, pl.ds(3 * own_rows, 3 * own_rows)] = high.astype(F32)
    s_parts[:, pl.ds(6 * own_rows, 3 * own_rows)] = low.astype(F32)
    s_all = s_parts[...].astype(BF16)

    lane = iota((own_rows, depth), 1)
    scale = jnp.concatenate([stiffness[...].reshape(cells, depth)] * comps, axis=0)
    weight = jnp.concatenate([mass[...].reshape(cells, depth)] * comps, axis=0)

    def adjoint(a, carry):
        d = load(d32, rows_of(a))
        w = d * scale
        before = jnp.where(lane == depth - 1, 0.0, pltpu.roll(w, depth - 1, axis=1))
        after = jnp.where(lane == 0, 0.0, pltpu.roll(w, 1, axis=1))
        parts = [split(shifted) for shifted in (before, w, after)]
        highs, lows = [part[0] for part in parts], [part[1] for part in parts]
        w_all = jnp.concatenate(highs + lows + highs, axis=0)
        image = jnp.dot(s_all, w_all, preferred_element_type=F32)
        t32[a, pl.ds(own_rows, total_rows - own_rows), :] = image[own_rows:]
        t32[a, pl.ds(0, own_rows), :] = image[:own_rows] + weight * d
        return carry

    lax.fori_loop(0, vectors // 2, adjoint, 0, unroll=4)
    wave_middle(0)
    await_all(narrow_rows, wave_recv, 4)
    mine = factors.at[parity, half_column]
    spread_out(mine, lambda k: mine, 5, along_wide[1::2])
    lax.fori_loop(vectors // 2, vectors, adjoint, 0, unroll=4)
    await_all(wide_rows, wave_recv, 5)
    hand_on = pltpu.make_async_remote_copy(
        src_ref=factors.at[parity],
        dst_ref=factors.at[parity],
        send_sem=wave_send.at[6],
        recv_sem=wave_recv.at[6],
        device_id=(row, column + 1 - 2 * parity),
        device_id_type=MESH,
    )
    hand_on.start()

    width = 9 * vectors

    def picked(product, row_of, left_size):
        columns = product.shape[1]
        kept = iota((left_size, columns), 0) == row_of(iota((1, columns), 1))
        parts = product.reshape(vectors, left_size, columns)
        return jnp.sum(jnp.where(kept[None], parts, 0.0), axis=1)

    def folded(values, lane_of):
        rows = values.shape[1]
        chosen = (lane_of(iota((rows, 1), 0)) == iota((rows, width), 1)).astype(F32)
        return exact_dot(values, chosen)

    def within(size):
        return lambda c: c - size * quotient(c, size, vectors)

    def lane_in(block, size):
        return lambda c: block * vectors + quotient(c, size, vectors)

    lefts = []
    rights = []
    for j in range(comps):
        left = t32[:, pl.ds(j * cells, cells), :]
        lefts.append(left.reshape(vectors * cells, depth))
        pieces = [load(d32, pl.ds((b * comps + j) * cells, cells)) for b in range(vectors)]
        rights.append(jnp.concatenate(pieces, axis=0).astype(BF16))
    total = gram(jnp.concatenate(lefts, axis=1), jnp.concatenate(rights, axis=1))

    for k, (source, target, landing, shift_x, shift_y) in enumerate(copies()):

        @pl.when(inside(shift_x, shift_y))
        def _(k=k, source=source, landing=landing, shift_x=shift_x, shift_y=shift_y):
            pltpu.make_async_remote_copy(
                src_ref=source,
                dst_ref=landing,
                send_sem=send_sems.at[k],
                recv_sem=recv_sems.at[k],
                device_id=(row + shift_x, column + shift_y),
                device_id_type=MESH,
            ).wait()

        @pl.when(jnp.logical_not(inside(shift_x, shift_y)))
        def _(landing=landing):
            landing[...] = jnp.zeros(landing.shape, BF16)

    y_padded = pad_to(y_rows, 8)
    c_padded = pad_to(4 * comps, 8)

    def corner_parts(c):
        corner = quotient(c, 32, 4)
        at = c - 32 * corner
        vector = quotient(at, comps, vectors)
        return at < vectors * comps, corner, vector, at - comps * vector

    def corner_row(c):
        real, corner, _, j = corner_parts(c)
        return jnp.where(real, corner * comps + j, -1)

    def corner_lane(c):
        real, corner, vector, _ = corner_parts(c)
        block = corner * 2 + jnp.where(corner >= 2, 2, 0)
        return jnp.where(real, block * vectors + vector, -1)

    coarse_rhs = wave_end(0)
    hand_on.wait()

    def solve(vector):
        def one(d, total):
            for k in range(2 * narrow):
                f = factors[k // narrow, d, k % narrow]
                total = total + f * jnp.sum(f * vector, axis=1, keepdims=True)
            return total

        zeros = jnp.zeros((factor.shape[0], order), F32)
        total = lax.fori_loop(0, wide // 2, one, zeros, unroll=4)
        return jnp.sum(total, axis=0, keepdims=True)

    first = solve(coarse_rhs)
    near = [
        iota((vectors, order), 1) == listing[0, 0, k] * vectors + iota((vectors, order), 0)
        for k in range(9)
    ]
    parts_of = [jnp.sum(jnp.where(m, first, 0.0), axis=1, keepdims=True) for m in near]

    def weights_on(lanes, block):
        chosen = iota((vectors, lanes.shape[1]), 0) == lanes
        return jnp.sum(jnp.where(chosen, parts_of[block], 0.0), axis=0, keepdims=True)

    def mixed(values, weights, row_of, count):
        lanes = iota((1, values.shape[0]), 1)
        matrix = jnp.where(iota((count, values.shape[0]), 0) == row_of(lanes), weights, 0.0)
        high = matrix.astype(BF16).astype(F32)
        both = jnp.concatenate([high, matrix - high], axis=0).astype(BF16)
        product = jnp.dot(both, values, preferred_element_type=F32)
        return product[:count] + product[count:]

    field = parts_of[4][0:1, :] * load(d32, rows_of(0))
    for b in range(1, vectors):
        field += parts_of[4][b : b + 1, :] * load(d32, rows_of(b))
    fields = [field]
    for side, block in enumerate((1, 7)):
        lanes = quotient(iota((1, vectors * x_rows), 1), x_rows, vectors)
        values = recv_x[side, pl.ds(0, vectors * x_rows), :]
        fields.append(mixed(values, weights_on(lanes, block), within(x_rows), x_rows))
    for side, block in enumerate((3, 5)):
        lanes = quotient(iota((1, vectors * y_rows), 1), y_rows, vectors)
        values = recv_y[side, pl.ds(0, vectors * y_rows), :]
        fields.append(mixed(values, weights_on(lanes, block), within(y_rows), y_padded))
    real, corner, vector, _ = corner_parts(iota((1, 4 * 32), 1))
    weights = jnp.zeros((1, 4 * 32), F32)
    for k, block in enumerate((0, 2, 6, 8)):
        weights += weights_on(jnp.where(real & (corner == k), vector, -1), block)
    fields.append(mixed(recv_c[...].reshape(4 * 32, depth), weights, corner_row, c_padded))
    field = jnp.concatenate(fields, axis=0)

    def imaged(a, carry):
        stage[pl.ds(a, 1), :] = jnp.sum(t32[a] * field, axis=0, keepdims=True)
        return carry

    lax.fori_loop(0, vectors, imaged, 0, unroll=2)
    message[1] = placed(jnp.sum(stage[pl.ds(0, vectors), :], axis=1, keepdims=True))
    wave_start(1)

    blocks = folded(picked(total, within(cells), cells), lane_in(4, cells))
    for side in range(2):
        block = 1 if side == 0 else 7
        left = t32[:, pl.ds(own_rows + side * x_rows, x_rows), :].reshape(vectors * x_rows, depth)
        part = gram(left, recv_x[side, pl.ds(0, vectors * x_rows), :])
        blocks += folded(picked(part, within(x_rows), x_rows), lane_in(block, x_rows))
    wave_middle(1)
    for side in range(2):
        block = 3 if side == 0 else 5
        left = t32[:, pl.ds(fixed + side * y_padded, y_padded), :]
        left = left.reshape(vectors * y_padded, depth)
        part = gram(left, recv_y[side, pl.ds(0, vectors * y_rows), :])
        blocks += folded(picked(part, within(y_rows), y_padded), lane_in(block, y_rows))
    left = t32[:, pl.ds(fixed + 2 * y_padded, c_padded), :].reshape(vectors * c_padded, depth)
    part = gram(left, recv_c[...].reshape(4 * 32, depth))

    blocks += folded(picked(part, corner_row, c_padded), corner_lane)

    pairs = vectors * vectors
    repeated = jnp.broadcast_to(blocks[:, None, :], (vectors, vectors, width))
    right = iota((1, vectors, width), 2)
    right = right - vectors * quotient(right, vectors, 9)
    kept = jnp.where(right == iota((1, vectors, width), 1), repeated, 0.0).reshape(pairs, width)
    neighbour = quotient(iota((width, 1), 0), vectors, 9)
    to_lane = (neighbour == iota((width, 9), 1)).astype(F32)
    turned_blocks = exact_dot(kept, to_lane)
    blocks_out[0, 0] = turned_blocks.reshape(vectors, vectors, 9)

    high_y = ny + 2

    def ext_at(j, f, e):
        return (j * high_y + f) * 8 + e

    for j in range(comps):
        for y in range(ny):
            values = load(r32, pl.ds(j * cells + y, nx, stride=ny))
            store(ext, values, pl.ds(ext_at(j, 1 + y, 1), nx))
    for side in range(2):
        at_x = side * (nx + 1)
        values = recv_x[side, pl.ds(vectors * x_rows, 32), :].astype(F32)
        for j in range(comps):
            for y in range(ny):
                line = values[j * ny + y : j * ny + y + 1]
                store(ext, line, pl.ds(ext_at(j, 1 + y, at_x), 1))
        at_y = side * (ny + 1)
        values = recv_y[side, pl.ds(vectors * y_rows, 16), :].astype(F32)
        for j in range(comps):
            store(ext, values[j * nx : (j + 1) * nx], pl.ds(ext_at(j, at_y, 1), nx))
        for side_y in range(2):
            values = recv_c[side * 2 + side_y].astype(F32)
            for j in range(comps):
                at = vectors * comps + j
                line = values[at : at + 1]
                store(ext, line, pl.ds(ext_at(j, side_y * (ny + 1), at_x), 1))

    half_x = (nx + 2) // 2
    half_y = (ny + 2) // 2
    kept_x = []
    for s in range(2):
        e = 2 * iota((half_x, depth), 0) + s
        kept_x.append((e >= margins[0, 0, 0, 0]) & (e < margins[0, 0, 0, 1]))
    fetches[6].wait()

    def local_row(v, carry):
        grouped = []
        for j in range(comps):
            for s in range(2):
                for t in range(2):
                    f = 2 * v + t
                    kept = (f >= margins[0, 0, 1, 0]) & (f < margins[0, 0, 1, 1])
                    factor_y = jnp.where(kept, 1.0, 0.0).astype(F32)
                    values = load(ext, pl.ds(ext_at(j, f, s), half_x, stride=2))
                    grouped.append(jnp.where(kept_x[s], values, 0.0) * factor_y)
        for j in range(comps):
            for s in range(2):
                for t in range(2):
                    i = 4 * j + 2 * s + t
                    acc = inverse[i, 0, v].astype(F32) * grouped[0]
                    for m in range(1, 4 * comps):
                        acc += inverse[i, m, v].astype(F32) * grouped[m]
                    store(loc, acc, pl.ds(ext_at(j, 2 * v + t, s), half_x, stride=2))
        return carry

    lax.fori_loop(0, half_y, local_row, 0)

    coarse_image = wave_end(1)
    refined = first + solve(coarse_rhs - coarse_image)
    solution_out[...] = refined
    weights = jnp.sum(jnp.where(own_place, refined, 0.0), axis=1, keepdims=True)
    for j in range(comps):
        for x in range(nx):
            value = load(loc, pl.ds(ext_at(j, 1, 1 + x), ny, stride=8))
            for a in range(vectors):
                at = (a * comps + j) * cells + x * ny
                value += weights[a : a + 1, :] * load(d32, pl.ds(at, ny))
            out[j, x] = value

    for number in range(2):
        await_all(slots_narrow.at[number], wave_send, 2 * number)
        await_all(slots_wide.at[number], wave_send, 2 * number + 1)
    await_all(narrow_rows, wave_send, 4)
    await_all(wide_rows, wave_send, 5)


def write_out(*refs):
    sources, targets, sems = refs[:3], refs[3:6], refs[6]
    copies = [
        pltpu.make_async_copy(source, target, sems.at[k])
        for k, (source, target) in enumerate(zip(sources, targets))
    ]
    for copy in copies:
        copy.start()
    for copy in copies:
        copy.wait()


def body(
    narrow,
    wide,
    deflation,
    residual,
    stiffness,
    mass,
    stencil,
    local_inverse,
    inverse_factor,
    margin_range,
    neighbor_blocks,
):
    vectors, comps, nx, ny, depth = deflation.shape
    order = inverse_factor.shape[1]
    cells = nx * ny
    places = stencil_places(comps, nx, ny)
    turned_inverse = local_inverse.transpose(0, 1, 3, 2, 4)
    x_send = vectors * comps * ny + 32
    y_send = vectors * comps * nx + 16
    anywhere = pl.BlockSpec(memory_space=pl.ANY)
    operands = (
        deflation,
        residual,
        stiffness,
        mass,
        jnp.asarray(places),
        stencil.transpose(1, 2, 0),
        turned_inverse,
        inverse_factor,
        margin_range,
        neighbor_blocks,
    )
    spaces = [pltpu.VMEM] * 5 + [pltpu.SMEM] + [pltpu.VMEM] * 2 + [pltpu.SMEM] * 2
    shapes = (
        jax.ShapeDtypeStruct(residual.shape, F32),
        jax.ShapeDtypeStruct((1, 1, vectors, vectors, 9), F32),
        jax.ShapeDtypeStruct((1, order), F32),
    )
    results = pl.pallas_call(
        functools.partial(kernel, narrow, wide, vectors, comps, nx, ny, depth),
        out_shape=tuple(pltpu.VMEM(shape.shape, shape.dtype) for shape in shapes),
        in_specs=[anywhere] * len(operands),
        out_specs=(pl.BlockSpec(memory_space=pltpu.VMEM),) * len(shapes),
        scratch_shapes=[space(o.shape, o.dtype) for space, o in zip(spaces, operands)]
        + [
            pltpu.VMEM((depth // 128, vectors * comps * cells, 128), F32),
            pltpu.VMEM((depth // 128, comps * cells, 128), F32),
            pltpu.VMEM((vectors, places.shape[0], depth), F32),
            pltpu.VMEM((places.shape[0], 9 * comps * cells), F32),
            pltpu.VMEM((32, depth), F32),
            pltpu.VMEM((depth // 128, comps * (ny + 2) * 8, 128), F32),
            pltpu.VMEM((depth // 128, comps * (ny + 2) * 8, 128), F32),
            pltpu.VMEM((2, x_send, depth), BF16),
            pltpu.VMEM((2, y_send, depth), BF16),
            pltpu.VMEM((4, 32, depth), BF16),
            pltpu.VMEM((2, x_send, depth), BF16),
            pltpu.VMEM((2, y_send, depth), BF16),
            pltpu.VMEM((4, 32, depth), BF16),
            pltpu.VMEM((2, wide // 2, narrow) + inverse_factor.shape, F32),
            pltpu.VMEM((2, 1, order), F32),
            pltpu.VMEM((2, 1, order), F32),
            pltpu.VMEM((2, narrow - 1, 1, order), F32),
            pltpu.VMEM((2, wide - 1, 1, order), F32),
            pltpu.SemaphoreType.DMA((len(operands),)),
            pltpu.SemaphoreType.DMA((8,)),
            pltpu.SemaphoreType.DMA((8,)),
            pltpu.SemaphoreType.DMA((7,)),
            pltpu.SemaphoreType.DMA((7,)),
        ],
        compiler_params=pltpu.CompilerParams(
            collective_id=0, has_side_effects=True, vmem_limit_bytes=60 * 1024 * 1024
        ),
    )(*operands)
    result, blocks, refined = pl.pallas_call(
        write_out,
        out_shape=tuple(jax.ShapeDtypeStruct(r.shape, r.dtype) for r in results),
        in_specs=[pl.BlockSpec(memory_space=pltpu.VMEM)] * 3,
        out_specs=(anywhere,) * 3,
        scratch_shapes=[pltpu.SemaphoreType.DMA((3,))],
        compiler_params=pltpu.CompilerParams(vmem_limit_bytes=2 * 1024 * 1024),
    )(*results)
    return result, blocks.transpose(0, 1, 4, 2, 3), refined.reshape(order)


def solution(mesh):
    placed = (
        P(None, None, "narrow", "wide", None),
        P(None, "narrow", "wide", None),
        P("narrow", "wide", None),
        P("narrow", "wide", None),
        P(),
        P(None, None, "narrow", "wide", None),
        P(("narrow", "wide"), None),
        P("narrow", "wide", None, None),
        P("narrow", "wide", None),
    )
    return jax.shard_map(
        functools.partial(body, mesh.shape["narrow"], mesh.shape["wide"]),
        mesh=mesh,
        in_specs=placed,
        out_specs=(P(None, "narrow", "wide", None), P("narrow", "wide", None, None, None), P()),
        check_vma=False,
    )
```

```python
import functools

import jax
import jax.numpy as jnp
import numpy as np
from jax import lax
from jax.experimental import pallas as pl
from jax.experimental.pallas import tpu as pltpu
from jax.sharding import PartitionSpec as P

F32 = jnp.float32
BF16 = jnp.bfloat16
MESH = pl.DeviceIdType.MESH


def pad_to(count, unit):
    return -(-count // unit) * unit


def stencil_places(comps, nx, ny):
    rows = []
    for j in range(comps):
        rows += [(j, x, y) for x in range(nx) for y in range(ny)]
    for x in (-1, nx):
        rows += [(j, x, y) for j in range(comps) for y in range(ny)]
    for y in (-1, ny):
        face = [(j, x, y) for j in range(comps) for x in range(nx)]
        rows += face + [None] * (pad_to(len(face), 8) - len(face))
    corners = [(j, x, y) for x in (-1, nx) for y in (-1, ny) for j in range(comps)]
    rows += corners + [None] * (pad_to(len(corners), 8) - len(corners))
    cells = comps * nx * ny
    table = np.full((len(rows), 3 * cells), -1, np.int32)
    for r, row in enumerate(rows):
        if row is None:
            continue
        j, x, y = row
        for oz in range(3):
            for i in range(comps):
                for px in range(nx):
                    for py in range(ny):
                        dx, dy = x - px, y - py
                        if abs(dx) <= 1 and abs(dy) <= 1:
                            column = oz * cells + i * nx * ny + px * ny + py
                            table[r, column] = j * 9 + (dx + 1) * 3 + dy + 1
    return table


def split(values):
    high = values.astype(BF16)
    return high, (values - high.astype(F32)).astype(BF16)


def iota(shape, axis):
    return lax.broadcasted_iota(jnp.int32, shape, axis)


def load(ref, *at):
    return jnp.concatenate([ref[(h,) + at] for h in range(ref.shape[0])], axis=-1)


def store(ref, values, *at):
    for h in range(ref.shape[0]):
        ref[(h,) + at] = values[:, h * 128 : (h + 1) * 128]


def quotient(values, size, count):
    return sum((values >= k * size).astype(jnp.int32) for k in range(1, count))


def exact_dot(values, chosen):
    rows = values.shape[0]
    high = values.astype(BF16).astype(F32)
    middle = (values - high).astype(BF16).astype(F32)
    low = values - high - middle
    parts = jnp.concatenate([high, middle, low], axis=0).astype(BF16)
    product = jnp.dot(parts, chosen.astype(BF16), preferred_element_type=F32)
    return product[:rows] + product[rows : 2 * rows] + product[2 * rows :]


def gram(left, right):
    dims = (((1,), (1,)), ((), ()))
    rows = left.shape[0]
    both = jnp.concatenate(split(left), axis=0)
    product = lax.dot_general(both, right, dims, preferred_element_type=F32)
    return product[:rows] + product[rows:]


def kernel(
    narrow,
    wide,
    vectors,
    comps,
    nx,
    ny,
    depth,
    *refs,
):
    operands, held = refs[:10], refs[13:23]
    deflation, residual, stiffness, mass, places, stencil = held[:6]
    inverse, factor, margins, listing = held[6:]
    out, blocks_out, solution_out = refs[10:13]
    (
        d32,
        r32,
        t32,
        s_parts,
        stage,
        ext,
        loc,
        send_x,
        send_y,
        send_c,
        recv_x,
        recv_y,
        recv_c,
        factors,
        message,
        partial,
        slots_narrow,
        slots_wide,
        in_sems,
        send_sems,
        recv_sems,
        wave_send,
        wave_recv,
    ) = refs[23:]
    order = factor.shape[1]
    row = lax.axis_index("narrow")
    column = lax.axis_index("wide")
    cells = nx * ny
    own_rows = comps * cells

    fetches = [
        pltpu.make_async_copy(source, target, in_sems.at[k])
        for k, (source, target) in enumerate(zip(operands, held))
    ]
    for fetch in fetches:
        fetch.start()

    def turned(here, count):
        places_of = [here + k for k in range(1, count)]
        return [jnp.where(at >= count, at - count, at) for at in places_of]

    along_narrow = [(at, column) for at in turned(row, narrow)]
    along_wide = [(row, at) for at in turned(column, wide)]
    diagonals = [(x, y) for x in (-1, 1) for y in (-1, 1)]

    def inside(shift_x, shift_y):
        along_x = (row + shift_x >= 0) & (row + shift_x < narrow)
        along_y = (column + shift_y >= 0) & (column + shift_y < wide)
        return along_x & along_y

    barrier = pltpu.get_barrier_semaphore()

    def greet(device):
        pl.semaphore_signal(barrier, inc=1, device_id=device, device_id_type=MESH)

    greetings = narrow - 1 + wide - 1
    for device in along_narrow + along_wide:
        greet(device)
    for shift_x, shift_y in diagonals:
        greetings += jnp.where(inside(shift_x, shift_y), 1, 0)

        @pl.when(inside(shift_x, shift_y))
        def _(shift_x=shift_x, shift_y=shift_y):
            greet((row + shift_x, column + shift_y))

    for k, fetch in enumerate(fetches):
        if k != 6:
            fetch.wait()

    pl.semaphore_wait(barrier, greetings)

    def spread_out(source, landing, sem, devices):
        for k, device in enumerate(devices):
            pltpu.make_async_remote_copy(
                src_ref=source,
                dst_ref=landing(k),
                send_sem=wave_send.at[sem],
                recv_sem=wave_recv.at[sem],
                device_id=device,
                device_id_type=MESH,
            ).start()

    def await_all(ref, sems, sem):
        pltpu.make_async_copy(ref, ref, sems.at[sem]).wait()

    def summed(ref, number, start):
        for k in range(ref.shape[1]):
            start = start + ref[number, k]
        return start

    def wave_start(number):
        landing = lambda k: slots_narrow.at[number, k]
        spread_out(message.at[number], landing, 2 * number, along_narrow)

    def wave_middle(number):
        await_all(slots_narrow.at[number], wave_recv, 2 * number)
        partial[number] = summed(slots_narrow, number, message[number])
        landing = lambda k: slots_wide.at[number, k]
        spread_out(partial.at[number], landing, 2 * number + 1, along_wide)

    def wave_end(number):
        await_all(slots_wide.at[number], wave_recv, 2 * number + 1)
        return summed(slots_wide, number, partial[number])

    parity = lax.rem(column, 2)
    half_column = column // 2
    factors[parity, half_column, row] = factor[...]
    spread_out(factor, lambda k: factors.at[parity, half_column, row], 4, along_narrow)
    narrow_rows = factors.at[0, 0, pl.ds(0, narrow - 1)]
    wide_rows = factors.at[0, pl.ds(0, wide // 2 - 1)]

    rounded = residual[...].astype(BF16).astype(F32).reshape(own_rows, depth)
    store(r32, rounded, pl.ds(0, own_rows))

    def rows_of(a):
        return pl.ds(pl.multiple_of(a * own_rows, own_rows), own_rows)

    def widen(a, carry):
        d = deflation[a].astype(F32).reshape(own_rows, depth)
        store(d32, d, rows_of(a))
        stage[pl.ds(a, 1), :] = jnp.sum(d * rounded, axis=0, keepdims=True)
        return carry

    lax.fori_loop(0, vectors, widen, 0, unroll=2)
    rhs_column = jnp.sum(stage[pl.ds(0, vectors), :], axis=1, keepdims=True)
    own_block = listing[0, 0, 4]
    own_place = iota((vectors, order), 1) == own_block * vectors + iota((vectors, order), 0)

    def placed(values):
        return jnp.sum(jnp.where(own_place, values, 0.0), axis=0, keepdims=True)

    message[0] = placed(rhs_column)

    x_rows = comps * ny
    y_rows = comps * nx
    for side, x in enumerate((0, nx - 1)):
        face = [
            load(d32, pl.ds((a * comps + j) * cells + x * ny, ny))
            for a in range(vectors)
            for j in range(comps)
        ]
        send_x[side, pl.ds(0, vectors * x_rows), :] = jnp.concatenate(face, axis=0).astype(BF16)
        stage[...] = jnp.zeros_like(stage)
        for j in range(comps):
            stage[pl.ds(j * ny, ny), :] = load(r32, pl.ds(j * cells + x * ny, ny))
        send_x[side, pl.ds(vectors * x_rows, 32), :] = stage[...].astype(BF16)
    for side, y in enumerate((0, ny - 1)):
        face = load(d32, pl.ds(y, vectors * y_rows, stride=ny))
        send_y[side, pl.ds(0, vectors * y_rows), :] = face.astype(BF16)
        stage[...] = jnp.zeros_like(stage)
        stage[pl.ds(0, y_rows), :] = load(r32, pl.ds(y, y_rows, stride=ny))
        send_y[side, pl.ds(vectors * y_rows, 16), :] = stage[pl.ds(0, 16), :].astype(BF16)
    for side_x, x in enumerate((0, nx - 1)):
        for side_y, y in enumerate((0, ny - 1)):
            stage[...] = jnp.zeros_like(stage)
            at = x * ny + y
            stage[pl.ds(0, vectors * comps), :] = load(d32, pl.ds(at, vectors * comps, stride=cells))
            stage[pl.ds(vectors * comps, comps), :] = load(r32, pl.ds(at, comps, stride=cells))
            send_c[side_x * 2 + side_y] = stage[...].astype(BF16)

    wave_start(0)

    def copies():
        found = []
        for side, shift in enumerate((-1, 1)):
            found.append((send_x.at[side], recv_x.at[1 - side], recv_x.at[side], shift, 0))
        for side, shift in enumerate((-1, 1)):
            found.append((send_y.at[side], recv_y.at[1 - side], recv_y.at[side], 0, shift))
        for side_x, shift_x in enumerate((-1, 1)):
            for side_y, shift_y in enumerate((-1, 1)):
                at = side_x * 2 + side_y
                found.append((send_c.at[at], recv_c.at[3 - at], recv_c.at[at], shift_x, shift_y))
        return found

    opposite = (1, 0, 3, 2, 7, 6, 5, 4)

    def face_copy(k, source, target, shift_x, shift_y):
        return pltpu.make_async_remote_copy(
            src_ref=source,
            dst_ref=target,
            send_sem=send_sems.at[k],
            recv_sem=recv_sems.at[opposite[k]],
            device_id=(row + shift_x, column + shift_y),
            device_id_type=MESH,
        )

    for k, (source, target, _, shift_x, shift_y) in enumerate(copies()):

        @pl.when(inside(shift_x, shift_y))
        def _(k=k, source=source, target=target, shift_x=shift_x, shift_y=shift_y):
            face_copy(k, source, target, shift_x, shift_y).start()

    total_rows = places.shape[0]
    fixed = own_rows + 2 * x_rows
    group = quotient(iota((1, 3 * own_rows), 1), cells, 3 * comps)
    lanes_of = [group == g for g in range(3 * comps)]
    coupling = []
    for j in range(comps):
        for d in range(9):
            line = jnp.zeros((1, 3 * own_rows), F32)
            for oz in range(3):
                for i in range(comps):
                    line = jnp.where(lanes_of[oz * comps + i], stencil[i, j, d * 3 + oz], line)
            coupling.append(line)
    all_j = range(comps)
    chunks = [(j * cells, cells, range(j * 9, j * 9 + 9)) for j in all_j]
    for side in range(2):
        at = own_rows + side * x_rows
        for j in all_j:
            dx = j * 9 + 6 * side
            chunks.append((at + j * ny, ny, range(dx, dx + 3)))
    y_size = pad_to(y_rows, 8)
    for side in range(2):
        entries = [j * 9 + 3 * dx + 2 * side for j in all_j for dx in range(3)]
        chunks.append((fixed + side * y_size, y_size, entries))
    corner_entries = [j * 9 + d for j in all_j for d in (0, 2, 6, 8)]
    chunks.append((fixed + 2 * y_size, total_rows - fixed - 2 * y_size, corner_entries))
    for start, size, entries in chunks:
        here = places[pl.ds(start, size), :]
        value = jnp.zeros(here.shape, F32)
        for e in entries:
            value = jnp.where(here == e, coupling[e], value)
        s_parts[pl.ds(start, size), pl.ds(0, 3 * own_rows)] = value
    high, low = split(s_parts[:, pl.ds(0, 3 * own_rows)])
    s_parts[:, pl.ds(3 * own_rows, 3 * own_rows)] = high.astype(F32)
    s_parts[:, pl.ds(6 * own_rows, 3 * own_rows)] = low.astype(F32)
    s_all = s_parts[...].astype(BF16)

    lane = iota((own_rows, depth), 1)
    scale = jnp.concatenate([stiffness[...].reshape(cells, depth)] * comps, axis=0)
    weight = jnp.concatenate([mass[...].reshape(cells, depth)] * comps, axis=0)

    def adjoint(a, carry):
        d = load(d32, rows_of(a))
        w = d * scale
        before = jnp.where(lane == depth - 1, 0.0, pltpu.roll(w, depth - 1, axis=1))
        after = jnp.where(lane == 0, 0.0, pltpu.roll(w, 1, axis=1))
        parts = [split(shifted) for shifted in (before, w, after)]
        highs, lows = [part[0] for part in parts], [part[1] for part in parts]
        w_all = jnp.concatenate(highs + lows + highs, axis=0)
        image = jnp.dot(s_all, w_all, preferred_element_type=F32)
        t32[a, pl.ds(own_rows, total_rows - own_rows), :] = image[own_rows:]
        t32[a, pl.ds(0, own_rows), :] = image[:own_rows] + weight * d
        return carry

    cuts = (0, vectors // 4, vectors * 5 // 8, vectors)
    lax.fori_loop(cuts[0], cuts[1], adjoint, 0, unroll=True)
    wave_middle(0)
    await_all(narrow_rows, wave_recv, 4)
    mine = factors.at[parity, half_column]
    spread_out(mine, lambda k: mine, 5, along_wide[1::2])
    lax.fori_loop(cuts[1], cuts[2], adjoint, 0, unroll=True)
    await_all(wide_rows, wave_recv, 5)
    hand_on = pltpu.make_async_remote_copy(
        src_ref=factors.at[parity],
        dst_ref=factors.at[parity],
        send_sem=wave_send.at[6],
        recv_sem=wave_recv.at[6],
        device_id=(row, column + 1 - 2 * parity),
        device_id_type=MESH,
    )
    hand_on.start()
    lax.fori_loop(cuts[2], cuts[3], adjoint, 0, unroll=True)

    width = 9 * vectors

    def picked(product, row_of, left_size):
        columns = product.shape[1]
        kept = iota((left_size, columns), 0) == row_of(iota((1, columns), 1))
        parts = product.reshape(vectors, left_size, columns)
        return jnp.sum(jnp.where(kept[None], parts, 0.0), axis=1)

    def folded(values, lane_of):
        rows = values.shape[1]
        chosen = (lane_of(iota((rows, 1), 0)) == iota((rows, width), 1)).astype(F32)
        return exact_dot(values, chosen)

    def within(size):
        return lambda c: c - size * quotient(c, size, vectors)

    def lane_in(block, size):
        return lambda c: block * vectors + quotient(c, size, vectors)

    lefts = []
    rights = []
    for j in range(comps):
        left = t32[:, pl.ds(j * cells, cells), :]
        lefts.append(left.reshape(vectors * cells, depth))
        pieces = [load(d32, pl.ds((b * comps + j) * cells, cells)) for b in range(vectors)]
        rights.append(jnp.concatenate(pieces, axis=0).astype(BF16))
    total = gram(jnp.concatenate(lefts, axis=1), jnp.concatenate(rights, axis=1))

    for k, (source, target, landing, shift_x, shift_y) in enumerate(copies()):

        @pl.when(inside(shift_x, shift_y))
        def _(k=k, source=source, landing=landing, shift_x=shift_x, shift_y=shift_y):
            pltpu.make_async_remote_copy(
                src_ref=source,
                dst_ref=landing,
                send_sem=send_sems.at[k],
                recv_sem=recv_sems.at[k],
                device_id=(row + shift_x, column + shift_y),
                device_id_type=MESH,
            ).wait()

        @pl.when(jnp.logical_not(inside(shift_x, shift_y)))
        def _(landing=landing):
            landing[...] = jnp.zeros(landing.shape, BF16)

    y_padded = pad_to(y_rows, 8)
    c_padded = pad_to(4 * comps, 8)

    def corner_parts(c):
        corner = quotient(c, 32, 4)
        at = c - 32 * corner
        vector = quotient(at, comps, vectors)
        return at < vectors * comps, corner, vector, at - comps * vector

    def corner_row(c):
        real, corner, _, j = corner_parts(c)
        return jnp.where(real, corner * comps + j, -1)

    def corner_lane(c):
        real, corner, vector, _ = corner_parts(c)
        block = corner * 2 + jnp.where(corner >= 2, 2, 0)
        return jnp.where(real, block * vectors + vector, -1)

    coarse_rhs = wave_end(0)
    hand_on.wait()

    def solve(vector):
        def one(d, total):
            for k in range(2 * narrow):
                f = factors[k // narrow, d, k % narrow]
                total = total + f * jnp.sum(f * vector, axis=1, keepdims=True)
            return total

        zeros = jnp.zeros((factor.shape[0], order), F32)
        total = lax.fori_loop(0, wide // 2, one, zeros, unroll=4)
        return jnp.sum(total, axis=0, keepdims=True)

    first = solve(coarse_rhs)
    near = [
        iota((vectors, order), 1) == listing[0, 0, k] * vectors + iota((vectors, order), 0)
        for k in range(9)
    ]
    parts_of = [jnp.sum(jnp.where(m, first, 0.0), axis=1, keepdims=True) for m in near]

    def weights_on(lanes, block):
        chosen = iota((vectors, lanes.shape[1]), 0) == lanes
        return jnp.sum(jnp.where(chosen, parts_of[block], 0.0), axis=0, keepdims=True)

    def mixed(values, weights, row_of, count):
        lanes = iota((1, values.shape[0]), 1)
        matrix = jnp.where(iota((count, values.shape[0]), 0) == row_of(lanes), weights, 0.0)
        high = matrix.astype(BF16).astype(F32)
        both = jnp.concatenate([high, matrix - high], axis=0).astype(BF16)
        product = jnp.dot(both, values, preferred_element_type=F32)
        return product[:count] + product[count:]

    field = parts_of[4][0:1, :] * load(d32, rows_of(0))
    for b in range(1, vectors):
        field += parts_of[4][b : b + 1, :] * load(d32, rows_of(b))
    fields = [field]
    for side, block in enumerate((1, 7)):
        lanes = quotient(iota((1, vectors * x_rows), 1), x_rows, vectors)
        values = recv_x[side, pl.ds(0, vectors * x_rows), :]
        fields.append(mixed(values, weights_on(lanes, block), within(x_rows), x_rows))
    for side, block in enumerate((3, 5)):
        lanes = quotient(iota((1, vectors * y_rows), 1), y_rows, vectors)
        values = recv_y[side, pl.ds(0, vectors * y_rows), :]
        fields.append(mixed(values, weights_on(lanes, block), within(y_rows), y_padded))
    real, corner, vector, _ = corner_parts(iota((1, 4 * 32), 1))
    weights = jnp.zeros((1, 4 * 32), F32)
    for k, block in enumerate((0, 2, 6, 8)):
        weights += weights_on(jnp.where(real & (corner == k), vector, -1), block)
    fields.append(mixed(recv_c[...].reshape(4 * 32, depth), weights, corner_row, c_padded))
    field = jnp.concatenate(fields, axis=0)

    def imaged(a, carry):
        stage[pl.ds(a, 1), :] = jnp.sum(t32[a] * field, axis=0, keepdims=True)
        return carry

    lax.fori_loop(0, vectors, imaged, 0, unroll=2)
    message[1] = placed(jnp.sum(stage[pl.ds(0, vectors), :], axis=1, keepdims=True))
    wave_start(1)

    blocks = folded(picked(total, within(cells), cells), lane_in(4, cells))
    for side in range(2):
        block = 1 if side == 0 else 7
        left = t32[:, pl.ds(own_rows + side * x_rows, x_rows), :].reshape(vectors * x_rows, depth)
        part = gram(left, recv_x[side, pl.ds(0, vectors * x_rows), :])
        blocks += folded(picked(part, within(x_rows), x_rows), lane_in(block, x_rows))
    wave_middle(1)
    for side in range(2):
        block = 3 if side == 0 else 5
        left = t32[:, pl.ds(fixed + side * y_padded, y_padded), :]
        left = left.reshape(vectors * y_padded, depth)
        part = gram(left, recv_y[side, pl.ds(0, vectors * y_rows), :])
        blocks += folded(picked(part, within(y_rows), y_padded), lane_in(block, y_rows))
    left = t32[:, pl.ds(fixed + 2 * y_padded, c_padded), :].reshape(vectors * c_padded, depth)
    part = gram(left, recv_c[...].reshape(4 * 32, depth))

    blocks += folded(picked(part, corner_row, c_padded), corner_lane)

    pairs = vectors * vectors
    repeated = jnp.broadcast_to(blocks[:, None, :], (vectors, vectors, width))
    right = iota((1, vectors, width), 2)
    right = right - vectors * quotient(right, vectors, 9)
    kept = jnp.where(right == iota((1, vectors, width), 1), repeated, 0.0).reshape(pairs, width)
    neighbour = quotient(iota((width, 1), 0), vectors, 9)
    to_lane = (neighbour == iota((width, 9), 1)).astype(F32)
    turned_blocks = exact_dot(kept, to_lane)
    blocks_out[0, 0] = turned_blocks.reshape(vectors, vectors, 9)

    high_y = ny + 2

    def ext_at(j, f, e):
        return (j * high_y + f) * 8 + e

    for j in range(comps):
        for y in range(ny):
            values = load(r32, pl.ds(j * cells + y, nx, stride=ny))
            store(ext, values, pl.ds(ext_at(j, 1 + y, 1), nx))
    for side in range(2):
        at_x = side * (nx + 1)
        values = recv_x[side, pl.ds(vectors * x_rows, 32), :].astype(F32)
        for j in range(comps):
            for y in range(ny):
                line = values[j * ny + y : j * ny + y + 1]
                store(ext, line, pl.ds(ext_at(j, 1 + y, at_x), 1))
        at_y = side * (ny + 1)
        values = recv_y[side, pl.ds(vectors * y_rows, 16), :].astype(F32)
        for j in range(comps):
            store(ext, values[j * nx : (j + 1) * nx], pl.ds(ext_at(j, at_y, 1), nx))
        for side_y in range(2):
            values = recv_c[side * 2 + side_y].astype(F32)
            for j in range(comps):
                at = vectors * comps + j
                line = values[at : at + 1]
                store(ext, line, pl.ds(ext_at(j, side_y * (ny + 1), at_x), 1))

    half_x = (nx + 2) // 2
    half_y = (ny + 2) // 2
    kept_x = []
    for s in range(2):
        e = 2 * iota((half_x, depth), 0) + s
        kept_x.append((e >= margins[0, 0, 0, 0]) & (e < margins[0, 0, 0, 1]))
    fetches[6].wait()

    def local_row(v, carry):
        grouped = []
        for j in range(comps):
            for s in range(2):
                for t in range(2):
                    f = 2 * v + t
                    kept = (f >= margins[0, 0, 1, 0]) & (f < margins[0, 0, 1, 1])
                    factor_y = jnp.where(kept, 1.0, 0.0).astype(F32)
                    values = load(ext, pl.ds(ext_at(j, f, s), half_x, stride=2))
                    grouped.append(jnp.where(kept_x[s], values, 0.0) * factor_y)
        for j in range(comps):
            for s in range(2):
                for t in range(2):
                    i = 4 * j + 2 * s + t
                    acc = inverse[i, 0, v].astype(F32) * grouped[0]
                    for m in range(1, 4 * comps):
                        acc += inverse[i, m, v].astype(F32) * grouped[m]
                    store(loc, acc, pl.ds(ext_at(j, 2 * v + t, s), half_x, stride=2))
        return carry

    lax.fori_loop(0, half_y, local_row, 0)

    coarse_image = wave_end(1)
    refined = first + solve(coarse_rhs - coarse_image)
    solution_out[...] = refined
    weights = jnp.sum(jnp.where(own_place, refined, 0.0), axis=1, keepdims=True)
    for j in range(comps):
        for x in range(nx):
            value = load(loc, pl.ds(ext_at(j, 1, 1 + x), ny, stride=8))
            for a in range(vectors):
                at = (a * comps + j) * cells + x * ny
                value += weights[a : a + 1, :] * load(d32, pl.ds(at, ny))
            out[j, x] = value

    for number in range(2):
        await_all(slots_narrow.at[number], wave_send, 2 * number)
        await_all(slots_wide.at[number], wave_send, 2 * number + 1)
    await_all(narrow_rows, wave_send, 4)
    await_all(wide_rows, wave_send, 5)


def write_out(*refs):
    sources, targets, sems = refs[:3], refs[3:6], refs[6]
    copies = [
        pltpu.make_async_copy(source, target, sems.at[k])
        for k, (source, target) in enumerate(zip(sources, targets))
    ]
    for copy in copies:
        copy.start()
    for copy in copies:
        copy.wait()


def body(
    narrow,
    wide,
    deflation,
    residual,
    stiffness,
    mass,
    stencil,
    local_inverse,
    inverse_factor,
    margin_range,
    neighbor_blocks,
):
    vectors, comps, nx, ny, depth = deflation.shape
    order = inverse_factor.shape[1]
    cells = nx * ny
    places = stencil_places(comps, nx, ny)
    turned_inverse = local_inverse.transpose(0, 1, 3, 2, 4)
    x_send = vectors * comps * ny + 32
    y_send = vectors * comps * nx + 16
    anywhere = pl.BlockSpec(memory_space=pl.ANY)
    operands = (
        deflation,
        residual,
        stiffness,
        mass,
        jnp.asarray(places),
        stencil.transpose(1, 2, 0),
        turned_inverse,
        inverse_factor,
        margin_range,
        neighbor_blocks,
    )
    spaces = [pltpu.VMEM] * 5 + [pltpu.SMEM] + [pltpu.VMEM] * 2 + [pltpu.SMEM] * 2
    shapes = (
        jax.ShapeDtypeStruct(residual.shape, F32),
        jax.ShapeDtypeStruct((1, 1, vectors, vectors, 9), F32),
        jax.ShapeDtypeStruct((1, order), F32),
    )
    results = pl.pallas_call(
        functools.partial(kernel, narrow, wide, vectors, comps, nx, ny, depth),
        out_shape=tuple(pltpu.VMEM(shape.shape, shape.dtype) for shape in shapes),
        in_specs=[anywhere] * len(operands),
        out_specs=(pl.BlockSpec(memory_space=pltpu.VMEM),) * len(shapes),
        scratch_shapes=[space(o.shape, o.dtype) for space, o in zip(spaces, operands)]
        + [
            pltpu.VMEM((depth // 128, vectors * comps * cells, 128), F32),
            pltpu.VMEM((depth // 128, comps * cells, 128), F32),
            pltpu.VMEM((vectors, places.shape[0], depth), F32),
            pltpu.VMEM((places.shape[0], 9 * comps * cells), F32),
            pltpu.VMEM((32, depth), F32),
            pltpu.VMEM((depth // 128, comps * (ny + 2) * 8, 128), F32),
            pltpu.VMEM((depth // 128, comps * (ny + 2) * 8, 128), F32),
            pltpu.VMEM((2, x_send, depth), BF16),
            pltpu.VMEM((2, y_send, depth), BF16),
            pltpu.VMEM((4, 32, depth), BF16),
            pltpu.VMEM((2, x_send, depth), BF16),
            pltpu.VMEM((2, y_send, depth), BF16),
            pltpu.VMEM((4, 32, depth), BF16),
            pltpu.VMEM((2, wide // 2, narrow) + inverse_factor.shape, F32),
            pltpu.VMEM((2, 1, order), F32),
            pltpu.VMEM((2, 1, order), F32),
            pltpu.VMEM((2, narrow - 1, 1, order), F32),
            pltpu.VMEM((2, wide - 1, 1, order), F32),
            pltpu.SemaphoreType.DMA((len(operands),)),
            pltpu.SemaphoreType.DMA((8,)),
            pltpu.SemaphoreType.DMA((8,)),
            pltpu.SemaphoreType.DMA((7,)),
            pltpu.SemaphoreType.DMA((7,)),
        ],
        compiler_params=pltpu.CompilerParams(
            collective_id=0, has_side_effects=True, vmem_limit_bytes=60 * 1024 * 1024
        ),
    )(*operands)
    result, blocks, refined = pl.pallas_call(
        write_out,
        out_shape=tuple(jax.ShapeDtypeStruct(r.shape, r.dtype) for r in results),
        in_specs=[pl.BlockSpec(memory_space=pltpu.VMEM)] * 3,
        out_specs=(anywhere,) * 3,
        scratch_shapes=[pltpu.SemaphoreType.DMA((3,))],
        compiler_params=pltpu.CompilerParams(vmem_limit_bytes=2 * 1024 * 1024),
    )(*results)
    return result, blocks.transpose(0, 1, 4, 2, 3), refined.reshape(order)


def solution(mesh):
    placed = (
        P(None, None, "narrow", "wide", None),
        P(None, "narrow", "wide", None),
        P("narrow", "wide", None),
        P("narrow", "wide", None),
        P(),
        P(None, None, "narrow", "wide", None),
        P(("narrow", "wide"), None),
        P("narrow", "wide", None, None),
        P("narrow", "wide", None),
    )
    return jax.shard_map(
        functools.partial(body, mesh.shape["narrow"], mesh.shape["wide"]),
        mesh=mesh,
        in_specs=placed,
        out_specs=(P(None, "narrow", "wide", None), P("narrow", "wide", None, None, None), P()),
        check_vma=False,
    )
```
